128 devices in a mesh: dp: 4 (over z_lo, core), tm: 8 (over x, z_hi), head: 4 (over y).
Axes of the slice: x: 4, y: 4, z: 4 (z_hi: 2, z_lo: 2; z = z_hi * 2 + z_lo), core: 2. Of those that a mesh axis runs over, the one named last changes fastest.
Arguments:
- frames: bfloat16 [4, 3072, 1536], P('dp', 'tm')
- projections: bfloat16 [4, 1536, 1536], P(None, None, 'head')
- kernel: bfloat16 [32, 1536], replicated, may hold values from -1 to 1
- pattern: int32 [4, 48, 12], P('dp', 'tm'), may hold values from -1 to 47, as said below
- cotangent: bfloat16 [4, 3072, 1536], P('dp', 'tm'), may hold values from -0.0546875 to 0.0546875
Outputs:
- encoded: bfloat16 [4, 3072, 1536], P('dp', 'tm')
- proj_grad: float32 [4, 1536, 1536], P(None, ('dp', 'tm'), 'head')
- kernel_grad: float32 [32, 1536], P(('dp', 'tm'))
The draws below stay inside these ranges and needn't reach their ends.
Inputs may be any that keep to these rules, and one draw needn't show every extreme that they name: `pattern`: in each row the strided key blocks come first: phase + j * 4 for j = 0, 1, ..., one phase below 4 for the row, 1 to 12 of them; the remaining entries are -1.
All inputs are finite; a program needn't handle non-finite values.
Results may differ from the reference program's by a relative error of at most 0.04.
Values may be sent and summed in bfloat16 or wider, within the bound.
A program may use at most 128 MiB of HBM per device.

```python
import jax
import jax.numpy as jnp
from jax import lax

D = 1536
HEADS = 16
HD = 96
BLK = 64
MAXSEL = 12
KW = 32
UTTS = 4
S = 3072
NBLK = 48
STRIDE = 4


def draw_frames(key, part):
    subkeys = jax.random.split(key, 1)
    drawn = jnp.clip(jax.random.normal(subkeys[0], (UTTS, S, D), jnp.float32), -6.0, 6.0)
    return drawn.astype(jnp.bfloat16)


def draw_projections(key, part):
    drawn = jax.random.normal(key, (4, D, HEADS * HD), jnp.float32) * D ** (-0.5)
    return drawn.astype(jnp.bfloat16)


def draw_pattern(key, part):
    subkeys = jax.random.split(key, 3)
    blocks = jnp.arange(NBLK, dtype=jnp.int32)
    busy_start = jax.random.randint(subkeys[0], (UTTS, 1), 0, NBLK)
    busy_rows = (blocks[None, :] - busy_start) % NBLK < max(NBLK // 4, 1)
    entry_count = jnp.where(busy_rows, MAXSEL, jax.random.randint(subkeys[1], (UTTS, NBLK), 1, MAXSEL // 2 + 1))
    row_phase = jax.random.randint(subkeys[2], (UTTS, NBLK), 0, STRIDE)
    row_phase = jnp.where(blocks[None, :] == busy_start, STRIDE - 1, row_phase)
    slot_index = jnp.arange(MAXSEL, dtype=jnp.int32)
    entries = row_phase[:, :, None] + slot_index[None, None, :] * STRIDE
    return jnp.where(slot_index[None, None, :] < entry_count[:, :, None], entries, -1).astype(jnp.int32)


def block_levels(key, dims, shards, smallest, largest):
    factor_of, own = 1.0, jax.random.fold_in(key, 6)
    for dim, blocks in shards:
        steps = jnp.exp(jax.random.uniform(jax.random.fold_in(own, dim), (blocks,), jnp.float32, smallest / len(shards), largest / len(shards)))
        factor_of = factor_of * jnp.repeat(steps, dims[dim] // blocks).reshape([-1 if axis == dim else 1 for axis in range(len(dims))])
    return factor_of


def normal_values(stream_key, shape, deviation, reach, shards=(), held_as=jnp.bfloat16):
    level = block_levels(stream_key, shape, shards, -0.22, 0.18) if shards else 1.0
    values = jax.random.normal(stream_key, shape, jnp.float32) * deviation * level
    return jnp.minimum(jnp.maximum(values, -reach), reach).astype(held_as)


def setup_inputs(seed: int = 0) -> dict:
    splits = jax.random.split(jax.random.key(seed), 6)
    return {
        "frames": draw_frames(jax.random.fold_in(splits[5], 71), 0),
        "projections": draw_projections(jax.random.fold_in(splits[5], 71), 0),
        "kernel": normal_values(splits[2], (KW, D), KW ** -0.5, 1.0),
        "pattern": draw_pattern(jax.random.fold_in(splits[5], 71), 0),
        "cotangent": normal_values(splits[4], (UTTS, S, D), ((UTTS * S) ** -0.5), 0.0546875, ((0, 4), (1, 8))),
    }


def key_lists(pattern, first_block, nblocks):
    query_count = pattern.shape[0]
    query_block = first_block + jnp.arange(query_count, dtype=jnp.int32)
    band_blocks = query_block[:, None] + jnp.arange(-1, 2, dtype=jnp.int32)[None, :]
    band_live = (band_blocks >= 0) & (band_blocks < nblocks)
    far_live = (pattern >= 0) & (jnp.abs(pattern - query_block[:, None]) > 1)
    listed = jnp.clip(jnp.concatenate([band_blocks, pattern], axis=1), 0, nblocks - 1).astype(jnp.int32)
    live_mask = jnp.concatenate([band_live, far_live], axis=1)
    return listed, live_mask


def gather_blocks(source, listed, block_len, head_dim):
    head_count = source.shape[1] // head_dim
    gathered = source.reshape(-1, block_len, head_count, head_dim)[listed]
    return gathered.reshape(listed.shape[0], listed.shape[1] * block_len, head_count, head_dim)


def masked_scores(query_tiles, key_tiles, live_mask, block_len):
    score_scale = query_tiles.shape[-1] ** -0.5
    scores = jnp.einsum("qthd,qkhd->qhtk", query_tiles.astype(jnp.float32), key_tiles.astype(jnp.float32)) * score_scale
    column_live = jnp.repeat(live_mask, block_len, axis=1)[:, None, None, :]
    return jnp.where(column_live, scores, -1e30), column_live


def attend(queries, key_rows, values, listed, live_mask, block_len, head_dim):
    head_count = queries.shape[1] // head_dim
    query_tiles = queries.reshape(listed.shape[0], block_len, head_count, head_dim)
    key_tiles = gather_blocks(key_rows, listed, block_len, head_dim)
    value_tiles = gather_blocks(values, listed, block_len, head_dim)
    scores, column_live = masked_scores(query_tiles, key_tiles, live_mask, block_len)
    highest = jnp.max(scores, axis=-1, keepdims=True)
    logsum = highest + jnp.log(jnp.sum(jnp.exp(scores - highest), axis=-1, keepdims=True))
    weights = jnp.where(column_live, jnp.exp(scores - logsum), 0.0).astype(jnp.bfloat16)
    mixed_rows = jnp.einsum("qhtk,qkhd->qthd", weights.astype(jnp.float32), value_tiles.astype(jnp.float32)).astype(jnp.bfloat16)
    return mixed_rows.reshape(queries.shape), logsum


def attend_back(queries, key_rows, values, listed, live_mask, logsum, mixed_rows, grad_mixed, block_len, head_dim, nblocks):
    head_count = queries.shape[1] // head_dim
    shape_tiles = (listed.shape[0], block_len, head_count, head_dim)
    query_tiles = queries.reshape(shape_tiles)
    grad_tiles = grad_mixed.reshape(shape_tiles).astype(jnp.float32)
    mixed_tiles = mixed_rows.reshape(shape_tiles).astype(jnp.float32)
    key_tiles = gather_blocks(key_rows, listed, block_len, head_dim)
    value_tiles = gather_blocks(values, listed, block_len, head_dim)
    scores, column_live = masked_scores(query_tiles, key_tiles, live_mask, block_len)
    probabilities = jnp.where(column_live, jnp.exp(scores - logsum), 0.0)
    weights = probabilities.astype(jnp.bfloat16)
    row_delta = jnp.einsum("qthd,qthd->qht", grad_tiles, mixed_tiles)
    grad_probs = jnp.einsum("qthd,qkhd->qhtk", grad_tiles, value_tiles.astype(jnp.float32))
    score_scale = head_dim ** -0.5
    grad_scores = (probabilities * (grad_probs - row_delta[..., None]) * score_scale).astype(jnp.bfloat16)
    grad_queries = jnp.einsum("qhtk,qkhd->qthd", grad_scores.astype(jnp.float32), key_tiles.astype(jnp.float32))
    grad_queries = grad_queries.astype(jnp.bfloat16).reshape(queries.shape)
    key_terms = jnp.einsum("qhtk,qthd->qkhd", grad_scores.astype(jnp.float32), query_tiles.astype(jnp.float32))
    value_terms = jnp.einsum("qhtk,qthd->qkhd", weights.astype(jnp.float32), grad_tiles)
    block_ids = jnp.arange(nblocks, dtype=jnp.int32)
    onehot = ((listed.reshape(-1)[:, None] == block_ids[None, :]) & live_mask.reshape(-1)[:, None]).astype(jnp.float32)
    tile_width = block_len * queries.shape[1]
    key_grad = jnp.dot(onehot.T, key_terms.reshape(-1, tile_width), precision=lax.Precision.HIGHEST)
    value_grad = jnp.dot(onehot.T, value_terms.reshape(-1, tile_width), precision=lax.Precision.HIGHEST)
    key_grad = key_grad.reshape(nblocks * block_len, queries.shape[1])
    value_grad = value_grad.reshape(nblocks * block_len, queries.shape[1])
    return grad_queries, key_grad, value_grad


def reference(frames, projections, kernel, pattern, cotangent):
    nblocks = S // BLK
    half_width = KW // 2
    contract = (((0,), (0,)), ((), ()))

    def one_utterance(inputs):
        source, rows_pattern, upstream = inputs
        listed, live_mask = key_lists(rows_pattern, 0, nblocks)
        queries = jnp.dot(source, projections[0], preferred_element_type=jnp.float32).astype(jnp.bfloat16)
        key_rows = jnp.dot(source, projections[1], preferred_element_type=jnp.float32).astype(jnp.bfloat16)
        values = jnp.dot(source, projections[2], preferred_element_type=jnp.float32).astype(jnp.bfloat16)
        mixed_rows, logsum = attend(queries, key_rows, values, listed, live_mask, BLK, HD)
        output_part = lax.dot_general(mixed_rows, projections[3], (((1,), (1,)), ((), ())), preferred_element_type=jnp.float32)
        residual = (source.astype(jnp.float32) + output_part).astype(jnp.bfloat16)
        padded = jnp.pad(residual, ((half_width, half_width), (0, 0)))
        padded_up = jnp.pad(upstream, ((half_width, half_width), (0, 0)))
        upstream_wide = upstream.astype(jnp.float32)
        encoded = residual.astype(jnp.float32)
        back_grad = upstream_wide
        taps_grad = []
        for offset in range(KW):
            weight_row = kernel[offset].astype(jnp.float32)
            shifted = padded[offset:offset + S].astype(jnp.float32)
            encoded = encoded + weight_row * shifted
            back_grad = back_grad + weight_row * padded_up[2 * half_width - offset:2 * half_width - offset + S].astype(jnp.float32)
            taps_grad.append(jnp.sum(upstream_wide * shifted, axis=0))
        encoded = encoded.astype(jnp.bfloat16)
        back_grad = back_grad.astype(jnp.bfloat16)
        kernel_grad = jnp.stack(taps_grad)
        grad_mixed = jnp.dot(back_grad, projections[3], preferred_element_type=jnp.float32).astype(jnp.bfloat16)
        grad_queries, key_grad, value_grad = attend_back(queries, key_rows, values, listed, live_mask, logsum, mixed_rows, grad_mixed, BLK, HD, nblocks)
        proj_grad = jnp.stack([
            lax.dot_general(source, grad_queries, contract, preferred_element_type=jnp.float32),
            lax.dot_general(source, key_grad.astype(jnp.bfloat16), contract, preferred_element_type=jnp.float32),
            lax.dot_general(source, value_grad.astype(jnp.bfloat16), contract, preferred_element_type=jnp.float32),
            lax.dot_general(back_grad, mixed_rows, contract, preferred_element_type=jnp.float32),
        ])
        return encoded, proj_grad, kernel_grad

    encoded, proj_grad, kernel_grad = lax.map(one_utterance, (frames, pattern, cotangent))
    return encoded, jnp.sum(proj_grad, axis=0), jnp.sum(kernel_grad, axis=0)
```

```python
import jax
import jax.numpy as jnp
from jax import lax
from jax.experimental import pallas as pl
from jax.experimental.pallas import tpu as pltpu
from jax.sharding import PartitionSpec as P

HD = 96
BLK = 64
KW = 32
HALF = KW // 2
T = 384
C = 1536
F = 384
NKB = 48
QC = 256
MESH = pl.DeviceIdType.MESH
BF = jnp.bfloat16
F32 = jnp.float32


def remote(src, dst, ssem, rsem, device):
    return pltpu.make_async_remote_copy(
        src_ref=src, dst_ref=dst, send_sem=ssem, recv_sem=rsem, device_id=device, device_id_type=MESH
    )


def greet(devices):
    barrier = pltpu.get_barrier_semaphore()
    for device in devices:
        pl.semaphore_signal(barrier, inc=1, device_id=device, device_id_type=MESH)
    pl.semaphore_wait(barrier, len(devices))


def place():
    dp, tm, hd = lax.axis_index("dp"), lax.axis_index("tm"), lax.axis_index("head")
    return dp, tm, hd


def tap_terms(window, offsets):
    for r in range(8):
        shifted = window[r : r + 88] if r else window
        for a in range(5):
            o = 8 * a + r
            if o in offsets:
                yield offsets[o], shifted[8 * a : 8 * a + 64]


def project_kernel(
    frames, cot, w, taps, meta, kv_out, qd_out, bg_t, frames_t,
    bg, upad, halo, tapsf, kv_s, q_s, d_s, hs, hr, kvs, kvr, qs, qr, ds, dr, ls,
):
    dp, tm, hd = place()
    x, zh = tm // 2, lax.rem(tm, 2)
    at_tm = lambda k: (dp, lax.rem(tm + k, 8), hd)
    greet([at_tm(k) for k in range(1, 8)])
    halos = [
        remote(cot.at[T - HALF : T], halo.at[0], hs.at[0], hr.at[0], at_tm(1)),
        remote(cot.at[0:HALF], halo.at[1], hs.at[1], hr.at[1], at_tm(7)),
    ]
    for c in halos:
        c.start()

    for p in (1, 2):
        y = jnp.dot(frames[...], w[p], preferred_element_type=F32).astype(BF).T
        for h in range(4):
            kv_s[h, (p - 1) * HD : p * HD, :] = y[h * HD : (h + 1) * HD]
    sends = []
    for k in range(1, 8):
        c = remote(kv_s.at[lax.rem(tm + k, 8) // 2], kv_out.at[tm], kvs.at[k], kvr.at[k], at_tm(k))
        c.start()
        sends.append(c)
    local = [pltpu.make_async_copy(kv_s.at[x], kv_out.at[tm], ls.at[0])]
    local[0].start()

    y = jnp.dot(frames[...], w[0], preferred_element_type=F32).astype(BF).T
    for h in range(4):
        q_s[h] = y[h * HD : (h + 1) * HD]
    for k in range(1, 4):
        xo = lax.rem(x + k, 4)
        c = remote(q_s.at[xo], qd_out.at[x, 0:HD], qs.at[k], qr.at[k], (dp, xo * 2 + zh, hd))
        c.start()
        sends.append(c)
    c = pltpu.make_async_copy(q_s.at[x], qd_out.at[x, 0:HD], ls.at[1])
    c.start()
    local.append(c)

    tapsf[...] = taps[...].astype(F32)
    upad[HALF : HALF + T] = cot[...].astype(F32)
    for c in halos:
        c.wait()
    upad[0:HALF] = jnp.where(tm > 0, halo[0].astype(F32), 0.0)
    upad[HALF + T :] = jnp.where(tm < 7, halo[1].astype(F32), 0.0)
    offsets = {2 * HALF - j: j for j in range(KW)}

    def conv(it, carry):
        i, l = it // 12, lax.rem(it, 12)
        lanes = pl.ds(pl.multiple_of(l * 128, 128), 128)
        window = upad[pl.ds(pl.multiple_of(i * 64, 64), 96), lanes]
        acc = window[HALF : HALF + 64]
        for j, rows in tap_terms(window, offsets):
            acc = acc + tapsf[j : j + 1, lanes] * rows
        bg[pl.ds(pl.multiple_of(i * 64, 64), 64), lanes] = acc.astype(BF)
        return carry

    lax.fori_loop(0, 72, conv, 0)
    y = jnp.dot(bg[...], w[3], preferred_element_type=F32).astype(BF).T
    for h in range(4):
        d_s[h, 0:HD] = y[h * HD : (h + 1) * HD]
        d_s[h, HD:] = meta[...]
    for k in range(1, 4):
        xo = lax.rem(x + k, 4)
        c = remote(d_s.at[xo], qd_out.at[x, HD:], ds.at[k], dr.at[k], (dp, xo * 2 + zh, hd))
        c.start()
        sends.append(c)
    c = pltpu.make_async_copy(d_s.at[x], qd_out.at[x, HD:], ls.at[2])
    c.start()
    local.append(c)

    frames_t[...] = frames[...].T
    bg_t[...] = bg[...].T
    for c in local:
        c.wait()
    for c in sends:
        c.wait()


def project(frames, cot, w, taps, meta):
    vmem = pl.BlockSpec(memory_space=pltpu.VMEM)
    anym = pl.BlockSpec(memory_space=pl.ANY)
    dma = pltpu.SemaphoreType.DMA
    return pl.pallas_call(
        project_kernel,
        out_shape=(
            jax.ShapeDtypeStruct((8, 2 * HD, T), BF),
            jax.ShapeDtypeStruct((4, 2 * HD + 16, T), BF),
            jax.ShapeDtypeStruct((C, T), BF),
            jax.ShapeDtypeStruct((C, T), BF),
        ),
        in_specs=[vmem] * 5,
        out_specs=(anym, anym, vmem, vmem),
        scratch_shapes=[
            pltpu.VMEM((T, C), BF),
            pltpu.VMEM((T + 2 * HALF, C), F32),
            pltpu.VMEM((2, HALF, C), BF),
            pltpu.VMEM((KW, C), F32),
            pltpu.VMEM((4, 2 * HD, T), BF),
            pltpu.VMEM((4, HD, T), BF),
            pltpu.VMEM((4, HD + 16, T), BF),
            dma((2,)), dma((2,)), dma((8,)), dma((8,)), dma((4,)), dma((4,)), dma((4,)), dma((4,)), dma((3,)),
        ],
        compiler_params=pltpu.CompilerParams(
            collective_id=0, has_side_effects=True, vmem_limit_bytes=48 << 20
        ),
        name="project_exchange",
    )(frames, cot, w, taps, meta)


def attention_kernel(
    kv, qd, qblock, o_out, dq_out, dkv_out,
    kn, vn, kt, vt, qt, dt, on, dqn, live, dk, dv, st, et,
):
    scale = HD ** -0.5
    c2 = scale * 1.4426950408889634
    for t in range(8):
        kt[:, t * T : (t + 1) * T] = kv[t, 0:HD]
        vt[:, t * T : (t + 1) * T] = kv[t, HD:]
        kn[t * T : (t + 1) * T, :] = kv[t, 0:HD].T
        vn[t * T : (t + 1) * T, :] = kv[t, HD:].T
    for a in range(4):
        lanes = slice(a * T, (a + 1) * T)
        qt[:, lanes] = qd[a, 0:HD]
        dt[:, lanes] = qd[a, HD : 2 * HD]
        meta = qd[a, 2 * HD :].astype(F32)
        phase, count = meta[0:1], meta[1:2]
        row = lax.broadcasted_iota(jnp.int32, (64, T), 0)
        kb = (row // 8) * 6 + lax.rem(row, 8)
        far = (lax.rem(kb, 4).astype(F32) == phase) & ((kb // 4).astype(F32) < count)
        near = jnp.abs(kb.astype(F32) - qblock[a : a + 1]) < 1.5
        live[:, lanes] = jnp.where(far | near, 1.0, 0.0)
    dk[...] = jnp.zeros_like(dk)
    dv[...] = jnp.zeros_like(dv)

    def step(c, carry):
        lanes = pl.ds(pl.multiple_of(c * QC, QC), QC)
        q_t = qt[:, lanes]

        def scores(t, top):
            rows = pl.ds(pl.multiple_of(t * T, T), T)
            s = jnp.dot(kn[rows, :], q_t, preferred_element_type=F32)
            mask = live[pl.ds(pl.multiple_of(t * 8, 8), 8), lanes]
            parts = []
            for b in range(6):
                part = jnp.where(mask[b : b + 1] > 0.5, s[b * BLK : (b + 1) * BLK], -1e30)
                top = jnp.maximum(top, jnp.max(part.reshape(8, 8, QC), axis=0))
                parts.append(part)
            st[rows, :] = jnp.concatenate(parts, axis=0)
            return top

        top = lax.fori_loop(0, 8, scores, jnp.full((8, QC), -jnp.inf, F32))
        top = jnp.max(top, axis=0, keepdims=True) * c2

        def weigh(t, carry):
            total, o = carry
            rows = pl.ds(pl.multiple_of(t * T, T), T)
            e = jnp.exp2(st[rows, :] * c2 - top)
            total = total + jnp.sum(e.reshape(T // 8, 8, QC), axis=0)
            eb = e.astype(BF)
            et[rows, :] = eb
            o = o + jnp.dot(vt[:, pl.ds(pl.multiple_of(t * T, T), T)], eb, preferred_element_type=F32)
            return total, o

        total, o = lax.fori_loop(
            0, 8, weigh, (jnp.zeros((8, QC), F32), jnp.zeros((HD, QC), F32))
        )
        inverse = 1.0 / jnp.sum(total, axis=0, keepdims=True)
        o = (o * inverse).astype(BF)
        on[:, lanes] = o
        d = dt[:, lanes].astype(F32)
        delta = jnp.sum(d * o.astype(F32), axis=0, keepdims=True) * inverse
        d_t = (d * inverse).astype(BF)
        d_n = d_t.T
        q_n = q_t.T

        def back(t, dq):
            rows = pl.ds(pl.multiple_of(t * T, T), T)
            eb = et[rows, :]
            dp = jnp.dot(vn[rows, :], d_t, preferred_element_type=F32)
            ds = (eb.astype(F32) * (dp - delta)).astype(BF)
            dk[rows, :] += jnp.dot(ds, q_n, preferred_element_type=F32)
            dv[rows, :] += jnp.dot(eb, d_n, preferred_element_type=F32)
            return dq + jnp.dot(
                kt[:, pl.ds(pl.multiple_of(t * T, T), T)], ds, preferred_element_type=F32
            )

        dq = lax.fori_loop(0, 8, back, jnp.zeros((HD, QC), F32))
        dqn[:, lanes] = (dq * scale).astype(BF)
        return carry

    lax.fori_loop(0, 4 * T // QC, step, 0)
    for a in range(4):
        lanes = slice(a * T, (a + 1) * T)
        o_out[a] = on[:, lanes]
        dq_out[a] = dqn[:, lanes]
    for t in range(8):
        dkv_out[t, 0:HD] = (dk[t * T : (t + 1) * T, :] * scale).astype(BF).T
        dkv_out[t, HD:] = dv[t * T : (t + 1) * T, :].astype(BF).T


def attention(kv, qd, qblock):
    vmem = pl.BlockSpec(memory_space=pltpu.VMEM)
    keys, queries = 8 * T, 4 * T
    return pl.pallas_call(
        attention_kernel,
        out_shape=(
            jax.ShapeDtypeStruct((4, HD, T), BF),
            jax.ShapeDtypeStruct((4, HD, T), BF),
            jax.ShapeDtypeStruct((8, 2 * HD, T), BF),
        ),
        in_specs=[vmem] * 3,
        out_specs=(vmem, vmem, vmem),
        scratch_shapes=[
            pltpu.VMEM((keys, HD), BF), pltpu.VMEM((keys, HD), BF),
            pltpu.VMEM((HD, keys), BF), pltpu.VMEM((HD, keys), BF),
            pltpu.VMEM((HD, queries), BF), pltpu.VMEM((HD, queries), BF),
            pltpu.VMEM((HD, queries), BF), pltpu.VMEM((HD, queries), BF),
            pltpu.VMEM((64, queries), F32),
            pltpu.VMEM((keys, HD), F32), pltpu.VMEM((keys, HD), F32),
            pltpu.VMEM((keys, QC), F32), pltpu.VMEM((keys, QC), BF),
        ],
        compiler_params=pltpu.CompilerParams(vmem_limit_bytes=48 << 20),
        name="attention_both",
    )(kv, qd, qblock)


def finish_kernel(
    frames, cot, w3, taps, bg_t, frames_t, o_in, dq_in, dkv_in,
    enc_out, pg_out, kg_out,
    mix_r, dq_r, dkv_r, op_s, op_r, g_s, g_r, h1, s1_r, h2, s2_r, rpad, res, halo, tapsf, enc, kacc, kg, kr, kgy,
    a_s, a_r, b_s, b_r, c_s, c_r, ls, os_, or_, gs, gr, s1s, s1r, s2s, s2r, hs, hr, es, er, ks, kr_s, ys, yr,
):
    dp, tm, hd = place()
    zl, core = dp // 2, lax.rem(dp, 2)
    x, zh = tm // 2, lax.rem(tm, 2)
    z = zh * 2 + zl
    at_tm = lambda k: (dp, lax.rem(tm + k, 8), hd)
    at_x = lambda k: (dp, lax.rem(x + k, 4) * 2 + zh, hd)
    at_y = lambda k: (dp, tm, lax.rem(hd + k, 4))

    def at_z(k):
        to = lax.rem(z + k, 4)
        return (lax.rem(to, 2) * 2 + core, x * 2 + to // 2, hd)

    me = dp * 8 + tm

    def at_plane(k):
        to = lax.rem(me + k, 32)
        return (to // 8, lax.rem(to, 8), hd)

    partner = (zl * 2 + 1 - core, tm, hd)
    greet([at_plane(k) for k in range(1, 32)] + [at_y(k) for k in range(1, 4)])

    waits = []

    def go(c):
        c.start()
        return c

    mix_c, dq_c, dkv_c = [], [], []
    for k in range(1, 4):
        xo = lax.rem(x + k, 4)
        mix_c.append(go(remote(o_in.at[xo], mix_r.at[x], a_s.at[k], a_r.at[k], at_x(k))))
    mix_c.append(go(pltpu.make_async_copy(o_in.at[x], mix_r.at[x], ls.at[0])))
    for k in range(1, 4):
        xo = lax.rem(x + k, 4)
        dq_c.append(go(remote(dq_in.at[xo], dq_r.at[x], b_s.at[k], b_r.at[k], at_x(k))))
    dq_c.append(go(pltpu.make_async_copy(dq_in.at[x], dq_r.at[x], ls.at[1])))
    for k in range(1, 8):
        to = lax.rem(tm + k, 8)
        dkv_c.append(go(remote(dkv_in.at[to], dkv_r.at[zh, x], c_s.at[k], c_r.at[k], at_tm(k))))
    dkv_c.append(go(pltpu.make_async_copy(dkv_in.at[tm], dkv_r.at[zh, x], ls.at[2])))

    tapsf[...] = taps[:, pl.ds(pl.multiple_of(hd * F, 128), F)].astype(F32)
    kacc[...] = jnp.zeros_like(kacc)

    for c in mix_c:
        c.wait()
    mixed = mix_r[...].reshape(F, T).T
    nt = (((1,), (1,)), ((), ()))
    op_c = []
    for k in range(1, 4):
        rows = pl.ds(pl.multiple_of(lax.rem(hd + k, 4) * F, F), F)
        op_s[k] = lax.dot_general(mixed, w3[rows, :], nt, preferred_element_type=F32).astype(BF)
        op_c.append(go(remote(op_s.at[k], op_r.at[k], os_.at[k], or_.at[k], at_y(k))))

    def away(p, left, right):
        for l in range(2):
            rows = pl.ds(pl.multiple_of((l * 2 + 1 - core) * F, F), F)
            g_s[p, l] = jnp.dot(left[rows, :], right, preferred_element_type=F32).astype(BF)
        return go(remote(g_s.at[p], g_r.at[p], gs.at[p], gr.at[p], partner))

    def keep(p, left, right, copy, by_x):
        copy.wait()
        for l in range(2):
            rows = pl.ds(pl.multiple_of((l * 2 + core) * F, F), F)
            g = jnp.dot(left[rows, :], right, preferred_element_type=F32) + g_r[p, l].astype(F32)
            g = g.astype(BF)
            for xo in range(4):
                for h in range(2):
                    piece = g[xo * 96 + h * 48 : xo * 96 + h * 48 + 48]
                    if by_x:
                        h1[p, xo * 4 + h * 2 + l] = piece
                    else:
                        h1[p, (h * 2 + l) * 4 + xo] = piece
        out = []
        for k in range(1, 4):
            to = lax.rem((x if by_x else z) + k, 4)
            device = at_x(k) if by_x else at_z(k)
            out.append(
                go(remote(h1.at[p, pl.ds(to * 4, 4)], s1_r.at[p, k], s1s.at[p, k], s1r.at[p, k], device))
            )
        return out

    def second(p, copies, by_x):
        for c in copies:
            c.wait()
        own = h1[p, pl.ds((x if by_x else z) * 4, 4)].astype(F32)
        for k in range(1, 4):
            own = own + s1_r[p, k].astype(F32)
        h2[p] = own.astype(BF)
        out = []
        for k in range(1, 4):
            to = lax.rem((z if by_x else x) + k, 4)
            device = at_z(k) if by_x else at_x(k)
            out.append(go(remote(h2.at[p, to], s2_r.at[p, k], s2s.at[p, k], s2r.at[p, k], device)))
        return out

    def last(p, copies, by_x):
        for c in copies:
            c.wait()
        own = h2[p, z if by_x else x].astype(F32)
        for k in range(1, 4):
            own = own + s2_r[p, k].astype(F32)
        pg_out[p] = own

    g3 = away(3, bg_t, mixed)
    for c in dq_c:
        c.wait()
    dq = dq_r[...].reshape(F, T).T
    g0 = away(0, frames_t, dq)
    r3 = keep(3, bg_t, mixed, g3, True)
    r0 = keep(0, frames_t, dq, g0, False)

    rows = pl.ds(pl.multiple_of(hd * F, F), F)
    summed = lax.dot_general(mixed, w3[rows, :], nt, preferred_element_type=F32)
    for c in op_c:
        c.wait()
    for k in range(1, 4):
        summed = summed + op_r[k].astype(F32)
    lanes = pl.ds(pl.multiple_of(hd * F, 128), F)
    res[...] = (frames[:, lanes].astype(F32) + summed).astype(BF)
    halos = [
        go(remote(res.at[T - HALF : T], halo.at[0], hs.at[0], hr.at[0], at_tm(1))),
        go(remote(res.at[0:HALF], halo.at[1], hs.at[1], hr.at[1], at_tm(7))),
    ]

    for c in dkv_c:
        c.wait()
    both = (dkv_r[0].astype(F32) + dkv_r[1].astype(F32)).astype(BF)
    dk = both[:, 0:HD].reshape(F, T).T
    dv = both[:, HD:].reshape(F, T).T
    g1 = away(1, frames_t, dk)
    g2 = away(2, frames_t, dv)
    r1 = keep(1, frames_t, dk, g1, True)
    r2 = keep(2, frames_t, dv, g2, False)

    rpad[HALF : HALF + T] = res[...].astype(F32)
    for c in halos:
        c.wait()
    rpad[0:HALF] = jnp.where(tm > 0, halo[0].astype(F32), 0.0)
    rpad[HALF + T :] = jnp.where(tm < 7, halo[1].astype(F32), 0.0)
    offsets = {j: j for j in range(KW)}

    def conv(it, carry):
        i, l = it // 3, lax.rem(it, 3)
        lane = pl.ds(pl.multiple_of(l * 128, 128), 128)
        window = rpad[pl.ds(pl.multiple_of(i * 64, 64), 96), lane]
        up = cot[
            pl.ds(pl.multiple_of(i * 64, 64), 64), pl.ds(pl.multiple_of(hd * F + l * 128, 128), 128)
        ].astype(F32)
        acc = window[HALF : HALF + 64]
        for j, rows in tap_terms(window, offsets):
            acc = acc + tapsf[j : j + 1, lane] * rows
            kacc[j, :, lane] += jnp.sum((up * rows).reshape(8, 8, 128), axis=0)
        enc[pl.ds(pl.multiple_of(i * 64, 64), 64), lane] = acc.astype(BF)
        return carry

    lax.fori_loop(0, 18, conv, 0)
    enc_c = [go(pltpu.make_async_copy(enc, enc_out.at[:, lanes], ls.at[3]))]
    for k in range(1, 4):
        enc_c.append(go(remote(enc, enc_out.at[:, lanes], es.at[k], er.at[k], at_y(k))))
    for j in range(KW):
        kg[j] = jnp.sum(kacc[j], axis=0, keepdims=True)
    kg_c = []
    for k in range(1, 32):
        to = lax.rem(me + k, 32)
        kg_c.append(go(remote(kg.at[to], kr.at[k], ks.at[k], kr_s.at[k], at_plane(k))))

    t3 = second(3, r3, True)
    t0 = second(0, r0, False)
    t1 = second(1, r1, True)
    t2 = second(2, r2, False)
    for c in kg_c:
        c.wait()
    total = kg[me]
    for k in range(1, 32):
        total = total + kr[k]
    kgy[hd] = total
    ky_c = [go(remote(kgy.at[hd], kgy.at[hd], ys.at[k], yr.at[k], at_y(k))) for k in range(1, 4)]
    last(3, t3, True)
    last(0, t0, False)
    last(1, t1, True)
    last(2, t2, False)
    for c in ky_c:
        c.wait()
    for y in range(4):
        kg_out[:, y * F : (y + 1) * F] = kgy[y]
    for c in enc_c:
        c.wait()


def finish(frames, cot, w3, taps, bg_t, frames_t, o, dq, dkv):
    vmem = pl.BlockSpec(memory_space=pltpu.VMEM)
    anym = pl.BlockSpec(memory_space=pl.ANY)
    dma = pltpu.SemaphoreType.DMA
    return pl.pallas_call(
        finish_kernel,
        out_shape=(
            jax.ShapeDtypeStruct((T, C), BF),
            jax.ShapeDtypeStruct((4, 48, F), F32),
            jax.ShapeDtypeStruct((1, C), F32),
        ),
        in_specs=[vmem] * 6 + [anym] * 3,
        out_specs=(anym, vmem, vmem),
        scratch_shapes=[
            pltpu.VMEM((4, HD, T), BF),
            pltpu.VMEM((4, HD, T), BF),
            pltpu.VMEM((2, 4, 2 * HD, T), BF),
            pltpu.VMEM((4, T, F), BF),
            pltpu.VMEM((4, T, F), BF),
            pltpu.VMEM((4, 2, F, F), BF),
            pltpu.VMEM((4, 2, F, F), BF),
            pltpu.VMEM((4, 16, 48, F), BF),
            pltpu.VMEM((4, 4, 4, 48, F), BF),
            pltpu.VMEM((4, 4, 48, F), BF),
            pltpu.VMEM((4, 4, 48, F), BF),
            pltpu.VMEM((T + 2 * HALF, F), F32),
            pltpu.VMEM((T, F), BF),
            pltpu.VMEM((2, HALF, F), BF),
            pltpu.VMEM((KW, F), F32),
            pltpu.VMEM((T, F), BF),
            pltpu.VMEM((KW, 8, F), F32),
            pltpu.VMEM((KW, 1, F), F32),
            pltpu.VMEM((KW, 1, F), F32),
            pltpu.VMEM((4, 1, F), F32),
            dma((4,)), dma((4,)), dma((4,)), dma((4,)), dma((8,)), dma((8,)), dma((4,)),
            dma((4,)), dma((4,)), dma((4,)), dma((4,)), dma((4, 4)), dma((4, 4)), dma((4, 4)), dma((4, 4)),
            dma((2,)), dma((2,)), dma((4,)), dma((4,)), dma((32,)), dma((32,)), dma((4,)), dma((4,)),
        ],
        compiler_params=pltpu.CompilerParams(
            collective_id=1, has_side_effects=True, vmem_limit_bytes=48 << 20
        ),
        name="finish_exchange",
    )(frames, cot, w3, taps, bg_t, frames_t, o, dq, dkv)


def shards(frames, projections, kernel, pattern, cotangent):
    source, upstream, rows_pattern = frames[0], cotangent[0], pattern[0]
    phase = jnp.repeat(rows_pattern[:, 0], BLK).astype(BF)
    count = jnp.repeat(jnp.sum((rows_pattern >= 0).astype(jnp.int32), axis=1), BLK).astype(BF)
    row = lax.broadcasted_iota(jnp.int32, (16, T), 0)
    meta = jnp.where(row == 0, phase[None], jnp.where(row == 1, count[None], jnp.zeros((), BF)))
    zh = lax.rem(lax.axis_index("tm"), 2)
    owner = jnp.arange(4)[:, None] * 2 + zh
    qblock = (owner * (T // BLK) + jnp.arange(T)[None, :] // BLK).astype(F32)
    kv, qd, bg_t, frames_t = project(source, upstream, projections, kernel, meta)
    o, dq, dkv = attention(kv, qd, qblock)
    enc, pg, kg = finish(source, upstream, projections[3], kernel, bg_t, frames_t, o, dq, dkv)
    return enc[None], pg, kg


def solution(mesh):
    placed = (
        P("dp", "tm", None),
        P(None, None, "head"),
        P(),
        P("dp", "tm", None),
        P("dp", "tm", None),
    )
    return jax.shard_map(
        shards,
        mesh=mesh,
        in_specs=placed,
        out_specs=(P("dp", "tm", None), P(None, ("dp", "tm"), "head"), P(("dp", "tm"), None)),
        check_vma=False,
    )
```

```python
import jax
import jax.numpy as jnp
from jax import lax
from jax.experimental import pallas as pl
from jax.experimental.pallas import tpu as pltpu
from jax.sharding import PartitionSpec as P

HD = 96
BLK = 64
KW = 32
HALF = KW // 2
T = 384
C = 1536
F = 384
NKB = 48
QC = 768
MESH = pl.DeviceIdType.MESH
BF = jnp.bfloat16
F32 = jnp.float32


def remote(src, dst, ssem, rsem, device):
    return pltpu.make_async_remote_copy(
        src_ref=src, dst_ref=dst, send_sem=ssem, recv_sem=rsem, device_id=device, device_id_type=MESH
    )


def greet(devices):
    barrier = pltpu.get_barrier_semaphore()
    for device in devices:
        pl.semaphore_signal(barrier, inc=1, device_id=device, device_id_type=MESH)
    pl.semaphore_wait(barrier, len(devices))


def place():
    dp, tm, hd = lax.axis_index("dp"), lax.axis_index("tm"), lax.axis_index("head")
    return dp, tm, hd


def tap_terms(window, offsets):
    for r in range(8):
        shifted = window[r : r + 88] if r else window
        for a in range(5):
            o = 8 * a + r
            if o in offsets:
                yield offsets[o], shifted[8 * a : 8 * a + 64]


def project_kernel(
    frames, cot, w, taps, meta, kv_out, qd_out, bg_t, frames_t,
    bg, upad, halo, tapsf, kv_s, q_s, d_s, hs, hr, kvs, kvr, qs, qr, ds, dr, ls,
):
    dp, tm, hd = place()
    x, zh = tm // 2, lax.rem(tm, 2)
    at_tm = lambda k: (dp, lax.rem(tm + k, 8), hd)
    greet([at_tm(k) for k in range(1, 8)])
    halos = [
        remote(cot.at[T - HALF : T], halo.at[0], hs.at[0], hr.at[0], at_tm(1)),
        remote(cot.at[0:HALF], halo.at[1], hs.at[1], hr.at[1], at_tm(7)),
    ]
    for c in halos:
        c.start()

    for p in (1, 2):
        y = jnp.dot(frames[...], w[p], preferred_element_type=F32).astype(BF).T
        for h in range(4):
            kv_s[h, (p - 1) * HD : p * HD, :] = y[h * HD : (h + 1) * HD]
    sends = []
    for k in range(1, 8):
        c = remote(kv_s.at[lax.rem(tm + k, 8) // 2], kv_out.at[tm], kvs.at[k], kvr.at[k], at_tm(k))
        c.start()
        sends.append(c)
    local = [pltpu.make_async_copy(kv_s.at[x], kv_out.at[tm], ls.at[0])]
    local[0].start()

    y = jnp.dot(frames[...], w[0], preferred_element_type=F32).astype(BF).T
    for h in range(4):
        q_s[h] = y[h * HD : (h + 1) * HD]
    for k in range(1, 4):
        xo = lax.rem(x + k, 4)
        c = remote(q_s.at[xo], qd_out.at[x, 0:HD], qs.at[k], qr.at[k], (dp, xo * 2 + zh, hd))
        c.start()
        sends.append(c)
    c = pltpu.make_async_copy(q_s.at[x], qd_out.at[x, 0:HD], ls.at[1])
    c.start()
    local.append(c)

    tapsf[...] = taps[...].astype(F32)
    upad[HALF : HALF + T] = cot[...].astype(F32)
    for c in halos:
        c.wait()
    upad[0:HALF] = jnp.where(tm > 0, halo[0].astype(F32), 0.0)
    upad[HALF + T :] = jnp.where(tm < 7, halo[1].astype(F32), 0.0)
    offsets = {2 * HALF - j: j for j in range(KW)}

    def conv(it, carry):
        i, l = it // 12, lax.rem(it, 12)
        lanes = pl.ds(pl.multiple_of(l * 128, 128), 128)
        window = upad[pl.ds(pl.multiple_of(i * 64, 64), 96), lanes]
        acc = window[HALF : HALF + 64]
        for j, rows in tap_terms(window, offsets):
            acc = acc + tapsf[j : j + 1, lanes] * rows
        bg[pl.ds(pl.multiple_of(i * 64, 64), 64), lanes] = acc.astype(BF)
        return carry

    lax.fori_loop(0, 72, conv, 0)
    y = jnp.dot(bg[...], w[3], preferred_element_type=F32).astype(BF).T
    for h in range(4):
        d_s[h, 0:HD] = y[h * HD : (h + 1) * HD]
        d_s[h, HD:] = meta[...]
    for k in range(1, 4):
        xo = lax.rem(x + k, 4)
        c = remote(d_s.at[xo], qd_out.at[x, HD:], ds.at[k], dr.at[k], (dp, xo * 2 + zh, hd))
        c.start()
        sends.append(c)
    c = pltpu.make_async_copy(d_s.at[x], qd_out.at[x, HD:], ls.at[2])
    c.start()
    local.append(c)

    frames_t[...] = frames[...].T
    bg_t[...] = bg[...].T
    for c in local:
        c.wait()
    for c in sends:
        c.wait()


def project(frames, cot, w, taps, meta):
    vmem = pl.BlockSpec(memory_space=pltpu.VMEM)
    anym = pl.BlockSpec(memory_space=pl.ANY)
    dma = pltpu.SemaphoreType.DMA
    return pl.pallas_call(
        project_kernel,
        out_shape=(
            jax.ShapeDtypeStruct((8, 2 * HD, T), BF),
            jax.ShapeDtypeStruct((4, 2 * HD + 16, T), BF),
            jax.ShapeDtypeStruct((C, T), BF),
            jax.ShapeDtypeStruct((C, T), BF),
        ),
        in_specs=[vmem] * 5,
        out_specs=(anym, anym, vmem, vmem),
        scratch_shapes=[
            pltpu.VMEM((T, C), BF),
            pltpu.VMEM((T + 2 * HALF, C), F32),
            pltpu.VMEM((2, HALF, C), BF),
            pltpu.VMEM((KW, C), F32),
            pltpu.VMEM((4, 2 * HD, T), BF),
            pltpu.VMEM((4, HD, T), BF),
            pltpu.VMEM((4, HD + 16, T), BF),
            dma((2,)), dma((2,)), dma((8,)), dma((8,)), dma((4,)), dma((4,)), dma((4,)), dma((4,)), dma((3,)),
        ],
        compiler_params=pltpu.CompilerParams(
            collective_id=0, has_side_effects=True, vmem_limit_bytes=48 << 20
        ),
        name="project_exchange",
    )(frames, cot, w, taps, meta)


def attention_kernel(
    kv, qd, qblock, o_out, dq_out, dkv_out,
    kn, vn, kt, vt, qt, dt, on, dqn, live, dk, dv, st, et,
):
    scale = HD ** -0.5
    c2 = scale * 1.4426950408889634
    for t in range(8):
        kt[:, t * T : (t + 1) * T] = kv[t, 0:HD]
        vt[:, t * T : (t + 1) * T] = kv[t, HD:]
        kn[t * T : (t + 1) * T, :] = kv[t, 0:HD].T
        vn[t * T : (t + 1) * T, :] = kv[t, HD:].T
    for a in range(4):
        lanes = slice(a * T, (a + 1) * T)
        qt[:, lanes] = qd[a, 0:HD]
        dt[:, lanes] = qd[a, HD : 2 * HD]
        meta = qd[a, 2 * HD :].astype(F32)
        phase, count = meta[0:1], meta[1:2]
        row = lax.broadcasted_iota(jnp.int32, (64, T), 0)
        kb = (row // 8) * 6 + lax.rem(row, 8)
        far = (lax.rem(kb, 4).astype(F32) == phase) & ((kb // 4).astype(F32) < count)
        near = jnp.abs(kb.astype(F32) - qblock[a : a + 1]) < 1.5
        live[:, lanes] = jnp.where(far | near, 1.0, 0.0)
    dk[...] = jnp.zeros_like(dk)
    dv[...] = jnp.zeros_like(dv)

    def step(c, carry):
        lanes = pl.ds(pl.multiple_of(c * QC, QC), QC)
        q_t = qt[:, lanes]

        def scores(t, top):
            rows = pl.ds(pl.multiple_of(t * T, T), T)
            s = jnp.dot(kn[rows, :], q_t, preferred_element_type=F32)
            mask = live[pl.ds(pl.multiple_of(t * 8, 8), 8), lanes]
            parts = []
            for b in range(6):
                part = jnp.where(mask[b : b + 1] > 0.5, s[b * BLK : (b + 1) * BLK], -1e30)
                top = jnp.maximum(top, jnp.max(part.reshape(8, 8, QC), axis=0))
                parts.append(part)
            st[rows, :] = jnp.concatenate(parts, axis=0)
            return top

        top = lax.fori_loop(0, 8, scores, jnp.full((8, QC), -jnp.inf, F32), unroll=8)
        top = jnp.max(top, axis=0, keepdims=True) * c2

        def weigh(t, carry):
            total, o = carry
            rows = pl.ds(pl.multiple_of(t * T, T), T)
            e = jnp.exp2(st[rows, :] * c2 - top)
            total = total + jnp.sum(e.reshape(T // 8, 8, QC), axis=0)
            eb = e.astype(BF)
            et[rows, :] = eb
            o = o + jnp.dot(vt[:, pl.ds(pl.multiple_of(t * T, T), T)], eb, preferred_element_type=F32)
            return total, o

        total, o = lax.fori_loop(
            0, 8, weigh, (jnp.zeros((8, QC), F32), jnp.zeros((HD, QC), F32)), unroll=8
        )
        inverse = 1.0 / jnp.sum(total, axis=0, keepdims=True)
        o = (o * inverse).astype(BF)
        on[:, lanes] = o
        d = dt[:, lanes].astype(F32)
        delta = jnp.sum(d * o.astype(F32), axis=0, keepdims=True) * inverse
        d_t = (d * inverse).astype(BF)
        d_n = d_t.T
        q_n = q_t.T

        def back(t, dq):
            rows = pl.ds(pl.multiple_of(t * T, T), T)
            eb = et[rows, :]
            dp = jnp.dot(vn[rows, :], d_t, preferred_element_type=F32)
            ds = (eb.astype(F32) * (dp - delta)).astype(BF)
            dk[rows, :] += jnp.dot(ds, q_n, preferred_element_type=F32)
            dv[rows, :] += jnp.dot(eb, d_n, preferred_element_type=F32)
            return dq + jnp.dot(
                kt[:, pl.ds(pl.multiple_of(t * T, T), T)], ds, preferred_element_type=F32
            )

        dq = lax.fori_loop(0, 8, back, jnp.zeros((HD, QC), F32), unroll=8)
        dqn[:, lanes] = (dq * scale).astype(BF)
        return carry

    lax.fori_loop(0, 4 * T // QC, step, 0)
    for a in range(4):
        lanes = slice(a * T, (a + 1) * T)
        o_out[a] = on[:, lanes]
        dq_out[a] = dqn[:, lanes]
    for t in range(8):
        dkv_out[t, 0:HD] = (dk[t * T : (t + 1) * T, :] * scale).astype(BF).T
        dkv_out[t, HD:] = dv[t * T : (t + 1) * T, :].astype(BF).T


def attention(kv, qd, qblock):
    vmem = pl.BlockSpec(memory_space=pltpu.VMEM)
    keys, queries = 8 * T, 4 * T
    return pl.pallas_call(
        attention_kernel,
        out_shape=(
            jax.ShapeDtypeStruct((4, HD, T), BF),
            jax.ShapeDtypeStruct((4, HD, T), BF),
            jax.ShapeDtypeStruct((8, 2 * HD, T), BF),
        ),
        in_specs=[vmem] * 3,
        out_specs=(vmem, vmem, vmem),
        scratch_shapes=[
            pltpu.VMEM((keys, HD), BF), pltpu.VMEM((keys, HD), BF),
            pltpu.VMEM((HD, keys), BF), pltpu.VMEM((HD, keys), BF),
            pltpu.VMEM((HD, queries), BF), pltpu.VMEM((HD, queries), BF),
            pltpu.VMEM((HD, queries), BF), pltpu.VMEM((HD, queries), BF),
            pltpu.VMEM((64, queries), F32),
            pltpu.VMEM((keys, HD), F32), pltpu.VMEM((keys, HD), F32),
            pltpu.VMEM((keys, QC), F32), pltpu.VMEM((keys, QC), BF),
        ],
        compiler_params=pltpu.CompilerParams(vmem_limit_bytes=48 << 20),
        name="attention_both",
    )(kv, qd, qblock)


def finish_kernel(
    frames, cot, w3, taps, bg_t, frames_t, o_in, dq_in, dkv_in,
    enc_out, pg_out, kg_out,
    mix_r, dq_r, dkv_r, op_s, op_r, g_s, g_r, h1, s1_r, h2, s2_r, rpad, res, halo, tapsf, enc, kacc, kg, kr, kgy,
    a_s, a_r, b_s, b_r, c_s, c_r, ls, os_, or_, gs, gr, s1s, s1r, s2s, s2r, hs, hr, es, er, ks, kr_s, ys, yr,
):
    dp, tm, hd = place()
    zl, core = dp // 2, lax.rem(dp, 2)
    x, zh = tm // 2, lax.rem(tm, 2)
    z = zh * 2 + zl
    at_tm = lambda k: (dp, lax.rem(tm + k, 8), hd)
    at_x = lambda k: (dp, lax.rem(x + k, 4) * 2 + zh, hd)
    at_y = lambda k: (dp, tm, lax.rem(hd + k, 4))

    def at_z(k):
        to = lax.rem(z + k, 4)
        return (lax.rem(to, 2) * 2 + core, x * 2 + to // 2, hd)

    me = dp * 8 + tm

    def at_plane(k):
        to = lax.rem(me + k, 32)
        return (to // 8, lax.rem(to, 8), hd)

    partner = (zl * 2 + 1 - core, tm, hd)
    greet([at_plane(k) for k in range(1, 32)] + [at_y(k) for k in range(1, 4)])

    waits = []

    def go(c):
        c.start()
        return c

    mix_c, dq_c, dkv_c = [], [], []
    for k in range(1, 4):
        xo = lax.rem(x + k, 4)
        mix_c.append(go(remote(o_in.at[xo], mix_r.at[x], a_s.at[k], a_r.at[k], at_x(k))))
    mix_c.append(go(pltpu.make_async_copy(o_in.at[x], mix_r.at[x], ls.at[0])))
    for k in range(1, 4):
        xo = lax.rem(x + k, 4)
        dq_c.append(go(remote(dq_in.at[xo], dq_r.at[x], b_s.at[k], b_r.at[k], at_x(k))))
    dq_c.append(go(pltpu.make_async_copy(dq_in.at[x], dq_r.at[x], ls.at[1])))
    for k in range(1, 8):
        to = lax.rem(tm + k, 8)
        dkv_c.append(go(remote(dkv_in.at[to], dkv_r.at[zh, x], c_s.at[k], c_r.at[k], at_tm(k))))
    dkv_c.append(go(pltpu.make_async_copy(dkv_in.at[tm], dkv_r.at[zh, x], ls.at[2])))

    tapsf[...] = taps[:, pl.ds(pl.multiple_of(hd * F, 128), F)].astype(F32)
    kacc[...] = jnp.zeros_like(kacc)

    for c in mix_c:
        c.wait()
    mixed = mix_r[...].reshape(F, T).T
    nt = (((1,), (1,)), ((), ()))
    op_c = []
    for k in range(1, 4):
        rows = pl.ds(pl.multiple_of(lax.rem(hd + k, 4) * F, F), F)
        op_s[k] = lax.dot_general(mixed, w3[rows, :], nt, preferred_element_type=F32).astype(BF)
        op_c.append(go(remote(op_s.at[k], op_r.at[k], os_.at[k], or_.at[k], at_y(k))))

    def away(p, left, right):
        for l in range(2):
            rows = pl.ds(pl.multiple_of((l * 2 + 1 - core) * F, F), F)
            g_s[p, l] = jnp.dot(left[rows, :], right, preferred_element_type=F32).astype(BF)
        return go(remote(g_s.at[p], g_r.at[p], gs.at[p], gr.at[p], partner))

    def keep(p, left, right, copy, by_x):
        copy.wait()
        for l in range(2):
            rows = pl.ds(pl.multiple_of((l * 2 + core) * F, F), F)
            g = jnp.dot(left[rows, :], right, preferred_element_type=F32) + g_r[p, l].astype(F32)
            g = g.astype(BF)
            for xo in range(4):
                for h in range(2):
                    piece = g[xo * 96 + h * 48 : xo * 96 + h * 48 + 48]
                    if by_x:
                        h1[p, xo * 4 + h * 2 + l] = piece
                    else:
                        h1[p, (h * 2 + l) * 4 + xo] = piece
        out = []
        for k in range(1, 4):
            to = lax.rem((x if by_x else z) + k, 4)
            device = at_x(k) if by_x else at_z(k)
            out.append(
                go(remote(h1.at[p, pl.ds(to * 4, 4)], s1_r.at[p, k], s1s.at[p, k], s1r.at[p, k], device))
            )
        return out

    def second(p, copies, by_x):
        for c in copies:
            c.wait()
        own = h1[p, pl.ds((x if by_x else z) * 4, 4)].astype(F32)
        for k in range(1, 4):
            own = own + s1_r[p, k].astype(F32)
        h2[p] = own.astype(BF)
        out = []
        for k in range(1, 4):
            to = lax.rem((z if by_x else x) + k, 4)
            device = at_z(k) if by_x else at_x(k)
            out.append(go(remote(h2.at[p, to], s2_r.at[p, k], s2s.at[p, k], s2r.at[p, k], device)))
        return out

    def last(p, copies, by_x):
        for c in copies:
            c.wait()
        own = h2[p, z if by_x else x].astype(F32)
        for k in range(1, 4):
            own = own + s2_r[p, k].astype(F32)
        pg_out[p] = own

    g3 = away(3, bg_t, mixed)
    for c in dq_c:
        c.wait()
    dq = dq_r[...].reshape(F, T).T
    g0 = away(0, frames_t, dq)
    r3 = keep(3, bg_t, mixed, g3, True)
    r0 = keep(0, frames_t, dq, g0, False)

    rows = pl.ds(pl.multiple_of(hd * F, F), F)
    summed = lax.dot_general(mixed, w3[rows, :], nt, preferred_element_type=F32)
    for c in op_c:
        c.wait()
    for k in range(1, 4):
        summed = summed + op_r[k].astype(F32)
    lanes = pl.ds(pl.multiple_of(hd * F, 128), F)
    res[...] = (frames[:, lanes].astype(F32) + summed).astype(BF)
    halos = [
        go(remote(res.at[T - HALF : T], halo.at[0], hs.at[0], hr.at[0], at_tm(1))),
        go(remote(res.at[0:HALF], halo.at[1], hs.at[1], hr.at[1], at_tm(7))),
    ]

    for c in dkv_c:
        c.wait()
    both = (dkv_r[0].astype(F32) + dkv_r[1].astype(F32)).astype(BF)
    dk = both[:, 0:HD].reshape(F, T).T
    dv = both[:, HD:].reshape(F, T).T
    g1 = away(1, frames_t, dk)
    g2 = away(2, frames_t, dv)
    r1 = keep(1, frames_t, dk, g1, True)
    r2 = keep(2, frames_t, dv, g2, False)

    rpad[HALF : HALF + T] = res[...].astype(F32)
    for c in halos:
        c.wait()
    rpad[0:HALF] = jnp.where(tm > 0, halo[0].astype(F32), 0.0)
    rpad[HALF + T :] = jnp.where(tm < 7, halo[1].astype(F32), 0.0)
    offsets = {j: j for j in range(KW)}

    def conv(it, carry):
        i, l = it // 3, lax.rem(it, 3)
        lane = pl.ds(pl.multiple_of(l * 128, 128), 128)
        window = rpad[pl.ds(pl.multiple_of(i * 64, 64), 96), lane]
        up = cot[
            pl.ds(pl.multiple_of(i * 64, 64), 64), pl.ds(pl.multiple_of(hd * F + l * 128, 128), 128)
        ].astype(F32)
        acc = window[HALF : HALF + 64]
        for j, rows in tap_terms(window, offsets):
            acc = acc + tapsf[j : j + 1, lane] * rows
            kacc[j, :, lane] += jnp.sum((up * rows).reshape(8, 8, 128), axis=0)
        enc[pl.ds(pl.multiple_of(i * 64, 64), 64), lane] = acc.astype(BF)
        return carry

    lax.fori_loop(0, 18, conv, 0)
    enc_c = [go(pltpu.make_async_copy(enc, enc_out.at[:, lanes], ls.at[3]))]
    for k in range(1, 4):
        enc_c.append(go(remote(enc, enc_out.at[:, lanes], es.at[k], er.at[k], at_y(k))))
    for j in range(KW):
        kg[j] = jnp.sum(kacc[j], axis=0, keepdims=True)
    kg_c = []
    for k in range(1, 32):
        to = lax.rem(me + k, 32)
        kg_c.append(go(remote(kg.at[to], kr.at[k], ks.at[k], kr_s.at[k], at_plane(k))))

    t3 = second(3, r3, True)
    t0 = second(0, r0, False)
    t1 = second(1, r1, True)
    t2 = second(2, r2, False)
    for c in kg_c:
        c.wait()
    total = kg[me]
    for k in range(1, 32):
        total = total + kr[k]
    kgy[hd] = total
    ky_c = [go(remote(kgy.at[hd], kgy.at[hd], ys.at[k], yr.at[k], at_y(k))) for k in range(1, 4)]
    last(3, t3, True)
    last(0, t0, False)
    last(1, t1, True)
    last(2, t2, False)
    for c in ky_c:
        c.wait()
    for y in range(4):
        kg_out[:, y * F : (y + 1) * F] = kgy[y]
    for c in enc_c:
        c.wait()


def finish(frames, cot, w3, taps, bg_t, frames_t, o, dq, dkv):
    vmem = pl.BlockSpec(memory_space=pltpu.VMEM)
    anym = pl.BlockSpec(memory_space=pl.ANY)
    dma = pltpu.SemaphoreType.DMA
    return pl.pallas_call(
        finish_kernel,
        out_shape=(
            jax.ShapeDtypeStruct((T, C), BF),
            jax.ShapeDtypeStruct((4, 48, F), F32),
            jax.ShapeDtypeStruct((1, C), F32),
        ),
        in_specs=[vmem] * 6 + [anym] * 3,
        out_specs=(anym, vmem, vmem),
        scratch_shapes=[
            pltpu.VMEM((4, HD, T), BF),
            pltpu.VMEM((4, HD, T), BF),
            pltpu.VMEM((2, 4, 2 * HD, T), BF),
            pltpu.VMEM((4, T, F), BF),
            pltpu.VMEM((4, T, F), BF),
            pltpu.VMEM((4, 2, F, F), BF),
            pltpu.VMEM((4, 2, F, F), BF),
            pltpu.VMEM((4, 16, 48, F), BF),
            pltpu.VMEM((4, 4, 4, 48, F), BF),
            pltpu.VMEM((4, 4, 48, F), BF),
            pltpu.VMEM((4, 4, 48, F), BF),
            pltpu.VMEM((T + 2 * HALF, F), F32),
            pltpu.VMEM((T, F), BF),
            pltpu.VMEM((2, HALF, F), BF),
            pltpu.VMEM((KW, F), F32),
            pltpu.VMEM((T, F), BF),
            pltpu.VMEM((KW, 8, F), F32),
            pltpu.VMEM((KW, 1, F), F32),
            pltpu.VMEM((KW, 1, F), F32),
            pltpu.VMEM((4, 1, F), F32),
            dma((4,)), dma((4,)), dma((4,)), dma((4,)), dma((8,)), dma((8,)), dma((4,)),
            dma((4,)), dma((4,)), dma((4,)), dma((4,)), dma((4, 4)), dma((4, 4)), dma((4, 4)), dma((4, 4)),
            dma((2,)), dma((2,)), dma((4,)), dma((4,)), dma((32,)), dma((32,)), dma((4,)), dma((4,)),
        ],
        compiler_params=pltpu.CompilerParams(
            collective_id=1, has_side_effects=True, vmem_limit_bytes=48 << 20
        ),
        name="finish_exchange",
    )(frames, cot, w3, taps, bg_t, frames_t, o, dq, dkv)


def shards(frames, projections, kernel, pattern, cotangent):
    source, upstream, rows_pattern = frames[0], cotangent[0], pattern[0]
    phase = jnp.repeat(rows_pattern[:, 0], BLK).astype(BF)
    count = jnp.repeat(jnp.sum((rows_pattern >= 0).astype(jnp.int32), axis=1), BLK).astype(BF)
    row = lax.broadcasted_iota(jnp.int32, (16, T), 0)
    meta = jnp.where(row == 0, phase[None], jnp.where(row == 1, count[None], jnp.zeros((), BF)))
    zh = lax.rem(lax.axis_index("tm"), 2)
    owner = jnp.arange(4)[:, None] * 2 + zh
    qblock = (owner * (T // BLK) + jnp.arange(T)[None, :] // BLK).astype(F32)
    kv, qd, bg_t, frames_t = project(source, upstream, projections, kernel, meta)
    o, dq, dkv = attention(kv, qd, qblock)
    enc, pg, kg = finish(source, upstream, projections[3], kernel, bg_t, frames_t, o, dq, dkv)
    return enc[None], pg, kg


def solution(mesh):
    placed = (
        P("dp", "tm", None),
        P(None, None, "head"),
        P(),
        P("dp", "tm", None),
        P("dp", "tm", None),
    )
    return jax.shard_map(
        shards,
        mesh=mesh,
        in_specs=placed,
        out_specs=(P("dp", "tm", None), P(None, ("dp", "tm"), "head"), P(("dp", "tm"), None)),
        check_vma=False,
    )
```

```python
import types

import jax
import jax.numpy as jnp
from jax import lax
from jax.experimental import pallas as pl
from jax.experimental.pallas import tpu as pltpu
from jax.sharding import PartitionSpec as P

HD = 96
BLK = 64
KW = 32
HALF = KW // 2
T = 384
C = 1536
F = 384
Q = 4 * T
QC = 768
MESH = pl.DeviceIdType.MESH
BF = jnp.bfloat16
F32 = jnp.float32
SCALE = HD**-0.5
NT = (((1,), (1,)), ((), ()))


def dma(*shape):
    return pltpu.SemaphoreType.DMA(shape)


def vm(dtype, *shape):
    return pltpu.VMEM(shape, dtype)


SCRATCH = dict(
    frames=vm(BF, T, C), cot=vm(BF, T, C), w=vm(BF, 4, C, F), taps=vm(BF, KW, C), pattern=vm(jnp.int32, 1, 6, 12),
    in_sem=dma(9),
    upad=vm(F32, T + 2 * HALF, C), uhalo=vm(BF, 2, HALF, C), tapsf=vm(F32, KW, C),
    bg=vm(BF, T, C), bg_t=vm(BF, C, T), frames_t=vm(BF, C, T), uh_s=dma(2), uh_r=dma(2),
    q_s=vm(BF, 4, HD + 16, T), k_s=vm(BF, 4, HD, T), v_s=vm(BF, 4, HD, T), d_s=vm(BF, 4, HD, T),
    q_r=vm(BF, 4, HD + 16, T), d_r=vm(BF, 4, HD, T), k_r=vm(BF, 8, HD, T), v_r=vm(BF, 8, HD, T),
    qs=dma(4), qr=dma(4), ks=dma(4), kr=dma(4), vs=dma(4), vr=dma(4), ds=dma(4), dr=dma(4),
    fks=dma(4), fkr=dma(4), fvs=dma(4), fvr=dma(4),
    kn=vm(BF, 8, T, HD), vn=vm(BF, 8, T, HD), qt=vm(BF, HD, Q), qn=vm(BF, Q, HD), dt=vm(BF, HD, Q), dn=vm(BF, Q, HD),
    live=vm(F32, 64, Q), st=vm(F32, 8, T, QC), et=vm(BF, 8, T, Q), dsb=vm(BF, 2, T, Q), dq=vm(F32, HD, Q),
    inverse=vm(F32, 1, Q), delta=vm(F32, 1, Q),
    o_s=vm(BF, 4, HD, T), dq_s=vm(BF, 4, HD, T), part_s=vm(BF, 4, 2 * HD, T), part_r=vm(BF, 4, 2 * HD, T),
    dkv_s=vm(BF, 4, 2 * HD, T), mix_r=vm(BF, 4, HD, T), dq_r=vm(BF, 4, HD, T), dkv_r=vm(BF, 4, 2 * HD, T),
    os=dma(4), orr=dma(4), dqs=dma(4), dqr=dma(4), ps=dma(4), pr=dma(4), dkvs=dma(4), dkvr=dma(4),
    op_s=vm(BF, 3, T, F), op_r=vm(BF, 3, T, F), ops=dma(3), opr=dma(3),
    rpad=vm(F32, T + 2 * HALF, F), res=vm(BF, T, F), rhalo=vm(BF, 2, HALF, F), enc=vm(BF, T, F),
    rh_s=dma(2), rh_r=dma(2), es=dma(4), er=dma(4),
    kacc=vm(F32, KW, 8, F), kg=vm(F32, KW, 1, F), kgr=vm(F32, KW, 1, F), kgy=vm(F32, 4, 1, F),
    kgs=dma(32), kgrs=dma(32), kys=dma(4), kyr=dma(4),
    g_s=vm(BF, 4, 2, F, F), g_r=vm(BF, 4, 2, F, F), gs=dma(4), gr=dma(4),
    h1=vm(BF, 4, 16, 48, F), s1=vm(BF, 4, 3, 4, 48, F), h2=vm(BF, 4, 4, 48, F), s2=vm(BF, 4, 3, 48, F),
    s1s=dma(4, 4), s1r=dma(4, 4), s2s=dma(4, 4), s2r=dma(4, 4),
)


def remote(src, dst, ssem, rsem, device):
    return pltpu.make_async_remote_copy(
        src_ref=src, dst_ref=dst, send_sem=ssem, recv_sem=rsem, device_id=device, device_id_type=MESH
    )


class Either:
    def __init__(self, here, src, dst, ssem, rsem, device):
        self.here = here
        self.local = pltpu.make_async_copy(src, dst, rsem)
        self.far = remote(src, dst, ssem, rsem, device)

    def start(self):
        pl.when(self.here)(lambda: self.local.start())
        pl.when(jnp.logical_not(self.here))(lambda: self.far.start())

    def wait(self):
        pl.when(self.here)(lambda: self.local.wait())
        pl.when(jnp.logical_not(self.here))(lambda: self.far.wait())


def go(copy):
    copy.start()
    return copy


def wait_all(copies):
    for c in copies:
        c.wait()


def tap_terms(window, offsets):
    for r in range(8):
        shifted = window[r : r + 88] if r else window
        for a in range(5):
            o = 8 * a + r
            if o in offsets:
                yield offsets[o], shifted[8 * a : 8 * a + 64]


def aligned(start, size, by):
    return pl.ds(pl.multiple_of(start, by), size)


def layer_kernel(frames_h, w_h, taps_h, pattern_h, cot_h, enc_out, pg_out, kg_out, *scratch):
    s = types.SimpleNamespace(**dict(zip(SCRATCH, scratch)))
    dp, tm, hd = lax.axis_index("dp"), lax.axis_index("tm"), lax.axis_index("head")
    zl, core = dp // 2, lax.rem(dp, 2)
    x, zh = tm // 2, lax.rem(tm, 2)
    z = zh * 2 + zl
    me = dp * 8 + tm
    around = lambda k: lax.rem(x + k, 4)
    at_tm = lambda k: (dp, lax.rem(tm + k, 8), hd)
    at_x = lambda k: (dp, around(k) * 2 + zh, hd)
    at_y = lambda k: (dp, tm, lax.rem(hd + k, 4))
    sibling = (zl * 2 + 1 - core, tm, hd)

    def at_z(k):
        to = lax.rem(z + k, 4)
        return (lax.rem(to, 2) * 2 + core, x * 2 + to // 2, hd)

    def at_plane(k):
        to = lax.rem(me + k, 32)
        return (to // 8, lax.rem(to, 8), hd)

    def swapped(k, src, dst, ssem, rsem):
        device = (zl * 2 + zh, around(k) * 2 + core, hd)
        if k:
            return go(remote(src, dst, ssem.at[k], rsem.at[k], device))
        return go(Either(zh == core, src, dst, ssem.at[0], rsem.at[0], device))

    load = [
        go(pltpu.make_async_copy(a, b, s.in_sem.at[i]))
        for i, (a, b) in enumerate(
            [
                (frames_h.at[0], s.frames),
                (w_h.at[1], s.w.at[1]),
                (w_h.at[0], s.w.at[0]),
                (w_h.at[2], s.w.at[2]),
                (cot_h.at[0], s.cot),
                (taps_h, s.taps),
                (pattern_h, s.pattern),
                (w_h.at[3], s.w.at[3]),
            ]
        )
    ]
    barrier = pltpu.get_barrier_semaphore()
    others = [at_plane(k) for k in range(1, 32)] + [at_y(k) for k in range(1, 4)]
    for device in others:
        pl.semaphore_signal(barrier, inc=1, device_id=device, device_id_type=MESH)

    def projected(rows, p):
        return jnp.dot(rows, s.w[p], preferred_element_type=F32).astype(BF).T

    load[0].wait()
    load[1].wait()
    y = projected(s.frames[...], 1)
    for h in range(4):
        s.k_s[h] = y[h * HD : (h + 1) * HD]
    pl.semaphore_wait(barrier, len(others))
    k_c = [swapped(k, s.k_s.at[around(k)], s.k_r.at[x], s.ks, s.kr) for k in (1, 2, 3, 0)]
    load[4].wait()
    halos = [
        go(remote(s.cot.at[T - HALF : T], s.uhalo.at[0], s.uh_s.at[0], s.uh_r.at[0], at_tm(1))),
        go(remote(s.cot.at[0:HALF], s.uhalo.at[1], s.uh_s.at[1], s.uh_r.at[1], at_tm(7))),
    ]
    load[2].wait()
    load[6].wait()
    y = projected(s.frames[...], 0)
    blocks = s.pattern[0]
    block_of = lax.broadcasted_iota(jnp.int32, (6, T), 1) // BLK == lax.broadcasted_iota(jnp.int32, (6, T), 0)
    spread = lambda column: jnp.sum(jnp.where(block_of, column.astype(F32), 0.0), axis=0, keepdims=True)
    phase = spread(blocks[:, 0:1])
    count = spread(jnp.sum((blocks >= 0).astype(F32), axis=1, keepdims=True))
    row = lax.broadcasted_iota(jnp.int32, (16, T), 0)
    meta = jnp.where(row == 0, phase, jnp.where(row == 1, count, 0.0)).astype(BF)
    for h in range(4):
        s.q_s[h, 0:HD] = y[h * HD : (h + 1) * HD]
        s.q_s[h, HD:] = meta
    q_c = [swapped(k, s.q_s.at[around(k)], s.q_r.at[x], s.qs, s.qr) for k in (1, 2, 3, 0)]
    load[3].wait()
    y = projected(s.frames[...], 2)
    for h in range(4):
        s.v_s[h] = y[h * HD : (h + 1) * HD]
    v_c = [swapped(k, s.v_s.at[around(k)], s.v_r.at[x], s.vs, s.vr) for k in (1, 2, 3, 0)]

    load[5].wait()
    s.tapsf[...] = s.taps[...].astype(F32)
    s.upad[HALF : HALF + T] = s.cot[...].astype(F32)
    wait_all(halos)
    s.upad[0:HALF] = jnp.where(tm > 0, s.uhalo[0].astype(F32), 0.0)
    s.upad[HALF + T :] = jnp.where(tm < 7, s.uhalo[1].astype(F32), 0.0)

    def conv_back(it, carry):
        i, l = it // 12, lax.rem(it, 12)
        lanes = aligned(l * 128, 128, 128)
        window = s.upad[aligned(i * 64, 96, 64), lanes]
        acc = window[HALF : HALF + 64]
        for j, rows in tap_terms(window, {2 * HALF - j: j for j in range(KW)}):
            acc = acc + s.tapsf[j : j + 1, lanes] * rows
        s.bg[aligned(i * 64, 64, 64), lanes] = acc.astype(BF)
        return carry

    lax.fori_loop(0, 72, conv_back, 0)
    load[7].wait()
    y = projected(s.bg[...], 3)
    for h in range(4):
        s.d_s[h] = y[h * HD : (h + 1) * HD]
    d_c = [swapped(k, s.d_s.at[around(k)], s.d_r.at[x], s.ds, s.dr) for k in (1, 2, 3, 0)]

    def forward(k, copy, buf, ssem, rsem):
        copy.wait()
        src = lax.rem(x + 4 - k, 4)
        return go(remote(buf.at[src], buf.at[4 + src], ssem.at[k], rsem.at[k], sibling))

    fk_c = [forward(k, c, s.k_r, s.fks, s.fkr) for k, c in zip((1, 2, 3, 0), k_c)]
    wait_all(q_c)
    for a in range(4):
        lanes = slice(a * T, (a + 1) * T)
        s.qt[:, lanes] = s.q_r[a, 0:HD]
        s.qn[lanes, :] = s.q_r[a, 0:HD].T
        got = s.q_r[a, HD:].astype(F32)
        row = lax.broadcasted_iota(jnp.int32, (64, T), 0)
        tile = row // 8
        owner = lax.rem(tile, 4) * 2 + jnp.where(tile < 4, core, 1 - core)
        key_block = owner * 6 + lax.rem(row, 8)
        query_block = (a * 2 + core) * 6 + lax.broadcasted_iota(jnp.int32, (64, T), 1) // BLK
        far = (lax.rem(key_block, 4).astype(F32) == got[0:1]) & ((key_block // 4).astype(F32) < got[1:2])
        near = jnp.abs(key_block - query_block) < 2
        s.live[:, lanes] = jnp.where(far | near, 1.0, 0.0)
    for t in range(4):
        s.kn[t] = s.k_r[t].T
    fv_c = [forward(k, c, s.v_r, s.fvs, s.fvr) for k, c in zip((1, 2, 3, 0), v_c)]
    wait_all(fk_c)
    for t in range(4, 8):
        s.kn[t] = s.k_r[t].T

    for c in range(Q // QC):
        lanes = slice(c * QC, (c + 1) * QC)
        q_t = s.qt[:, lanes]

        def scores(t, top):
            sc = jnp.dot(s.kn[t], q_t, preferred_element_type=F32)
            mask = s.live[aligned(t * 8, 8, 8), lanes]
            for b in range(6):
                part = jnp.where(mask[b : b + 1] > 0.5, sc[b * BLK : (b + 1) * BLK], -1e30)
                top = jnp.maximum(top, jnp.max(part.reshape(8, 8, QC), axis=0))
                s.st[t, b * BLK : (b + 1) * BLK] = part
            return top

        top = lax.fori_loop(0, 8, scores, jnp.full((8, QC), -jnp.inf, F32), unroll=8)
        c2 = SCALE * 1.4426950408889634
        top = jnp.max(top, axis=0, keepdims=True) * c2
        if c == 0:
            wait_all(fv_c)

        def weigh(t, carry):
            total, o = carry
            e = jnp.exp2(s.st[t] * c2 - top)
            total = total + jnp.sum(e.reshape(T // 8, 8, QC), axis=0)
            eb = e.astype(BF)
            s.et[t, :, lanes] = eb
            return total, o + jnp.dot(s.v_r[t], eb, preferred_element_type=F32)

        total, o = lax.fori_loop(
            0, 8, weigh, (jnp.zeros((8, QC), F32), jnp.zeros((HD, QC), F32)), unroll=8
        )
        inverse = 1.0 / jnp.sum(total, axis=0, keepdims=True)
        s.inverse[:, lanes] = inverse
        o = (o * inverse).astype(BF)
        for a in range(2):
            s.o_s[c * 2 + a] = o[:, a * T : (a + 1) * T]
    o_c = [swapped(k, s.o_s.at[around(k)], s.mix_r.at[x], s.os, s.orr) for k in (1, 2, 3, 0)]

    wait_all(d_c)
    for a in range(4):
        lanes = slice(a * T, (a + 1) * T)
        d = s.d_r[a].astype(F32)
        inverse = s.inverse[:, lanes]
        s.delta[:, lanes] = jnp.sum(d * s.o_s[a].astype(F32), axis=0, keepdims=True) * inverse
        d = (d * inverse).astype(BF)
        s.dt[:, lanes] = d
        s.dn[lanes, :] = d.T
    for t in range(8):
        s.vn[t] = s.v_r[t].T
    s.dq[...] = jnp.zeros_like(s.dq)

    def back(first, k, slot):
        t = first + around(k)
        for c in range(Q // QC):
            lanes = slice(c * QC, (c + 1) * QC)
            dp_ = jnp.dot(s.vn[t], s.dt[:, lanes], preferred_element_type=F32)
            s.dsb[slot, :, lanes] = (s.et[t, :, lanes].astype(F32) * (dp_ - s.delta[:, lanes])).astype(BF)
        dk = jnp.dot(s.dsb[slot], s.qn[...], preferred_element_type=F32) * SCALE
        dv = jnp.dot(s.et[t], s.dn[...], preferred_element_type=F32)
        s.dq[...] += jnp.dot(s.k_r[t], s.dsb[slot], preferred_element_type=F32)
        return dk, dv

    def back_pair(first, ks, out):
        for slot, k in enumerate(ks):
            dk, dv = back(first, k, slot)
            out[around(k), 0:HD] = dk.astype(BF).T
            out[around(k), HD:] = dv.astype(BF).T

    p_c = {}
    for ks in ((1, 2), (3, 0)):
        back_pair(4, ks, s.part_s)
        for k in ks:
            i = around(k)
            p_c[k] = go(remote(s.part_s.at[i], s.part_r.at[i], s.ps.at[k], s.pr.at[k], sibling))

    wait_all(o_c)
    mixed = s.mix_r[...].reshape(F, T).T
    op_c = []
    for k in range(1, 4):
        rows = aligned(lax.rem(hd + k, 4) * F, F, F)
        s.op_s[k - 1] = lax.dot_general(mixed, s.w[3, rows, :], NT, preferred_element_type=F32).astype(BF)
        op_c.append(go(remote(s.op_s.at[k - 1], s.op_r.at[k - 1], s.ops.at[k - 1], s.opr.at[k - 1], at_y(k))))
    s.frames_t[...] = s.frames[...].T
    s.bg_t[...] = s.bg[...].T

    def away(p, left, right):
        for l in range(2):
            rows = aligned((l * 2 + 1 - core) * F, F, F)
            s.g_s[p, l] = jnp.dot(left[rows, :], right, preferred_element_type=F32).astype(BF)
        return go(remote(s.g_s.at[p], s.g_r.at[p], s.gs.at[p], s.gr.at[p], sibling))

    def keep(p, left, right, copy, by_x):
        copy.wait()
        for l in range(2):
            rows = aligned((l * 2 + core) * F, F, F)
            g = jnp.dot(left[rows, :], right, preferred_element_type=F32) + s.g_r[p, l].astype(F32)
            g = g.astype(BF)
            for xo in range(4):
                for h in range(2):
                    piece = g[xo * 96 + h * 48 : xo * 96 + h * 48 + 48]
                    s.h1[p, xo * 4 + h * 2 + l if by_x else (h * 2 + l) * 4 + xo] = piece
        out = []
        for k in range(1, 4):
            to = lax.rem((x if by_x else z) + k, 4)
            device = at_x(k) if by_x else at_z(k)
            out.append(
                go(remote(s.h1.at[p, pl.ds(to * 4, 4)], s.s1.at[p, k - 1], s.s1s.at[p, k], s.s1r.at[p, k], device))
            )
        return out

    def second(p, copies, by_x):
        wait_all(copies)
        own = s.h1[p, pl.ds((x if by_x else z) * 4, 4)].astype(F32)
        for k in range(3):
            own = own + s.s1[p, k].astype(F32)
        s.h2[p] = own.astype(BF)
        out = []
        for k in range(1, 4):
            to = lax.rem((z if by_x else x) + k, 4)
            device = at_z(k) if by_x else at_x(k)
            out.append(go(remote(s.h2.at[p, to], s.s2.at[p, k - 1], s.s2s.at[p, k], s.s2r.at[p, k], device)))
        return out

    def last(p, copies, by_x):
        wait_all(copies)
        own = s.h2[p, z if by_x else x].astype(F32)
        for k in range(3):
            own = own + s.s2[p, k].astype(F32)
        pg_out[p] = own

    by_x = (False, False, True, True)
    g3 = away(3, s.bg_t, mixed)

    dkv_c = []
    for n, ks in enumerate(((1, 2), (3, 0))):
        for slot, k in enumerate(ks):
            dk, dv = back(0, k, slot)
            p_c[k].wait()
            i = around(k)
            s.dkv_s[i, 0:HD] = (dk.T + s.part_r[i, 0:HD].astype(F32)).astype(BF)
            s.dkv_s[i, HD:] = (dv.T + s.part_r[i, HD:].astype(F32)).astype(BF)
        for k in ks:
            dkv_c.append(swapped(k, s.dkv_s.at[around(k)], s.dkv_r.at[x], s.dkvs, s.dkvr))
        if n == 0:
            r3 = keep(3, s.bg_t, mixed, g3, by_x[3])
    for a in range(4):
        s.dq_s[a] = (s.dq[:, a * T : (a + 1) * T] * SCALE).astype(BF)
    dq_c = [swapped(k, s.dq_s.at[around(k)], s.dq_r.at[x], s.dqs, s.dqr) for k in (1, 2, 3, 0)]

    summed = lax.dot_general(mixed, s.w[3, aligned(hd * F, F, F), :], NT, preferred_element_type=F32)
    wait_all(op_c)
    for k in range(3):
        summed = summed + s.op_r[k].astype(F32)
    mine = aligned(hd * F, F, 128)
    s.res[...] = (s.frames[:, mine].astype(F32) + summed).astype(BF)
    halos = [
        go(remote(s.res.at[T - HALF : T], s.rhalo.at[0], s.rh_s.at[0], s.rh_r.at[0], at_tm(1))),
        go(remote(s.res.at[0:HALF], s.rhalo.at[1], s.rh_s.at[1], s.rh_r.at[1], at_tm(7))),
    ]

    wait_all(dkv_c)
    dk = s.dkv_r[:, 0:HD].reshape(F, T).T
    g1 = away(1, s.frames_t, dk)
    dv = s.dkv_r[:, HD:].reshape(F, T).T
    g2 = away(2, s.frames_t, dv)
    wait_all(dq_c)
    dq = s.dq_r[...].reshape(F, T).T
    g0 = away(0, s.frames_t, dq)
    r1 = keep(1, s.frames_t, dk, g1, by_x[1])
    r2 = keep(2, s.frames_t, dv, g2, by_x[2])
    r0 = keep(0, s.frames_t, dq, g0, by_x[0])
    t3 = second(3, r3, by_x[3])

    s.kacc[...] = jnp.zeros_like(s.kacc)
    s.rpad[HALF : HALF + T] = s.res[...].astype(F32)
    wait_all(halos)
    s.rpad[0:HALF] = jnp.where(tm > 0, s.rhalo[0].astype(F32), 0.0)
    s.rpad[HALF + T :] = jnp.where(tm < 7, s.rhalo[1].astype(F32), 0.0)

    def conv(it, carry):
        i, l = it // 3, lax.rem(it, 3)
        lanes = aligned(l * 128, 128, 128)
        whole = aligned(hd * F + l * 128, 128, 128)
        window = s.rpad[aligned(i * 64, 96, 64), lanes]
        up = s.cot[aligned(i * 64, 64, 64), whole].astype(F32)
        acc = window[HALF : HALF + 64]
        for j, rows in tap_terms(window, {j: j for j in range(KW)}):
            acc = acc + s.tapsf[j : j + 1, whole] * rows
            s.kacc[j, :, lanes] += jnp.sum((up * rows).reshape(8, 8, 128), axis=0)
        s.enc[aligned(i * 64, 64, 64), lanes] = acc.astype(BF)
        return carry

    lax.fori_loop(0, 18, conv, 0)
    e_c = [go(remote(s.enc, enc_out.at[0, :, mine], s.es.at[k], s.er.at[k], at_y(k))) for k in range(1, 4)]
    e_c.append(go(pltpu.make_async_copy(s.enc, enc_out.at[0, :, mine], s.in_sem.at[8])))
    for j in range(KW):
        s.kg[j] = jnp.sum(s.kacc[j], axis=0, keepdims=True)
    kg_c = []
    for k in range(1, 32):
        to = lax.rem(me + k, 32)
        kg_c.append(go(remote(s.kg.at[to], s.kgr.at[k], s.kgs.at[k], s.kgrs.at[k], at_plane(k))))

    t1 = second(1, r1, by_x[1])
    t2 = second(2, r2, by_x[2])
    t0 = second(0, r0, by_x[0])
    wait_all(kg_c)
    total = s.kg[me]
    for k in range(1, 32):
        total = total + s.kgr[k]
    s.kgy[hd] = total
    ky_c = [go(remote(s.kgy.at[hd], s.kgy.at[hd], s.kys.at[k], s.kyr.at[k], at_y(k))) for k in range(1, 4)]
    for p, t in ((3, t3), (1, t1), (2, t2), (0, t0)):
        last(p, t, by_x[p])
    wait_all(ky_c)
    for y in range(4):
        kg_out[:, y * F : (y + 1) * F] = s.kgy[y]
    wait_all(e_c)


def shards(frames, projections, kernel, pattern, cotangent):
    vmem = pl.BlockSpec(memory_space=pltpu.VMEM)
    anym = pl.BlockSpec(memory_space=pl.ANY)
    return pl.pallas_call(
        layer_kernel,
        out_shape=(
            jax.ShapeDtypeStruct((1, T, C), BF),
            jax.ShapeDtypeStruct((4, 48, F), F32),
            jax.ShapeDtypeStruct((1, C), F32),
        ),
        in_specs=[anym] * 5,
        out_specs=(anym, vmem, vmem),
        scratch_shapes=list(SCRATCH.values()),
        compiler_params=pltpu.CompilerParams(
            collective_id=0, has_side_effects=True, vmem_limit_bytes=60 << 20
        ),
        name="conformer_layer",
    )(frames, projections, kernel, pattern, cotangent)


def solution(mesh):
    placed = (
        P("dp", "tm", None),
        P(None, None, "head"),
        P(),
        P("dp", "tm", None),
        P("dp", "tm", None),
    )
    return jax.shard_map(
        shards,
        mesh=mesh,
        in_specs=placed,
        out_specs=(P("dp", "tm", None), P(None, ("dp", "tm"), "head"), P(("dp", "tm"), None)),
        check_vma=False,
    )
```

```python
import types

import jax
import jax.numpy as jnp
from jax import lax
from jax.experimental import pallas as pl
from jax.experimental.pallas import tpu as pltpu
from jax.sharding import PartitionSpec as P

HD = 96
BLK = 64
KW = 32
HALF = KW // 2
T = 384
C = 1536
F = 384
Q = 4 * T
QC = 768
CR = 192
MESH = pl.DeviceIdType.MESH
BF = jnp.bfloat16
F32 = jnp.float32
SCALE = HD**-0.5
NT = (((1,), (1,)), ((), ()))


def dma(*shape):
    return pltpu.SemaphoreType.DMA(shape)


def vm(dtype, *shape):
    return pltpu.VMEM(shape, dtype)


SCRATCH = dict(
    frames=vm(BF, T, C), cot=vm(BF, T, C), w=vm(BF, 4, C, F), taps=vm(BF, KW, C),
    in_sem=dma(9),
    upad=vm(F32, T + 2 * HALF, C), uhalo=vm(BF, 2, HALF, C), tapsf=vm(F32, KW, C),
    bg=vm(BF, T, C), bg_t=vm(BF, C, T), frames_t=vm(BF, C, T), uh_s=dma(2), uh_r=dma(2),
    q_s=vm(BF, 4, HD + 16, T), k_s=vm(BF, 4, HD, T), v_s=vm(BF, 4, HD, T), d_s=vm(BF, 4, HD, T),
    q_r=vm(BF, 4, HD + 16, T), d_r=vm(BF, 4, HD, T), k_r=vm(BF, 8, HD, T), v_r=vm(BF, 8, HD, T),
    qs=dma(4), qr=dma(4), ks=dma(4), kr=dma(4), vs=dma(4), vr=dma(4), ds=dma(4), dr=dma(4),
    fks=dma(4), fkr=dma(4), fvs=dma(4), fvr=dma(4),
    kn=vm(BF, 8, T, HD), vn=vm(BF, 8, T, HD), qt=vm(BF, HD, Q), qn=vm(BF, Q, HD), dt=vm(BF, HD, Q), dn=vm(BF, Q, HD),
    live=vm(F32, 64, Q), st=vm(F32, 8, T, QC), et=vm(BF, 8, T, Q), dsb=vm(BF, 2, T, Q), dq=vm(F32, HD, Q),
    inverse=vm(F32, 1, Q), delta=vm(F32, 1, Q),
    o_s=vm(BF, 4, HD, T), dq_s=vm(BF, 4, HD, T), part_s=vm(BF, 4, 2 * HD, T), part_r=vm(BF, 4, 2 * HD, T),
    dkv_s=vm(BF, 4, 2 * HD, T), mix_r=vm(BF, 4, HD, T), dq_r=vm(BF, 4, HD, T), dkv_r=vm(BF, 4, 2 * HD, T),
    os=dma(4), orr=dma(4), dqs=dma(4), dqr=dma(4), ps=dma(4), pr=dma(4), dkvs=dma(4), dkvr=dma(4),
    op_s=vm(BF, 3, T, F), op_r=vm(BF, 3, T, F), ops=dma(3), opr=dma(3),
    rpad=vm(F32, T + 2 * HALF, F), res=vm(BF, T, F), rhalo=vm(BF, 2, HALF, F), enc=vm(BF, T, F),
    rh_s=dma(2), rh_r=dma(2), es=dma(4), er=dma(4),
    kacc=vm(F32, KW, 8, F), kg=vm(F32, KW, 1, F), kgr=vm(F32, KW, 1, F), kgy=vm(F32, 4, 1, F),
    kgs=dma(32), kgrs=dma(32), kys=dma(4), kyr=dma(4),
    g_s=vm(BF, 4, 2, F, F), g_r=vm(BF, 4, 2, F, F), gs=dma(4), gr=dma(4),
    h1=vm(BF, 4, 16, 48, F), s1=vm(BF, 4, 3, 4, 48, F), h2=vm(BF, 4, 4, 48, F), s2=vm(BF, 4, 3, 48, F),
    s1s=dma(4, 4), s1r=dma(4, 4), s2s=dma(4, 4), s2r=dma(4, 4),
)


def remote(src, dst, ssem, rsem, device):
    return pltpu.make_async_remote_copy(
        src_ref=src, dst_ref=dst, send_sem=ssem, recv_sem=rsem, device_id=device, device_id_type=MESH
    )


class Either:
    def __init__(self, here, src, dst, ssem, rsem, device):
        self.here = here
        self.local = pltpu.make_async_copy(src, dst, rsem)
        self.far = remote(src, dst, ssem, rsem, device)

    def start(self):
        pl.when(self.here)(lambda: self.local.start())
        pl.when(jnp.logical_not(self.here))(lambda: self.far.start())

    def wait(self):
        pl.when(self.here)(lambda: self.local.wait())
        pl.when(jnp.logical_not(self.here))(lambda: self.far.wait())


def go(copy):
    copy.start()
    return copy


def wait_all(copies):
    for c in copies:
        c.wait()


def correlate(acc, load, taps, offsets, rows):
    for r in range(8):
        part = None
        for o in sorted(offsets):
            if o % 8 == r:
                term = taps(offsets[o]) * load(o - r, rows + 8 if r else rows)
                part = term if part is None else part + term
        acc = acc + (part[r : r + rows] if r else part)
    return acc


def aligned(start, size, by):
    return pl.ds(pl.multiple_of(start, by), size)


def layer_kernel(frames_h, w_h, taps_h, pattern_h, cot_h, enc_out, pg_out, kg_out, *scratch):
    s = types.SimpleNamespace(**dict(zip(SCRATCH, scratch)))
    dp, tm, hd = lax.axis_index("dp"), lax.axis_index("tm"), lax.axis_index("head")
    zl, core = dp // 2, lax.rem(dp, 2)
    x, zh = tm // 2, lax.rem(tm, 2)
    z = zh * 2 + zl
    me = dp * 8 + tm
    around = lambda k: lax.rem(x + k, 4)
    at_tm = lambda k: (dp, lax.rem(tm + k, 8), hd)
    at_x = lambda k: (dp, around(k) * 2 + zh, hd)
    at_y = lambda k: (dp, tm, lax.rem(hd + k, 4))
    sibling = (zl * 2 + 1 - core, tm, hd)

    def at_z(k):
        to = lax.rem(z + k, 4)
        return (lax.rem(to, 2) * 2 + core, x * 2 + to // 2, hd)

    def at_plane(k):
        to = lax.rem(me + k, 32)
        return (to // 8, lax.rem(to, 8), hd)

    def swapped(k, src, dst, ssem, rsem):
        device = (zl * 2 + zh, around(k) * 2 + core, hd)
        if k:
            return go(remote(src, dst, ssem.at[k], rsem.at[k], device))
        return go(Either(zh == core, src, dst, ssem.at[0], rsem.at[0], device))

    load = [
        go(pltpu.make_async_copy(a, b, s.in_sem.at[i]))
        for i, (a, b) in enumerate(
            [
                (frames_h.at[0], s.frames),
                (w_h.at[1], s.w.at[1]),
                (w_h.at[0], s.w.at[0]),
                (w_h.at[2], s.w.at[2]),
                (cot_h.at[0], s.cot),
                (taps_h, s.taps),
                (w_h.at[3], s.w.at[3]),
            ]
        )
    ]
    barrier = pltpu.get_barrier_semaphore()
    others = [at_plane(k) for k in range(1, 32)] + [at_y(k) for k in range(1, 4)]
    for device in others:
        pl.semaphore_signal(barrier, inc=1, device_id=device, device_id_type=MESH)

    def projected(rows, p):
        return jnp.dot(rows, s.w[p], preferred_element_type=F32).astype(BF).T

    load[0].wait()
    load[1].wait()
    y = projected(s.frames[...], 1)
    for h in range(4):
        s.k_s[h] = y[h * HD : (h + 1) * HD]
    pl.semaphore_wait(barrier, len(others))
    k_c = [swapped(k, s.k_s.at[around(k)], s.k_r.at[x], s.ks, s.kr) for k in (1, 2, 3, 0)]
    load[4].wait()
    halos = [
        go(remote(s.cot.at[T - HALF : T], s.uhalo.at[0], s.uh_s.at[0], s.uh_r.at[0], at_tm(1))),
        go(remote(s.cot.at[0:HALF], s.uhalo.at[1], s.uh_s.at[1], s.uh_r.at[1], at_tm(7))),
    ]
    load[2].wait()
    y = projected(s.frames[...], 0)
    blocks = pattern_h[0]
    block_of = lax.broadcasted_iota(jnp.int32, (6, T), 1) // BLK == lax.broadcasted_iota(jnp.int32, (6, T), 0)
    spread = lambda column: jnp.sum(jnp.where(block_of, column.astype(F32), 0.0), axis=0, keepdims=True)
    phase = spread(blocks[:, 0:1])
    count = spread(jnp.sum((blocks >= 0).astype(F32), axis=1, keepdims=True))
    row = lax.broadcasted_iota(jnp.int32, (16, T), 0)
    meta = jnp.where(row == 0, phase, jnp.where(row == 1, count, 0.0)).astype(BF)
    for h in range(4):
        s.q_s[h, 0:HD] = y[h * HD : (h + 1) * HD]
        s.q_s[h, HD:] = meta
    q_c = [swapped(k, s.q_s.at[around(k)], s.q_r.at[x], s.qs, s.qr) for k in (1, 2, 3, 0)]
    load[3].wait()
    y = projected(s.frames[...], 2)
    for h in range(4):
        s.v_s[h] = y[h * HD : (h + 1) * HD]
    v_c = [swapped(k, s.v_s.at[around(k)], s.v_r.at[x], s.vs, s.vr) for k in (1, 2, 3, 0)]

    load[5].wait()
    s.tapsf[...] = s.taps[...].astype(F32)
    s.upad[HALF : HALF + T] = s.cot[...].astype(F32)
    wait_all(halos)
    s.upad[0:HALF] = jnp.where(tm > 0, s.uhalo[0].astype(F32), 0.0)
    s.upad[HALF + T :] = jnp.where(tm < 7, s.uhalo[1].astype(F32), 0.0)

    def conv_back(it, carry):
        i, l = it // 12, lax.rem(it, 12)
        lanes = aligned(l * 128, 128, 128)
        base = i * CR
        acc = correlate(
            s.upad[aligned(base + HALF, CR, 16), lanes],
            lambda o, n: s.upad[aligned(base + o, n, 8), lanes],
            lambda j: s.tapsf[j : j + 1, lanes],
            {2 * HALF - j: j for j in range(KW)},
            CR,
        )
        s.bg[aligned(base, CR, CR), lanes] = acc.astype(BF)
        return carry

    lax.fori_loop(0, 12 * T // CR, conv_back, 0)
    load[6].wait()
    y = projected(s.bg[...], 3)
    for h in range(4):
        s.d_s[h] = y[h * HD : (h + 1) * HD]
    d_c = [swapped(k, s.d_s.at[around(k)], s.d_r.at[x], s.ds, s.dr) for k in (1, 2, 3, 0)]

    s.frames_t[...] = s.frames[...].T

    def forward(k, copy, buf, ssem, rsem):
        copy.wait()
        src = lax.rem(x + 4 - k, 4)
        return go(remote(buf.at[src], buf.at[4 + src], ssem.at[k], rsem.at[k], sibling))

    fk_c = [forward(k, c, s.k_r, s.fks, s.fkr) for k, c in zip((1, 2, 3, 0), k_c)]
    wait_all(q_c)
    for a in range(4):
        lanes = slice(a * T, (a + 1) * T)
        s.qt[:, lanes] = s.q_r[a, 0:HD]
        s.qn[lanes, :] = s.q_r[a, 0:HD].T
        got = s.q_r[a, HD:].astype(F32)
        row = lax.broadcasted_iota(jnp.int32, (64, T), 0)
        tile = row // 8
        owner = lax.rem(tile, 4) * 2 + jnp.where(tile < 4, core, 1 - core)
        key_block = owner * 6 + lax.rem(row, 8)
        query_block = (a * 2 + core) * 6 + lax.broadcasted_iota(jnp.int32, (64, T), 1) // BLK
        far = (lax.rem(key_block, 4).astype(F32) == got[0:1]) & ((key_block // 4).astype(F32) < got[1:2])
        near = jnp.abs(key_block - query_block) < 2
        s.live[:, lanes] = jnp.where(far | near, 1.0, 0.0)
    for t in range(4):
        s.kn[t] = s.k_r[t].T
    fv_c = [forward(k, c, s.v_r, s.fvs, s.fvr) for k, c in zip((1, 2, 3, 0), v_c)]
    wait_all(fk_c)
    for t in range(4, 8):
        s.kn[t] = s.k_r[t].T

    for c in range(Q // QC):
        lanes = slice(c * QC, (c + 1) * QC)
        q_t = s.qt[:, lanes]

        def scores(t, top):
            sc = jnp.dot(s.kn[t], q_t, preferred_element_type=F32)
            mask = s.live[aligned(t * 8, 8, 8), lanes]
            for b in range(6):
                part = jnp.where(mask[b : b + 1] > 0.5, sc[b * BLK : (b + 1) * BLK], -1e30)
                top = jnp.maximum(top, jnp.max(part.reshape(8, 8, QC), axis=0))
                s.st[t, b * BLK : (b + 1) * BLK] = part
            return top

        top = lax.fori_loop(0, 8, scores, jnp.full((8, QC), -jnp.inf, F32), unroll=8)
        c2 = SCALE * 1.4426950408889634
        top = jnp.max(top, axis=0, keepdims=True) * c2
        if c == 0:
            wait_all(fv_c)

        def weigh(t, carry):
            total, o = carry
            e = jnp.exp2(s.st[t] * c2 - top)
            total = total + jnp.sum(e.reshape(T // 8, 8, QC), axis=0)
            eb = e.astype(BF)
            s.et[t, :, lanes] = eb
            return total, o + jnp.dot(s.v_r[t], eb, preferred_element_type=F32)

        total, o = lax.fori_loop(
            0, 8, weigh, (jnp.zeros((8, QC), F32), jnp.zeros((HD, QC), F32)), unroll=8
        )
        inverse = 1.0 / jnp.sum(total, axis=0, keepdims=True)
        s.inverse[:, lanes] = inverse
        o = (o * inverse).astype(BF)
        for a in range(2):
            s.o_s[c * 2 + a] = o[:, a * T : (a + 1) * T]
    o_c = [swapped(k, s.o_s.at[around(k)], s.mix_r.at[x], s.os, s.orr) for k in (1, 2, 3, 0)]

    wait_all(d_c)
    for a in range(4):
        lanes = slice(a * T, (a + 1) * T)
        d = s.d_r[a].astype(F32)
        inverse = s.inverse[:, lanes]
        s.delta[:, lanes] = jnp.sum(d * s.o_s[a].astype(F32), axis=0, keepdims=True) * inverse
        d = (d * inverse).astype(BF)
        s.dt[:, lanes] = d
        s.dn[lanes, :] = d.T
    for t in range(8):
        s.vn[t] = s.v_r[t].T
    s.dq[...] = jnp.zeros_like(s.dq)

    def back(first, k, slot):
        t = first + around(k)
        for c in range(Q // QC):
            lanes = slice(c * QC, (c + 1) * QC)
            dp_ = jnp.dot(s.vn[t], s.dt[:, lanes], preferred_element_type=F32)
            s.dsb[slot, :, lanes] = (s.et[t, :, lanes].astype(F32) * (dp_ - s.delta[:, lanes])).astype(BF)
        dk = jnp.dot(s.dsb[slot], s.qn[...], preferred_element_type=F32) * SCALE
        dv = jnp.dot(s.et[t], s.dn[...], preferred_element_type=F32)
        s.dq[...] += jnp.dot(s.k_r[t], s.dsb[slot], preferred_element_type=F32)
        return dk, dv

    def back_pair(first, ks, out):
        for slot, k in enumerate(ks):
            dk, dv = back(first, k, slot)
            out[around(k), 0:HD] = dk.astype(BF).T
            out[around(k), HD:] = dv.astype(BF).T

    p_c = {}
    for ks in ((1, 2), (3, 0)):
        back_pair(4, ks, s.part_s)
        for k in ks:
            i = around(k)
            p_c[k] = go(remote(s.part_s.at[i], s.part_r.at[i], s.ps.at[k], s.pr.at[k], sibling))

    wait_all(o_c)
    mixed = s.mix_r[...].reshape(F, T).T
    op_c = []
    for k in range(1, 4):
        rows = aligned(lax.rem(hd + k, 4) * F, F, F)
        s.op_s[k - 1] = lax.dot_general(mixed, s.w[3, rows, :], NT, preferred_element_type=F32).astype(BF)
        op_c.append(go(remote(s.op_s.at[k - 1], s.op_r.at[k - 1], s.ops.at[k - 1], s.opr.at[k - 1], at_y(k))))

    def away(p, left, right):
        for l in range(2):
            rows = aligned((l * 2 + 1 - core) * F, F, F)
            s.g_s[p, l] = jnp.dot(left[rows, :], right, preferred_element_type=F32).astype(BF)
        return go(remote(s.g_s.at[p], s.g_r.at[p], s.gs.at[p], s.gr.at[p], sibling))

    def keep(p, left, right, copy, by_x):
        copy.wait()
        for l in range(2):
            rows = aligned((l * 2 + core) * F, F, F)
            g = jnp.dot(left[rows, :], right, preferred_element_type=F32) + s.g_r[p, l].astype(F32)
            g = g.astype(BF)
            for xo in range(4):
                for h in range(2):
                    piece = g[xo * 96 + h * 48 : xo * 96 + h * 48 + 48]
                    s.h1[p, xo * 4 + h * 2 + l if by_x else (h * 2 + l) * 4 + xo] = piece
        out = []
        for k in range(1, 4):
            to = lax.rem((x if by_x else z) + k, 4)
            device = at_x(k) if by_x else at_z(k)
            out.append(
                go(remote(s.h1.at[p, pl.ds(to * 4, 4)], s.s1.at[p, k - 1], s.s1s.at[p, k], s.s1r.at[p, k], device))
            )
        return out

    def second(p, copies, by_x):
        wait_all(copies)
        own = s.h1[p, pl.ds((x if by_x else z) * 4, 4)].astype(F32)
        for k in range(3):
            own = own + s.s1[p, k].astype(F32)
        s.h2[p] = own.astype(BF)
        out = []
        for k in range(1, 4):
            to = lax.rem((z if by_x else x) + k, 4)
            device = at_z(k) if by_x else at_x(k)
            out.append(go(remote(s.h2.at[p, to], s.s2.at[p, k - 1], s.s2s.at[p, k], s.s2r.at[p, k], device)))
        return out

    def last(p, copies, by_x):
        wait_all(copies)
        own = s.h2[p, z if by_x else x].astype(F32)
        for k in range(3):
            own = own + s.s2[p, k].astype(F32)
        pg_out[p] = own

    by_x = (False, False, True, True)
    dkv_c = []
    for ks in ((1, 2), (3, 0)):
        for slot, k in enumerate(ks):
            dk, dv = back(0, k, slot)
            p_c[k].wait()
            i = around(k)
            s.dkv_s[i, 0:HD] = (dk.T + s.part_r[i, 0:HD].astype(F32)).astype(BF)
            s.dkv_s[i, HD:] = (dv.T + s.part_r[i, HD:].astype(F32)).astype(BF)
        for k in ks:
            dkv_c.append(swapped(k, s.dkv_s.at[around(k)], s.dkv_r.at[x], s.dkvs, s.dkvr))
    for a in range(4):
        s.dq_s[a] = (s.dq[:, a * T : (a + 1) * T] * SCALE).astype(BF)
    dq_c = [swapped(k, s.dq_s.at[around(k)], s.dq_r.at[x], s.dqs, s.dqr) for k in (1, 2, 3, 0)]

    s.bg_t[...] = s.bg[...].T
    g3 = away(3, s.bg_t, mixed)

    summed = lax.dot_general(mixed, s.w[3, aligned(hd * F, F, F), :], NT, preferred_element_type=F32)
    wait_all(op_c)
    for k in range(3):
        summed = summed + s.op_r[k].astype(F32)
    mine = aligned(hd * F, F, 128)
    s.res[...] = (s.frames[:, mine].astype(F32) + summed).astype(BF)
    halos = [
        go(remote(s.res.at[T - HALF : T], s.rhalo.at[0], s.rh_s.at[0], s.rh_r.at[0], at_tm(1))),
        go(remote(s.res.at[0:HALF], s.rhalo.at[1], s.rh_s.at[1], s.rh_r.at[1], at_tm(7))),
    ]

    r3 = keep(3, s.bg_t, mixed, g3, by_x[3])
    wait_all(dkv_c)
    dk = s.dkv_r[:, 0:HD].reshape(F, T).T
    g1 = away(1, s.frames_t, dk)
    dv = s.dkv_r[:, HD:].reshape(F, T).T
    g2 = away(2, s.frames_t, dv)
    wait_all(dq_c)
    dq = s.dq_r[...].reshape(F, T).T
    g0 = away(0, s.frames_t, dq)
    r1 = keep(1, s.frames_t, dk, g1, by_x[1])
    r2 = keep(2, s.frames_t, dv, g2, by_x[2])
    r0 = keep(0, s.frames_t, dq, g0, by_x[0])

    s.kacc[...] = jnp.zeros_like(s.kacc)
    s.rpad[HALF : HALF + T] = s.res[...].astype(F32)
    wait_all(halos)
    s.rpad[0:HALF] = jnp.where(tm > 0, s.rhalo[0].astype(F32), 0.0)
    s.rpad[HALF + T :] = jnp.where(tm < 7, s.rhalo[1].astype(F32), 0.0)

    def conv(it, carry):
        i, l = it // 3, lax.rem(it, 3)
        lanes = aligned(l * 128, 128, 128)
        whole = aligned(hd * F + l * 128, 128, 128)
        base = i * CR
        window = lambda o, n: s.rpad[aligned(base + o, n, 8), lanes]
        acc = correlate(
            window(HALF, CR), window, lambda j: s.tapsf[j : j + 1, whole], {j: j for j in range(KW)}, CR
        )
        s.enc[aligned(base, CR, CR), lanes] = acc.astype(BF)
        up = s.cot[aligned(base, CR, CR), whole].astype(F32)
        edge = jnp.zeros((8, 128), F32)
        up = jnp.concatenate([edge, up, edge], axis=0)
        for r in range(8):
            moved = up[8 - r : CR + 16 - r] if r else up[8 : CR + 8]
            for a in range(KW // 8):
                term = moved * window(8 * a, CR + 8 if r else CR)
                s.kacc[8 * a + r, :, lanes] += jnp.sum(term.reshape(-1, 8, 128), axis=0)
        return carry

    lax.fori_loop(0, 3 * T // CR, conv, 0)
    e_c = [go(remote(s.enc, enc_out.at[0, :, mine], s.es.at[k], s.er.at[k], at_y(k))) for k in range(1, 4)]
    e_c.append(go(pltpu.make_async_copy(s.enc, enc_out.at[0, :, mine], s.in_sem.at[8])))
    for j in range(KW):
        s.kg[j] = jnp.sum(s.kacc[j], axis=0, keepdims=True)
    kg_c = []
    for k in range(1, 32):
        to = lax.rem(me + k, 32)
        kg_c.append(go(remote(s.kg.at[to], s.kgr.at[k], s.kgs.at[k], s.kgrs.at[k], at_plane(k))))

    t3 = second(3, r3, by_x[3])
    t2 = second(2, r2, by_x[2])
    t1 = second(1, r1, by_x[1])
    t0 = second(0, r0, by_x[0])
    wait_all(kg_c)
    total = s.kg[me]
    for k in range(1, 32):
        total = total + s.kgr[k]
    s.kgy[hd] = total
    ky_c = [go(remote(s.kgy.at[hd], s.kgy.at[hd], s.kys.at[k], s.kyr.at[k], at_y(k))) for k in range(1, 4)]
    for p, t in ((3, t3), (1, t1), (2, t2), (0, t0)):
        last(p, t, by_x[p])
    wait_all(ky_c)
    for y in range(4):
        kg_out[:, y * F : (y + 1) * F] = s.kgy[y]
    wait_all(e_c)


def shards(frames, projections, kernel, pattern, cotangent):
    vmem = pl.BlockSpec(memory_space=pltpu.VMEM)
    anym = pl.BlockSpec(memory_space=pl.ANY)
    return pl.pallas_call(
        layer_kernel,
        out_shape=(
            jax.ShapeDtypeStruct((1, T, C), BF),
            jax.ShapeDtypeStruct((4, 48, F), F32),
            jax.ShapeDtypeStruct((1, C), F32),
        ),
        in_specs=[anym, anym, anym, vmem, anym],
        out_specs=(vmem, vmem, vmem),
        scratch_shapes=list(SCRATCH.values()),
        compiler_params=pltpu.CompilerParams(
            collective_id=0, has_side_effects=True, vmem_limit_bytes=60 << 20
        ),
        name="conformer_layer",
    )(frames, projections, kernel, pattern, cotangent)


def solution(mesh):
    placed = (
        P("dp", "tm", None),
        P(None, None, "head"),
        P(),
        P("dp", "tm", None),
        P("dp", "tm", None),
    )
    return jax.shard_map(
        shards,
        mesh=mesh,
        in_specs=placed,
        out_specs=(P("dp", "tm", None), P(None, ("dp", "tm"), "head"), P(("dp", "tm"), None)),
        check_vma=False,
    )
```

```python
import types

import jax
import jax.numpy as jnp
from jax import lax
from jax.experimental import pallas as pl
from jax.experimental.pallas import tpu as pltpu
from jax.sharding import PartitionSpec as P

HD = 96
BLK = 64
KW = 32
HALF = KW // 2
T = 384
C = 1536
F = 384
Q = 4 * T
QC = 768
CR = 192
MESH = pl.DeviceIdType.MESH
BF = jnp.bfloat16
F32 = jnp.float32
SCALE = HD**-0.5
LOG2E = 1.4426950408889634
NT = (((1,), (1,)), ((), ()))


def dma(*shape):
    return pltpu.SemaphoreType.DMA(shape)


def vm(dtype, *shape):
    return pltpu.VMEM(shape, dtype)


SCRATCH = dict(
    frames=vm(BF, T, C), cot=vm(BF, T, C), w=vm(BF, 4, C, F), taps=vm(BF, KW, C),
    in_sem=dma(9),
    upad=vm(F32, T + 2 * HALF, C), uhalo=vm(BF, 2, HALF, C), tapsf=vm(F32, KW, C),
    bg=vm(BF, T, C), bg_t=vm(BF, C, T), frames_t=vm(BF, C, T), uh_s=dma(2), uh_r=dma(2),
    q_s=vm(BF, 4, HD + 16, T), k_s=vm(BF, 4, HD, T), v_s=vm(BF, 4, HD, T), d_s=vm(BF, 4, HD, T),
    q_r=vm(BF, 4, HD + 16, T), d_r=vm(BF, 4, HD, T), k_r=vm(BF, 8, HD, T), v_r=vm(BF, 8, HD, T),
    qs=dma(4), qr=dma(4), ks=dma(4), kr=dma(4), vs=dma(4), vr=dma(4), ds=dma(4), dr=dma(4),
    fks=dma(4), fkr=dma(4), fvs=dma(4), fvr=dma(4),
    kn=vm(BF, 8, T, HD), vn=vm(BF, 8, T, HD), qt=vm(BF, HD, Q), qn=vm(BF, Q, HD), dt=vm(BF, HD, Q), dn=vm(BF, Q, HD),
    live=vm(F32, 64, Q), st=vm(F32, 8, T, QC), et=vm(BF, 8, T, Q), dsb=vm(BF, 2, T, Q), dq=vm(F32, HD, Q),
    inverse=vm(F32, 1, Q), delta=vm(F32, 1, Q),
    o_s=vm(BF, 4, HD, T), dq_s=vm(BF, 4, HD, T), part_s=vm(BF, 4, 2 * HD, T), part_r=vm(BF, 4, 2 * HD, T),
    dkv_s=vm(BF, 4, 2 * HD, T), mix_r=vm(BF, 4, HD, T), dq_r=vm(BF, 4, HD, T), dkv_r=vm(BF, 4, 2 * HD, T),
    os=dma(4), orr=dma(4), dqs=dma(4), dqr=dma(4), ps=dma(4), pr=dma(4), dkvs=dma(4), dkvr=dma(4),
    op_s=vm(BF, 3, T, F), op_r=vm(BF, 3, T, F), ops=dma(3), opr=dma(3),
    rpad=vm(F32, T + 2 * HALF, F), res=vm(BF, T, F), rhalo=vm(BF, 2, HALF, F), enc=vm(BF, T, F),
    rh_s=dma(2), rh_r=dma(2), es=dma(4), er=dma(4),
    kacc=vm(F32, KW, 8, F), kg=vm(F32, KW, 1, F), kgr=vm(F32, KW, 1, F), kgy=vm(F32, 4, 1, F),
    kgs=dma(32), kgrs=dma(32), kys=dma(4), kyr=dma(4),
    g_s=vm(BF, 4, 2, F, F), g_r=vm(BF, 4, 2, F, F), gs=dma(4), gr=dma(4),
    s1s=dma(5, 4), s1r=dma(5, 4), s2s=dma(5, 4), s2r=dma(5, 4),
)


PARTS = ((3, 0, 48, True), (1, 0, 48, False), (2, 0, 48, True), (0, 0, 32, False), (0, 32, 16, True))
for i, (_, _, n, _) in enumerate(PARTS):
    SCRATCH[f"h1_{i}"] = vm(BF, 16, n, F)
    SCRATCH[f"s1_{i}"] = vm(BF, 3, 4, n, F)
    SCRATCH[f"h2_{i}"] = vm(BF, 4, n, F)
    SCRATCH[f"s2_{i}"] = vm(BF, 3, n, F)


def remote(src, dst, ssem, rsem, device):
    return pltpu.make_async_remote_copy(
        src_ref=src, dst_ref=dst, send_sem=ssem, recv_sem=rsem, device_id=device, device_id_type=MESH
    )


class Either:
    def __init__(self, here, src, dst, ssem, rsem, device):
        self.here = here
        self.local = pltpu.make_async_copy(src, dst, rsem)
        self.far = remote(src, dst, ssem, rsem, device)

    def start(self):
        pl.when(self.here)(lambda: self.local.start())
        pl.when(jnp.logical_not(self.here))(lambda: self.far.start())

    def wait(self):
        pl.when(self.here)(lambda: self.local.wait())
        pl.when(jnp.logical_not(self.here))(lambda: self.far.wait())


def go(copy):
    copy.start()
    return copy


def wait_all(copies):
    for c in copies:
        c.wait()


def correlate(acc, load, taps, offsets, rows):
    for r in range(8):
        part = None
        for o in sorted(offsets):
            if o % 8 == r:
                term = taps(offsets[o]) * load(o - r, rows + 8 if r else rows)
                part = term if part is None else part + term
        acc = acc + (part[r : r + rows] if r else part)
    return acc


def aligned(start, size, by):
    return pl.ds(pl.multiple_of(start, by), size)


def layer_kernel(frames_h, w_h, taps_h, pattern_h, cot_h, enc_out, pg_out, kg_out, *scratch):
    s = types.SimpleNamespace(**dict(zip(SCRATCH, scratch)))
    dp, tm, hd = lax.axis_index("dp"), lax.axis_index("tm"), lax.axis_index("head")
    zl, core = dp // 2, lax.rem(dp, 2)
    x, zh = tm // 2, lax.rem(tm, 2)
    z = zh * 2 + zl
    me = dp * 8 + tm
    around = lambda k: lax.rem(x + k, 4)
    at_tm = lambda k: (dp, lax.rem(tm + k, 8), hd)
    at_x = lambda k: (dp, around(k) * 2 + zh, hd)
    at_y = lambda k: (dp, tm, lax.rem(hd + k, 4))
    sibling = (zl * 2 + 1 - core, tm, hd)

    def at_z(k):
        to = lax.rem(z + k, 4)
        return (lax.rem(to, 2) * 2 + core, x * 2 + to // 2, hd)

    def at_plane(k):
        to = lax.rem(me + k, 32)
        return (to // 8, lax.rem(to, 8), hd)

    def swapped(k, src, dst, ssem, rsem):
        device = (zl * 2 + zh, around(k) * 2 + core, hd)
        if k:
            return go(remote(src, dst, ssem.at[k], rsem.at[k], device))
        return go(Either(zh == core, src, dst, ssem.at[0], rsem.at[0], device))

    load = [
        go(pltpu.make_async_copy(a, b, s.in_sem.at[i]))
        for i, (a, b) in enumerate(
            [
                (frames_h.at[0], s.frames),
                (w_h.at[1], s.w.at[1]),
                (w_h.at[0], s.w.at[0]),
                (w_h.at[2], s.w.at[2]),
                (cot_h.at[0], s.cot),
                (taps_h, s.taps),
                (w_h.at[3], s.w.at[3]),
            ]
        )
    ]
    barrier = pltpu.get_barrier_semaphore()
    others = [at_plane(k) for k in range(1, 32)] + [at_y(k) for k in range(1, 4)]
    for device in others:
        pl.semaphore_signal(barrier, inc=1, device_id=device, device_id_type=MESH)

    def projected(rows, p, factor=None):
        y = jnp.dot(rows, s.w[p], preferred_element_type=F32)
        return (y if factor is None else y * factor).astype(BF).T

    load[0].wait()
    load[1].wait()
    y = projected(s.frames[...], 1)
    for h in range(4):
        s.k_s[h] = y[h * HD : (h + 1) * HD]
    pl.semaphore_wait(barrier, len(others))
    k_c = [swapped(k, s.k_s.at[around(k)], s.k_r.at[x], s.ks, s.kr) for k in (1, 2, 3, 0)]
    load[4].wait()
    halos = [
        go(remote(s.cot.at[T - HALF : T], s.uhalo.at[0], s.uh_s.at[0], s.uh_r.at[0], at_tm(1))),
        go(remote(s.cot.at[0:HALF], s.uhalo.at[1], s.uh_s.at[1], s.uh_r.at[1], at_tm(7))),
    ]
    load[2].wait()
    y = projected(s.frames[...], 0, SCALE * LOG2E)
    row = lax.broadcasted_iota(jnp.int32, (16, T), 0)
    block = lax.broadcasted_iota(jnp.int32, (1, T), 1) // BLK
    phase = count = jnp.zeros((1, T), F32)
    for b in range(6):
        entries = pattern_h[b]
        phase = jnp.where(block == b, entries[:, 0:1].astype(F32), phase)
        count = jnp.where(block == b, jnp.sum((entries >= 0).astype(F32), axis=1, keepdims=True), count)
    meta = jnp.where(row == 0, phase, jnp.where(row == 1, count, 0.0)).astype(BF)
    for h in range(4):
        s.q_s[h, 0:HD] = y[h * HD : (h + 1) * HD]
        s.q_s[h, HD:] = meta
    q_c = [swapped(k, s.q_s.at[around(k)], s.q_r.at[x], s.qs, s.qr) for k in (1, 2, 3, 0)]
    load[3].wait()
    y = projected(s.frames[...], 2)
    for h in range(4):
        s.v_s[h] = y[h * HD : (h + 1) * HD]
    v_c = [swapped(k, s.v_s.at[around(k)], s.v_r.at[x], s.vs, s.vr) for k in (1, 2, 3, 0)]

    load[5].wait()
    s.tapsf[...] = s.taps[...].astype(F32)
    s.upad[HALF : HALF + T] = s.cot[...].astype(F32)
    wait_all(halos)
    s.upad[0:HALF] = jnp.where(tm > 0, s.uhalo[0].astype(F32), 0.0)
    s.upad[HALF + T :] = jnp.where(tm < 7, s.uhalo[1].astype(F32), 0.0)

    def conv_back(it, carry):
        i, l = it // 12, lax.rem(it, 12)
        lanes = aligned(l * 128, 128, 128)
        base = i * CR
        acc = correlate(
            s.upad[aligned(base + HALF, CR, 16), lanes],
            lambda o, n: s.upad[aligned(base + o, n, 8), lanes],
            lambda j: s.tapsf[j : j + 1, lanes],
            {2 * HALF - j: j for j in range(KW)},
            CR,
        )
        s.bg[aligned(base, CR, CR), lanes] = acc.astype(BF)
        return carry

    lax.fori_loop(0, 12 * T // CR, conv_back, 0)
    load[6].wait()
    y = projected(s.bg[...], 3)
    for h in range(4):
        s.d_s[h] = y[h * HD : (h + 1) * HD]
    d_c = [swapped(k, s.d_s.at[around(k)], s.d_r.at[x], s.ds, s.dr) for k in (1, 2, 3, 0)]

    s.frames_t[...] = s.frames[...].T
    s.bg_t[...] = s.bg[...].T

    def forward(k, copy, buf, ssem, rsem):
        copy.wait()
        src = lax.rem(x + 4 - k, 4)
        return go(remote(buf.at[src], buf.at[4 + src], ssem.at[k], rsem.at[k], sibling))

    fk_c = [forward(k, c, s.k_r, s.fks, s.fkr) for k, c in zip((1, 2, 3, 0), k_c)]
    wait_all(q_c)
    for a in range(4):
        lanes = slice(a * T, (a + 1) * T)
        s.qt[:, lanes] = s.q_r[a, 0:HD]
        s.qn[lanes, :] = s.q_r[a, 0:HD].T
        got = s.q_r[a, HD:].astype(F32)
        row = lax.broadcasted_iota(jnp.int32, (64, T), 0)
        tile = row // 8
        owner = lax.rem(tile, 4) * 2 + jnp.where(tile < 4, core, 1 - core)
        key_block = owner * 6 + lax.rem(row, 8)
        query_block = (a * 2 + core) * 6 + lax.broadcasted_iota(jnp.int32, (64, T), 1) // BLK
        far = (lax.rem(key_block, 4).astype(F32) == got[0:1]) & ((key_block // 4).astype(F32) < got[1:2])
        near = jnp.abs(key_block - query_block) < 2
        s.live[:, lanes] = jnp.where(far | near, 1.0, 0.0)
    for t in range(4):
        s.kn[t] = s.k_r[t].T
    fv_c = [forward(k, c, s.v_r, s.fvs, s.fvr) for k, c in zip((1, 2, 3, 0), v_c)]
    wait_all(fk_c)
    for t in range(4, 8):
        s.kn[t] = s.k_r[t].T

    for c in range(Q // QC):
        lanes = slice(c * QC, (c + 1) * QC)
        q_t = s.qt[:, lanes]

        def scores(t, top):
            sc = jnp.dot(s.kn[t], q_t, preferred_element_type=F32)
            mask = s.live[aligned(t * 8, 8, 8), lanes]
            for b in range(6):
                part = jnp.where(mask[b : b + 1] > 0.5, sc[b * BLK : (b + 1) * BLK], -1e30)
                top = jnp.maximum(top, jnp.max(part.reshape(8, 8, QC), axis=0))
                s.st[t, b * BLK : (b + 1) * BLK] = part
            return top

        top = lax.fori_loop(0, 8, scores, jnp.full((8, QC), -jnp.inf, F32), unroll=8)
        top = jnp.max(top, axis=0, keepdims=True)
        if c == 0:
            wait_all(fv_c)

        def weigh(t, o):
            eb = jnp.exp2(s.st[t] - top).astype(BF)
            s.et[t, :, lanes] = eb
            values = jnp.concatenate([s.v_r[t], jnp.ones((16, T), BF)], axis=0)
            return o + jnp.dot(values, eb, preferred_element_type=F32)

        o = lax.fori_loop(0, 8, weigh, jnp.zeros((HD + 16, QC), F32), unroll=8)
        inverse = 1.0 / o[HD : HD + 1]
        o = o[0:HD]
        s.inverse[:, lanes] = inverse
        o = (o * inverse).astype(BF)
        for a in range(2):
            s.o_s[c * 2 + a] = o[:, a * T : (a + 1) * T]
    o_c = [swapped(k, s.o_s.at[around(k)], s.mix_r.at[x], s.os, s.orr) for k in (1, 2, 3, 0)]

    wait_all(d_c)
    for a in range(4):
        lanes = slice(a * T, (a + 1) * T)
        d = s.d_r[a].astype(F32)
        inverse = s.inverse[:, lanes]
        s.delta[:, lanes] = jnp.sum(d * s.o_s[a].astype(F32), axis=0, keepdims=True) * inverse
        d = (d * inverse).astype(BF)
        s.dt[:, lanes] = d
        s.dn[lanes, :] = d.T
    for t in range(8):
        s.vn[t] = s.v_r[t].T
    s.dq[...] = jnp.zeros_like(s.dq)

    def back(first, k, slot):
        t = first + around(k)
        for c in range(Q // QC):
            lanes = slice(c * QC, (c + 1) * QC)
            dp_ = jnp.dot(s.vn[t], s.dt[:, lanes], preferred_element_type=F32)
            s.dsb[slot, :, lanes] = (s.et[t, :, lanes].astype(F32) * (dp_ - s.delta[:, lanes])).astype(BF)
        dk = jnp.dot(s.dsb[slot], s.qn[...], preferred_element_type=F32) * (1 / LOG2E)
        dv = jnp.dot(s.et[t], s.dn[...], preferred_element_type=F32)
        s.dq[...] += jnp.dot(s.k_r[t], s.dsb[slot], preferred_element_type=F32)
        return dk, dv

    def back_pair(first, ks, out):
        for slot, k in enumerate(ks):
            dk, dv = back(first, k, slot)
            out[around(k), 0:HD] = dk.astype(BF).T
            out[around(k), HD:] = dv.astype(BF).T

    p_c = {}
    for ks in ((1, 2), (3, 0)):
        back_pair(4, ks, s.part_s)
        for k in ks:
            i = around(k)
            p_c[k] = go(remote(s.part_s.at[i], s.part_r.at[i], s.ps.at[k], s.pr.at[k], sibling))

    wait_all(o_c)
    mixed = s.mix_r[...].reshape(F, T).T
    op_c = []
    for k in range(1, 4):
        rows = aligned(lax.rem(hd + k, 4) * F, F, F)
        s.op_s[k - 1] = lax.dot_general(mixed, s.w[3, rows, :], NT, preferred_element_type=F32).astype(BF)
        op_c.append(go(remote(s.op_s.at[k - 1], s.op_r.at[k - 1], s.ops.at[k - 1], s.opr.at[k - 1], at_y(k))))

    def away(p, left, right):
        for l in range(2):
            rows = aligned((l * 2 + 1 - core) * F, F, F)
            s.g_s[p, l] = jnp.dot(left[rows, :], right, preferred_element_type=F32).astype(BF)
        return go(remote(s.g_s.at[p], s.g_r.at[p], s.gs.at[p], s.gr.at[p], sibling))

    first_c, second_c = {}, {}

    def keep(p, left, right, copy):
        copy.wait()
        parts = [(i, r0, n, by_x) for i, (q, r0, n, by_x) in enumerate(PARTS) if q == p]
        for l in range(2):
            rows = aligned((l * 2 + core) * F, F, F)
            g = jnp.dot(left[rows, :], right, preferred_element_type=F32) + s.g_r[p, l].astype(F32)
            g = g.astype(BF)
            for xo in range(4):
                for h in range(2):
                    for i, r0, n, by_x in parts:
                        start = xo * 96 + h * 48 + r0
                        slot = xo * 4 + h * 2 + l if by_x else (h * 2 + l) * 4 + xo
                        getattr(s, f"h1_{i}")[slot] = g[start : start + n]
        for i, r0, n, by_x in parts:
            h1, s1 = getattr(s, f"h1_{i}"), getattr(s, f"s1_{i}")
            first_c[i] = []
            for k in range(1, 4):
                to = lax.rem((x if by_x else z) + k, 4)
                device = at_x(k) if by_x else at_z(k)
                c = remote(h1.at[pl.ds(to * 4, 4)], s1.at[k - 1], s.s1s.at[i, k], s.s1r.at[i, k], device)
                first_c[i].append(go(c))

    def second(i):
        by_x = PARTS[i][3]
        h1, s1 = getattr(s, f"h1_{i}"), getattr(s, f"s1_{i}")
        h2, s2 = getattr(s, f"h2_{i}"), getattr(s, f"s2_{i}")
        wait_all(first_c[i])
        own = h1[pl.ds((x if by_x else z) * 4, 4)].astype(F32)
        for k in range(3):
            own = own + s1[k].astype(F32)
        h2[...] = own.astype(BF)
        second_c[i] = []
        for k in range(1, 4):
            to = lax.rem((z if by_x else x) + k, 4)
            device = at_z(k) if by_x else at_x(k)
            c = remote(h2.at[to], s2.at[k - 1], s.s2s.at[i, k], s.s2r.at[i, k], device)
            second_c[i].append(go(c))

    def last(i):
        p, r0, n, by_x = PARTS[i]
        h2, s2 = getattr(s, f"h2_{i}"), getattr(s, f"s2_{i}")
        wait_all(second_c[i])
        own = h2[z if by_x else x].astype(F32)
        for k in range(3):
            own = own + s2[k].astype(F32)
        pg_out[p, r0 : r0 + n] = own

    g3 = away(3, s.bg_t, mixed)

    dkv_c = []
    for ks in ((1, 2), (3, 0)):
        for slot, k in enumerate(ks):
            dk, dv = back(0, k, slot)
            p_c[k].wait()
            i = around(k)
            s.dkv_s[i, 0:HD] = (dk.T + s.part_r[i, 0:HD].astype(F32)).astype(BF)
            s.dkv_s[i, HD:] = (dv.T + s.part_r[i, HD:].astype(F32)).astype(BF)
        for k in ks:
            dkv_c.append(swapped(k, s.dkv_s.at[around(k)], s.dkv_r.at[x], s.dkvs, s.dkvr))
        if ks[0] == 1:
            keep(3, s.bg_t, mixed, g3)
    for a in range(4):
        s.dq_s[a] = (s.dq[:, a * T : (a + 1) * T] * SCALE).astype(BF)
    dq_c = [swapped(k, s.dq_s.at[around(k)], s.dq_r.at[x], s.dqs, s.dqr) for k in (1, 2, 3, 0)]

    summed = lax.dot_general(mixed, s.w[3, aligned(hd * F, F, F), :], NT, preferred_element_type=F32)
    wait_all(op_c)
    for k in range(3):
        summed = summed + s.op_r[k].astype(F32)
    mine = aligned(hd * F, F, 128)
    s.res[...] = (s.frames[:, mine].astype(F32) + summed).astype(BF)
    halos = [
        go(remote(s.res.at[T - HALF : T], s.rhalo.at[0], s.rh_s.at[0], s.rh_r.at[0], at_tm(1))),
        go(remote(s.res.at[0:HALF], s.rhalo.at[1], s.rh_s.at[1], s.rh_r.at[1], at_tm(7))),
    ]

    wait_all(dkv_c)
    dk = s.dkv_r[:, 0:HD].reshape(F, T).T
    g1 = away(1, s.frames_t, dk)
    dv = s.dkv_r[:, HD:].reshape(F, T).T
    g2 = away(2, s.frames_t, dv)
    wait_all(dq_c)
    dq = s.dq_r[...].reshape(F, T).T
    g0 = away(0, s.frames_t, dq)
    keep(1, s.frames_t, dk, g1)
    keep(2, s.frames_t, dv, g2)
    keep(0, s.frames_t, dq, g0)

    s.kacc[...] = jnp.zeros_like(s.kacc)
    s.rpad[HALF : HALF + T] = s.res[...].astype(F32)
    wait_all(halos)
    s.rpad[0:HALF] = jnp.where(tm > 0, s.rhalo[0].astype(F32), 0.0)
    s.rpad[HALF + T :] = jnp.where(tm < 7, s.rhalo[1].astype(F32), 0.0)

    def conv(it, carry):
        i, l = it // 3, lax.rem(it, 3)
        lanes = aligned(l * 128, 128, 128)
        whole = aligned(hd * F + l * 128, 128, 128)
        base = i * CR
        window = lambda o, n: s.rpad[aligned(base + o, n, 8), lanes]
        acc = correlate(
            window(HALF, CR), window, lambda j: s.tapsf[j : j + 1, whole], {j: j for j in range(KW)}, CR
        )
        s.enc[aligned(base, CR, CR), lanes] = acc.astype(BF)
        up = s.cot[aligned(base, CR, CR), whole].astype(F32)
        edge = jnp.zeros((8, 128), F32)
        up = jnp.concatenate([edge, up, edge], axis=0)
        for r in range(8):
            moved = up[8 - r : CR + 16 - r] if r else up[8 : CR + 8]
            for a in range(KW // 8):
                term = moved * window(8 * a, CR + 8 if r else CR)
                s.kacc[8 * a + r, :, lanes] += jnp.sum(term.reshape(-1, 8, 128), axis=0)
        return carry

    lax.fori_loop(0, 3 * T // CR, conv, 0)
    e_c = [go(remote(s.enc, enc_out.at[:, mine], s.es.at[k], s.er.at[k], at_y(k))) for k in range(1, 4)]
    e_c.append(go(pltpu.make_async_copy(s.enc, enc_out.at[:, mine], s.in_sem.at[8])))
    for j in range(KW):
        s.kg[j] = jnp.sum(s.kacc[j], axis=0, keepdims=True)
    kg_c = []
    for k in range(1, 32):
        to = lax.rem(me + k, 32)
        kg_c.append(go(remote(s.kg.at[to], s.kgr.at[k], s.kgs.at[k], s.kgrs.at[k], at_plane(k))))

    for i in (0, 2, 1, 4, 3):
        second(i)
    wait_all(kg_c)
    total = s.kg[me]
    for k in range(1, 32):
        total = total + s.kgr[k]
    s.kgy[hd] = total
    ky_c = [go(remote(s.kgy.at[hd], s.kgy.at[hd], s.kys.at[k], s.kyr.at[k], at_y(k))) for k in range(1, 4)]
    for i in (0, 2, 1, 4, 3):
        last(i)
    wait_all(ky_c)
    for y in range(4):
        kg_out[:, y * F : (y + 1) * F] = s.kgy[y]
    wait_all(e_c)


def shards(frames, projections, kernel, pattern, cotangent):
    vmem = pl.BlockSpec(memory_space=pltpu.VMEM)
    anym = pl.BlockSpec(memory_space=pl.ANY)
    enc, pg, kg = pl.pallas_call(
        layer_kernel,
        out_shape=(
            jax.ShapeDtypeStruct((T, C), BF),
            jax.ShapeDtypeStruct((4, 48, F), F32),
            jax.ShapeDtypeStruct((1, C), F32),
        ),
        in_specs=[anym, anym, anym, vmem, anym],
        out_specs=(vmem, vmem, vmem),
        scratch_shapes=list(SCRATCH.values()),
        compiler_params=pltpu.CompilerParams(
            collective_id=0, has_side_effects=True, vmem_limit_bytes=60 << 20
        ),
        name="conformer_layer",
    )(frames, projections, kernel, jnp.transpose(pattern, (1, 0, 2)), cotangent)
    return enc[None], pg, kg


def solution(mesh):
    placed = (
        P("dp", "tm", None),
        P(None, None, "head"),
        P(),
        P("dp", "tm", None),
        P("dp", "tm", None),
    )
    return jax.shard_map(
        shards,
        mesh=mesh,
        in_specs=placed,
        out_specs=(P("dp", "tm", None), P(None, ("dp", "tm"), "head"), P(("dp", "tm"), None)),
        check_vma=False,
    )
```

```python
import types

import jax
import jax.numpy as jnp
from jax import lax
from jax.experimental import pallas as pl
from jax.experimental.pallas import tpu as pltpu
from jax.sharding import PartitionSpec as P

HD = 96
BLK = 64
KW = 32
HALF = KW // 2
T = 384
C = 1536
F = 384
Q = 4 * T
QC = 768
CR = 192
MESH = pl.DeviceIdType.MESH
BF = jnp.bfloat16
F32 = jnp.float32
SCALE = HD**-0.5
LOG2E = 1.4426950408889634
NT = (((1,), (1,)), ((), ()))


def dma(*shape):
    return pltpu.SemaphoreType.DMA(shape)


def vm(dtype, *shape):
    return pltpu.VMEM(shape, dtype)


SCRATCH = dict(
    frames=vm(BF, T, C), cot=vm(BF, T, C), w=vm(BF, 4, C, F), taps=vm(BF, KW, C),
    in_sem=dma(9),
    upad=vm(F32, T + 2 * HALF, C), uhalo=vm(BF, 2, HALF, C), tapsf=vm(F32, KW, C),
    bg=vm(BF, T, C), uh_s=dma(2), uh_r=dma(2),
    q_s=vm(BF, 4, HD + 16, T), k_s=vm(BF, 4, HD, T), v_s=vm(BF, 4, HD, T), d_s=vm(BF, 4, HD, T),
    q_r=vm(BF, 4, HD + 16, T), d_r=vm(BF, 4, HD, T), k_r=vm(BF, 8, HD, T), v_r=vm(BF, 8, HD, T),
    qs=dma(4), qr=dma(4), ks=dma(4), kr=dma(4), vs=dma(4), vr=dma(4), ds=dma(4), dr=dma(4),
    fks=dma(4), fkr=dma(4), fvs=dma(4), fvr=dma(4),
    kn=vm(BF, 8, T, HD), vn=vm(BF, 8, T, HD), qt=vm(BF, HD, Q), qn=vm(BF, Q, HD), dt=vm(BF, HD, Q), dn=vm(BF, Q, HD),
    live=vm(F32, 64, Q), st=vm(F32, 8, T, QC), et=vm(BF, 8, T, Q), dsb=vm(BF, 2, T, Q), dq=vm(F32, HD, Q),
    inverse=vm(F32, 1, Q), delta=vm(F32, 1, Q),
    o_s=vm(BF, 4, HD, T), dq_s=vm(BF, 4, HD, T), part_s=vm(BF, 4, 2 * HD, T), part_r=vm(BF, 4, 2 * HD, T),
    dkv_s=vm(BF, 4, 2 * HD, T), mix_r=vm(BF, 4, HD, T), dq_r=vm(BF, 4, HD, T), dkv_r=vm(BF, 4, 2 * HD, T),
    os=dma(4), orr=dma(4), dqs=dma(4), dqr=dma(4), ps=dma(4), pr=dma(4), dkvs=dma(4), dkvr=dma(4),
    op_s=vm(BF, 3, T, F), op_r=vm(BF, 3, T, F), ops=dma(3), opr=dma(3),
    rpad=vm(F32, T + 2 * HALF, F), res=vm(BF, T, F), rhalo=vm(BF, 2, HALF, F), enc=vm(BF, T, F),
    rh_s=dma(2), rh_r=dma(2), es=dma(4), er=dma(4),
    kacc=vm(F32, KW, 8, F), kg=vm(F32, KW, 1, F), kgr=vm(F32, KW, 1, F), kgy=vm(F32, 4, 1, F),
    kgs=dma(32), kgrs=dma(32), kys=dma(4), kyr=dma(4),
    g_s=vm(BF, 4, 2, F, F), g_r=vm(BF, 4, 2, F, F), gs=dma(4), gr=dma(4),
    s1s=dma(5, 4), s1r=dma(5, 4), s2s=dma(5, 4), s2r=dma(5, 4),
)


PARTS = ((3, 0, 48, True), (1, 0, 48, False), (2, 0, 48, True), (0, 0, 32, False), (0, 32, 16, True))
for i, (_, _, n, _) in enumerate(PARTS):
    SCRATCH[f"h1_{i}"] = vm(BF, 16, n, F)
    SCRATCH[f"s1_{i}"] = vm(BF, 3, 4, n, F)
    SCRATCH[f"h2_{i}"] = vm(BF, 4, n, F)
    SCRATCH[f"s2_{i}"] = vm(BF, 3, n, F)


def remote(src, dst, ssem, rsem, device):
    return pltpu.make_async_remote_copy(
        src_ref=src, dst_ref=dst, send_sem=ssem, recv_sem=rsem, device_id=device, device_id_type=MESH
    )


class Either:
    def __init__(self, here, src, dst, ssem, rsem, device):
        self.here = here
        self.local = pltpu.make_async_copy(src, dst, rsem)
        self.far = remote(src, dst, ssem, rsem, device)

    def start(self):
        pl.when(self.here)(lambda: self.local.start())
        pl.when(jnp.logical_not(self.here))(lambda: self.far.start())

    def wait(self):
        pl.when(self.here)(lambda: self.local.wait())
        pl.when(jnp.logical_not(self.here))(lambda: self.far.wait())


def go(copy):
    copy.start()
    return copy


def wait_all(copies):
    for c in copies:
        c.wait()


def correlate(acc, load, taps, offsets, rows):
    for r in range(8):
        part = None
        for o in sorted(offsets):
            if o % 8 == r:
                term = taps(offsets[o]) * load(o - r, rows + 8 if r else rows)
                part = term if part is None else part + term
        acc = acc + (part[r : r + rows] if r else part)
    return acc


def aligned(start, size, by):
    return pl.ds(pl.multiple_of(start, by), size)


def layer_kernel(frames_h, w_h, taps_h, pattern_h, cot_h, enc_out, pg_out, kg_out, *scratch):
    s = types.SimpleNamespace(**dict(zip(SCRATCH, scratch)))
    dp, tm, hd = lax.axis_index("dp"), lax.axis_index("tm"), lax.axis_index("head")
    zl, core = dp // 2, lax.rem(dp, 2)
    x, zh = tm // 2, lax.rem(tm, 2)
    z = zh * 2 + zl
    me = dp * 8 + tm
    around = lambda k: lax.rem(x + k, 4)
    at_tm = lambda k: (dp, lax.rem(tm + k, 8), hd)
    at_x = lambda k: (dp, around(k) * 2 + zh, hd)
    at_y = lambda k: (dp, tm, lax.rem(hd + k, 4))
    sibling = (zl * 2 + 1 - core, tm, hd)

    def at_z(k):
        to = lax.rem(z + k, 4)
        return (lax.rem(to, 2) * 2 + core, x * 2 + to // 2, hd)

    def at_plane(k):
        to = lax.rem(me + k, 32)
        return (to // 8, lax.rem(to, 8), hd)

    def swapped(k, src, dst, ssem, rsem):
        device = (zl * 2 + zh, around(k) * 2 + core, hd)
        if k:
            return go(remote(src, dst, ssem.at[k], rsem.at[k], device))
        return go(Either(zh == core, src, dst, ssem.at[0], rsem.at[0], device))

    load = [
        go(pltpu.make_async_copy(a, b, s.in_sem.at[i]))
        for i, (a, b) in enumerate(
            [
                (frames_h.at[0], s.frames),
                (w_h.at[1], s.w.at[1]),
                (w_h.at[0], s.w.at[0]),
                (w_h.at[2], s.w.at[2]),
                (cot_h.at[0], s.cot),
                (taps_h, s.taps),
                (w_h.at[3], s.w.at[3]),
            ]
        )
    ]
    barrier = pltpu.get_barrier_semaphore()
    others = [at_plane(k) for k in range(1, 32)] + [at_y(k) for k in range(1, 4)]
    for device in others:
        pl.semaphore_signal(barrier, inc=1, device_id=device, device_id_type=MESH)

    def projected(rows, p, factor=None):
        y = jnp.dot(rows, s.w[p], preferred_element_type=F32)
        return (y if factor is None else y * factor).astype(BF).T

    load[0].wait()
    load[1].wait()
    y = projected(s.frames[...], 1)
    for h in range(4):
        s.k_s[h] = y[h * HD : (h + 1) * HD]
    pl.semaphore_wait(barrier, len(others))
    k_c = [swapped(k, s.k_s.at[around(k)], s.k_r.at[x], s.ks, s.kr) for k in (1, 2, 3, 0)]
    load[4].wait()
    halos = [
        go(remote(s.cot.at[T - HALF : T], s.uhalo.at[0], s.uh_s.at[0], s.uh_r.at[0], at_tm(1))),
        go(remote(s.cot.at[0:HALF], s.uhalo.at[1], s.uh_s.at[1], s.uh_r.at[1], at_tm(7))),
    ]
    load[2].wait()
    y = projected(s.frames[...], 0, SCALE * LOG2E)
    row = lax.broadcasted_iota(jnp.int32, (16, T), 0)
    block = lax.broadcasted_iota(jnp.int32, (1, T), 1) // BLK
    phase = count = jnp.zeros((1, T), F32)
    for b in range(6):
        entries = pattern_h[b]
        phase = jnp.where(block == b, entries[:, 0:1].astype(F32), phase)
        count = jnp.where(block == b, jnp.sum((entries >= 0).astype(F32), axis=1, keepdims=True), count)
    meta = jnp.where(row == 0, phase, jnp.where(row == 1, count, 0.0)).astype(BF)
    for h in range(4):
        s.q_s[h, 0:HD] = y[h * HD : (h + 1) * HD]
        s.q_s[h, HD:] = meta
    q_c = [swapped(k, s.q_s.at[around(k)], s.q_r.at[x], s.qs, s.qr) for k in (1, 2, 3, 0)]
    load[3].wait()
    y = projected(s.frames[...], 2)
    for h in range(4):
        s.v_s[h] = y[h * HD : (h + 1) * HD]
    v_c = [swapped(k, s.v_s.at[around(k)], s.v_r.at[x], s.vs, s.vr) for k in (1, 2, 3, 0)]

    load[5].wait()
    s.tapsf[...] = s.taps[...].astype(F32)
    s.upad[HALF : HALF + T] = s.cot[...].astype(F32)
    wait_all(halos)
    s.upad[0:HALF] = jnp.where(tm > 0, s.uhalo[0].astype(F32), 0.0)
    s.upad[HALF + T :] = jnp.where(tm < 7, s.uhalo[1].astype(F32), 0.0)

    def conv_back(it, carry):
        i, l = it // 12, lax.rem(it, 12)
        lanes = aligned(l * 128, 128, 128)
        base = i * CR
        acc = correlate(
            s.upad[aligned(base + HALF, CR, 16), lanes],
            lambda o, n: s.upad[aligned(base + o, n, 8), lanes],
            lambda j: s.tapsf[j : j + 1, lanes],
            {2 * HALF - j: j for j in range(KW)},
            CR,
        )
        s.bg[aligned(base, CR, CR), lanes] = acc.astype(BF)
        return carry

    lax.fori_loop(0, 12 * T // CR, conv_back, 0)
    load[6].wait()
    y = projected(s.bg[...], 3)
    for h in range(4):
        s.d_s[h] = y[h * HD : (h + 1) * HD]
    d_c = [swapped(k, s.d_s.at[around(k)], s.d_r.at[x], s.ds, s.dr) for k in (1, 2, 3, 0)]

    def forward(k, copy, buf, ssem, rsem):
        copy.wait()
        src = lax.rem(x + 4 - k, 4)
        return go(remote(buf.at[src], buf.at[4 + src], ssem.at[k], rsem.at[k], sibling))

    fk_c = [forward(k, c, s.k_r, s.fks, s.fkr) for k, c in zip((1, 2, 3, 0), k_c)]
    wait_all(q_c)
    for a in range(4):
        lanes = slice(a * T, (a + 1) * T)
        s.qt[:, lanes] = s.q_r[a, 0:HD]
        s.qn[lanes, :] = s.q_r[a, 0:HD].T
        got = s.q_r[a, HD:].astype(F32)
        row = lax.broadcasted_iota(jnp.int32, (64, T), 0)
        tile = row // 8
        owner = lax.rem(tile, 4) * 2 + jnp.where(tile < 4, core, 1 - core)
        key_block = owner * 6 + lax.rem(row, 8)
        query_block = (a * 2 + core) * 6 + lax.broadcasted_iota(jnp.int32, (64, T), 1) // BLK
        far = (lax.rem(key_block, 4).astype(F32) == got[0:1]) & ((key_block // 4).astype(F32) < got[1:2])
        near = jnp.abs(key_block - query_block) < 2
        s.live[:, lanes] = jnp.where(far | near, 1.0, 0.0)
    for t in range(4):
        s.kn[t] = s.k_r[t].T
    fv_c = [forward(k, c, s.v_r, s.fvs, s.fvr) for k, c in zip((1, 2, 3, 0), v_c)]
    wait_all(fk_c)
    for t in range(4, 8):
        s.kn[t] = s.k_r[t].T

    for c in range(Q // QC):
        lanes = slice(c * QC, (c + 1) * QC)
        q_t = s.qt[:, lanes]

        def scores(t, top):
            sc = jnp.dot(s.kn[t], q_t, preferred_element_type=F32)
            mask = s.live[aligned(t * 8, 8, 8), lanes]
            for b in range(6):
                part = jnp.where(mask[b : b + 1] > 0.5, sc[b * BLK : (b + 1) * BLK], -1e30)
                top = jnp.maximum(top, jnp.max(part.reshape(8, 8, QC), axis=0))
                s.st[t, b * BLK : (b + 1) * BLK] = part
            return top

        top = lax.fori_loop(0, 8, scores, jnp.full((8, QC), -jnp.inf, F32), unroll=8)
        top = jnp.max(top, axis=0, keepdims=True)
        if c == 0:
            wait_all(fv_c)

        def weigh(t, o):
            eb = jnp.exp2(s.st[t] - top).astype(BF)
            s.et[t, :, lanes] = eb
            values = jnp.concatenate([s.v_r[t], jnp.ones((16, T), BF)], axis=0)
            return o + jnp.dot(values, eb, preferred_element_type=F32)

        o = lax.fori_loop(0, 8, weigh, jnp.zeros((HD + 16, QC), F32), unroll=8)
        inverse = 1.0 / o[HD : HD + 1]
        o = o[0:HD]
        s.inverse[:, lanes] = inverse
        o = (o * inverse).astype(BF)
        for a in range(2):
            s.o_s[c * 2 + a] = o[:, a * T : (a + 1) * T]
    o_c = [swapped(k, s.o_s.at[around(k)], s.mix_r.at[x], s.os, s.orr) for k in (1, 2, 3, 0)]

    wait_all(d_c)
    for a in range(4):
        lanes = slice(a * T, (a + 1) * T)
        d = s.d_r[a].astype(F32)
        inverse = s.inverse[:, lanes]
        s.delta[:, lanes] = jnp.sum(d * s.o_s[a].astype(F32), axis=0, keepdims=True) * inverse
        d = (d * inverse).astype(BF)
        s.dt[:, lanes] = d
        s.dn[lanes, :] = d.T
    for t in range(8):
        s.vn[t] = s.v_r[t].T
    s.dq[...] = jnp.zeros_like(s.dq)

    def back(first, k, slot):
        t = first + around(k)
        for c in range(Q // QC):
            lanes = slice(c * QC, (c + 1) * QC)
            dp_ = jnp.dot(s.vn[t], s.dt[:, lanes], preferred_element_type=F32)
            s.dsb[slot, :, lanes] = (s.et[t, :, lanes].astype(F32) * (dp_ - s.delta[:, lanes])).astype(BF)
        dk = jnp.dot(s.dsb[slot], s.qn[...], preferred_element_type=F32) * (1 / LOG2E)
        dv = jnp.dot(s.et[t], s.dn[...], preferred_element_type=F32)
        s.dq[...] += jnp.dot(s.k_r[t], s.dsb[slot], preferred_element_type=F32)
        return dk, dv

    def back_pair(first, ks, out):
        for slot, k in enumerate(ks):
            dk, dv = back(first, k, slot)
            out[around(k), 0:HD] = dk.astype(BF).T
            out[around(k), HD:] = dv.astype(BF).T

    def sibling_pair(ks):
        back_pair(4, ks, s.part_s)
        for k in ks:
            i = around(k)
            p_c[k] = go(remote(s.part_s.at[i], s.part_r.at[i], s.ps.at[k], s.pr.at[k], sibling))

    p_c = {}
    sibling_pair((1, 2))

    wait_all(o_c)
    mixed = s.mix_r[...].reshape(F, T).T
    op_c = []
    for k in range(1, 4):
        rows = aligned(lax.rem(hd + k, 4) * F, F, F)
        s.op_s[k - 1] = lax.dot_general(mixed, s.w[3, rows, :], NT, preferred_element_type=F32).astype(BF)
        op_c.append(go(remote(s.op_s.at[k - 1], s.op_r.at[k - 1], s.ops.at[k - 1], s.opr.at[k - 1], at_y(k))))

    sibling_pair((3, 0))

    def away(p, left, right):
        for l in range(2):
            rows = aligned((l * 2 + 1 - core) * F, F, F)
            s.g_s[p, l] = jnp.dot(left[rows, :], right, preferred_element_type=F32).astype(BF)
        return go(remote(s.g_s.at[p], s.g_r.at[p], s.gs.at[p], s.gr.at[p], sibling))

    first_c, second_c = {}, {}

    def keep(p, left, right, copy):
        copy.wait()
        parts = [(i, r0, n, by_x) for i, (q, r0, n, by_x) in enumerate(PARTS) if q == p]
        for l in range(2):
            rows = aligned((l * 2 + core) * F, F, F)
            g = jnp.dot(left[rows, :], right, preferred_element_type=F32) + s.g_r[p, l].astype(F32)
            g = g.astype(BF)
            for xo in range(4):
                for h in range(2):
                    for i, r0, n, by_x in parts:
                        start = xo * 96 + h * 48 + r0
                        slot = xo * 4 + h * 2 + l if by_x else (h * 2 + l) * 4 + xo
                        getattr(s, f"h1_{i}")[slot] = g[start : start + n]
        for i, r0, n, by_x in parts:
            h1, s1 = getattr(s, f"h1_{i}"), getattr(s, f"s1_{i}")
            first_c[i] = []
            for k in range(1, 4):
                to = lax.rem((x if by_x else z) + k, 4)
                device = at_x(k) if by_x else at_z(k)
                c = remote(h1.at[pl.ds(to * 4, 4)], s1.at[k - 1], s.s1s.at[i, k], s.s1r.at[i, k], device)
                first_c[i].append(go(c))

    def second(i):
        by_x = PARTS[i][3]
        h1, s1 = getattr(s, f"h1_{i}"), getattr(s, f"s1_{i}")
        h2, s2 = getattr(s, f"h2_{i}"), getattr(s, f"s2_{i}")
        wait_all(first_c[i])
        own = h1[pl.ds((x if by_x else z) * 4, 4)].astype(F32)
        for k in range(3):
            own = own + s1[k].astype(F32)
        h2[...] = own.astype(BF)
        second_c[i] = []
        for k in range(1, 4):
            to = lax.rem((z if by_x else x) + k, 4)
            device = at_z(k) if by_x else at_x(k)
            c = remote(h2.at[to], s2.at[k - 1], s.s2s.at[i, k], s.s2r.at[i, k], device)
            second_c[i].append(go(c))

    def last(i):
        p, r0, n, by_x = PARTS[i]
        h2, s2 = getattr(s, f"h2_{i}"), getattr(s, f"s2_{i}")
        wait_all(second_c[i])
        own = h2[z if by_x else x].astype(F32)
        for k in range(3):
            own = own + s2[k].astype(F32)
        pg_out[p, r0 : r0 + n] = own

    dkv_c = []
    for ks in ((1, 2), (3, 0)):
        for slot, k in enumerate(ks):
            dk, dv = back(0, k, slot)
            p_c[k].wait()
            i = around(k)
            s.dkv_s[i, 0:HD] = (dk.T + s.part_r[i, 0:HD].astype(F32)).astype(BF)
            s.dkv_s[i, HD:] = (dv.T + s.part_r[i, HD:].astype(F32)).astype(BF)
        for k in ks:
            dkv_c.append(swapped(k, s.dkv_s.at[around(k)], s.dkv_r.at[x], s.dkvs, s.dkvr))
    for a in range(4):
        s.dq_s[a] = (s.dq[:, a * T : (a + 1) * T] * SCALE).astype(BF)
    dq_c = [swapped(k, s.dq_s.at[around(k)], s.dq_r.at[x], s.dqs, s.dqr) for k in (1, 2, 3, 0)]

    summed = lax.dot_general(mixed, s.w[3, aligned(hd * F, F, F), :], NT, preferred_element_type=F32)
    wait_all(op_c)
    for k in range(3):
        summed = summed + s.op_r[k].astype(F32)
    mine = aligned(hd * F, F, 128)
    s.res[...] = (s.frames[:, mine].astype(F32) + summed).astype(BF)
    halos = [
        go(remote(s.res.at[T - HALF : T], s.rhalo.at[0], s.rh_s.at[0], s.rh_r.at[0], at_tm(1))),
        go(remote(s.res.at[0:HALF], s.rhalo.at[1], s.rh_s.at[1], s.rh_r.at[1], at_tm(7))),
    ]

    bg_t, frames_t = s.w.at[0], s.w.at[1]
    bg_t[...] = s.bg[...].T
    g3 = away(3, bg_t, mixed)

    s.rpad[HALF : HALF + T] = s.res[...].astype(F32)
    wait_all(halos)
    s.rpad[0:HALF] = jnp.where(tm > 0, s.rhalo[0].astype(F32), 0.0)
    s.rpad[HALF + T :] = jnp.where(tm < 7, s.rhalo[1].astype(F32), 0.0)

    def conv(it, carry):
        i, l = it // 3, lax.rem(it, 3)
        lanes = aligned(l * 128, 128, 128)
        whole = aligned(hd * F + l * 128, 128, 128)
        base = i * CR
        window = lambda o, n: s.rpad[aligned(base + o, n, 8), lanes]
        acc = correlate(
            window(HALF, CR), window, lambda j: s.tapsf[j : j + 1, whole], {j: j for j in range(KW)}, CR
        )
        s.enc[aligned(base, CR, CR), lanes] = acc.astype(BF)
        return carry

    lax.fori_loop(0, 3 * T // CR, conv, 0)
    e_c = [go(remote(s.enc, enc_out.at[:, mine], s.es.at[k], s.er.at[k], at_y(k))) for k in range(1, 4)]
    e_c.append(go(pltpu.make_async_copy(s.enc, enc_out.at[:, mine], s.in_sem.at[8])))
    keep(3, bg_t, mixed, g3)
    frames_t[...] = s.frames[...].T
    wait_all(dkv_c)
    dk = s.dkv_r[:, 0:HD].reshape(F, T).T
    g1 = away(1, frames_t, dk)
    dv = s.dkv_r[:, HD:].reshape(F, T).T
    g2 = away(2, frames_t, dv)
    wait_all(dq_c)
    dq = s.dq_r[...].reshape(F, T).T
    g0 = away(0, frames_t, dq)
    keep(1, frames_t, dk, g1)
    keep(2, frames_t, dv, g2)
    keep(0, frames_t, dq, g0)

    s.kacc[...] = jnp.zeros_like(s.kacc)

    def taps_grad(it, carry):
        i, l = it // 3, lax.rem(it, 3)
        lanes = aligned(l * 128, 128, 128)
        base = i * CR
        up = s.cot[aligned(base, CR, CR), aligned(hd * F + l * 128, 128, 128)].astype(F32)
        edge = jnp.zeros((8, 128), F32)
        up = jnp.concatenate([edge, up, edge], axis=0)
        for r in range(8):
            moved = up[8 - r : CR + 16 - r] if r else up[8 : CR + 8]
            for a in range(KW // 8):
                term = moved * s.rpad[aligned(base + 8 * a, CR + 8 if r else CR, 8), lanes]
                s.kacc[8 * a + r, :, lanes] += jnp.sum(term.reshape(-1, 8, 128), axis=0)
        return carry

    lax.fori_loop(0, 3 * T // CR, taps_grad, 0)
    for j in range(KW):
        s.kg[j] = jnp.sum(s.kacc[j], axis=0, keepdims=True)
    kg_c = []
    for k in range(1, 32):
        to = lax.rem(me + k, 32)
        kg_c.append(go(remote(s.kg.at[to], s.kgr.at[k], s.kgs.at[k], s.kgrs.at[k], at_plane(k))))

    for i in (0, 2, 1, 4, 3):
        second(i)
    wait_all(kg_c)
    total = s.kg[me]
    for k in range(1, 32):
        total = total + s.kgr[k]
    s.kgy[hd] = total
    ky_c = [go(remote(s.kgy.at[hd], s.kgy.at[hd], s.kys.at[k], s.kyr.at[k], at_y(k))) for k in range(1, 4)]
    for i in (0, 2, 1, 4, 3):
        last(i)
    wait_all(ky_c)
    for y in range(4):
        kg_out[:, y * F : (y + 1) * F] = s.kgy[y]
    wait_all(e_c)


def shards(frames, projections, kernel, pattern, cotangent):
    vmem = pl.BlockSpec(memory_space=pltpu.VMEM)
    anym = pl.BlockSpec(memory_space=pl.ANY)
    enc, pg, kg = pl.pallas_call(
        layer_kernel,
        out_shape=(
            jax.ShapeDtypeStruct((T, C), BF),
            jax.ShapeDtypeStruct((4, 48, F), F32),
            jax.ShapeDtypeStruct((1, C), F32),
        ),
        in_specs=[anym, anym, anym, vmem, anym],
        out_specs=(anym, vmem, vmem),
        scratch_shapes=list(SCRATCH.values()),
        compiler_params=pltpu.CompilerParams(
            collective_id=0, has_side_effects=True, vmem_limit_bytes=55 << 20
        ),
        name="conformer_layer",
    )(frames, projections, kernel, jnp.transpose(pattern, (1, 0, 2)), cotangent)
    return enc[None], pg, kg


def solution(mesh):
    placed = (
        P("dp", "tm", None),
        P(None, None, "head"),
        P(),
        P("dp", "tm", None),
        P("dp", "tm", None),
    )
    return jax.shard_map(
        shards,
        mesh=mesh,
        in_specs=placed,
        out_specs=(P("dp", "tm", None), P(None, ("dp", "tm"), "head"), P(("dp", "tm"), None)),
        check_vma=False,
    )
```

```python
import types

import jax
import jax.numpy as jnp
from jax import lax
from jax.experimental import pallas as pl
from jax.experimental.pallas import tpu as pltpu
from jax.sharding import PartitionSpec as P

HD = 96
BLK = 64
KW = 32
HALF = KW // 2
T = 384
C = 1536
F = 384
Q = 4 * T
QC = 768
CR = 192
MESH = pl.DeviceIdType.MESH
BF = jnp.bfloat16
F32 = jnp.float32
SCALE = HD**-0.5
LOG2E = 1.4426950408889634
NT = (((1,), (1,)), ((), ()))


def dma(*shape):
    return pltpu.SemaphoreType.DMA(shape)


def vm(dtype, *shape):
    return pltpu.VMEM(shape, dtype)


SCRATCH = dict(
    frames=vm(BF, T, C), cot=vm(BF, T, C), w=vm(BF, 4, C, F), taps=vm(BF, KW, C),
    in_sem=dma(9),
    upad=vm(F32, T + 2 * HALF, C), uhalo=vm(BF, 2, HALF, C), tapsf=vm(F32, KW, C),
    bg=vm(BF, T, C), uh_s=dma(2), uh_r=dma(2),
    q_s=vm(BF, 4, HD + 16, T), k_s=vm(BF, 4, HD, T), v_s=vm(BF, 4, HD, T), d_s=vm(BF, 4, HD, T),
    q_r=vm(BF, 4, HD + 16, T), d_r=vm(BF, 4, HD, T), k_r=vm(BF, 8, HD, T), v_r=vm(BF, 8, HD, T),
    qs=dma(4), qr=dma(4), ks=dma(4), kr=dma(4), vs=dma(4), vr=dma(4), ds=dma(4), dr=dma(4),
    fks=dma(4), fkr=dma(4), fvs=dma(4), fvr=dma(4),
    kn=vm(BF, 8, T, HD), vn=vm(BF, 8, T, HD), qt=vm(BF, HD, Q), qn=vm(BF, Q, HD), dt=vm(BF, HD, Q), dn=vm(BF, Q, HD),
    live=vm(F32, 64, Q), st=vm(F32, 8, T, QC), et=vm(BF, 8, T, Q), dsb=vm(BF, 2, T, Q), dq=vm(F32, HD, Q),
    inverse=vm(F32, 1, Q), delta=vm(F32, 1, Q),
    o_s=vm(BF, 4, HD, T), dq_s=vm(BF, 4, HD, T), part_s=vm(BF, 4, 2 * HD, T), part_r=vm(BF, 4, 2 * HD, T),
    dkv_s=vm(BF, 4, 2 * HD, T), mix_r=vm(BF, 4, HD, T), dq_r=vm(BF, 4, HD, T), dkv_r=vm(BF, 4, 2 * HD, T),
    os=dma(4), orr=dma(4), dqs=dma(4), dqr=dma(4), ps=dma(4), pr=dma(4), dkvs=dma(4), dkvr=dma(4),
    op_s=vm(BF, 3, T, F), op_r=vm(BF, 3, T, F), ops=dma(3), opr=dma(3),
    rpad=vm(F32, T + 2 * HALF, F), res=vm(BF, T, F), rhalo=vm(BF, 2, HALF, F), enc=vm(BF, T, F),
    rh_s=dma(2), rh_r=dma(2), es=dma(4), er=dma(4),
    kacc=vm(F32, KW, 8, F), kg=vm(F32, KW, 1, F), kgr=vm(F32, KW, 1, F), kgy=vm(F32, 4, 1, F),
    kgs=dma(32), kgrs=dma(32), kys=dma(4), kyr=dma(4),
    g_s=vm(BF, 4, 2, F, F), g_r=vm(BF, 4, 2, F, F), gs=dma(4), gr=dma(4),
    s1s=dma(5, 4), s1r=dma(5, 4), s2s=dma(5, 4), s2r=dma(5, 4),
)


PARTS = ((3, 0, 48, True), (1, 0, 48, False), (2, 0, 48, True), (0, 0, 32, False), (0, 32, 16, True))
for i, (_, _, n, _) in enumerate(PARTS):
    SCRATCH[f"h1_{i}"] = vm(BF, 16, n, F)
    SCRATCH[f"s1_{i}"] = vm(BF, 3, 4, n, F)
    SCRATCH[f"h2_{i}"] = vm(BF, 4, n, F)
    SCRATCH[f"s2_{i}"] = vm(BF, 3, n, F)


def remote(src, dst, ssem, rsem, device):
    return pltpu.make_async_remote_copy(
        src_ref=src, dst_ref=dst, send_sem=ssem, recv_sem=rsem, device_id=device, device_id_type=MESH
    )


class Either:
    def __init__(self, here, src, dst, ssem, rsem, device):
        self.here = here
        self.local = pltpu.make_async_copy(src, dst, rsem)
        self.far = remote(src, dst, ssem, rsem, device)

    def start(self):
        pl.when(self.here)(lambda: self.local.start())
        pl.when(jnp.logical_not(self.here))(lambda: self.far.start())

    def wait(self):
        pl.when(self.here)(lambda: self.local.wait())
        pl.when(jnp.logical_not(self.here))(lambda: self.far.wait())


def go(copy):
    copy.start()
    return copy


def wait_all(copies):
    for c in copies:
        c.wait()


def correlate(acc, load, taps, offsets, rows):
    for r in range(8):
        part = None
        for o in sorted(offsets):
            if o % 8 == r:
                term = taps(offsets[o]) * load(o - r, rows + 8 if r else rows)
                part = term if part is None else part + term
        acc = acc + (part[r : r + rows] if r else part)
    return acc


def aligned(start, size, by):
    return pl.ds(pl.multiple_of(start, by), size)


def layer_kernel(frames_h, w_h, taps_h, pattern_h, cot_h, enc_out, pg_out, kg_out, *scratch):
    s = types.SimpleNamespace(**dict(zip(SCRATCH, scratch)))
    dp, tm, hd = lax.axis_index("dp"), lax.axis_index("tm"), lax.axis_index("head")
    zl, core = dp // 2, lax.rem(dp, 2)
    x, zh = tm // 2, lax.rem(tm, 2)
    z = zh * 2 + zl
    me = dp * 8 + tm
    around = lambda k: lax.rem(x + k, 4)
    at_tm = lambda k: (dp, lax.rem(tm + k, 8), hd)
    at_x = lambda k: (dp, around(k) * 2 + zh, hd)
    at_y = lambda k: (dp, tm, lax.rem(hd + k, 4))
    sibling = (zl * 2 + 1 - core, tm, hd)

    def at_z(k):
        to = lax.rem(z + k, 4)
        return (lax.rem(to, 2) * 2 + core, x * 2 + to // 2, hd)

    def at_plane(k):
        to = lax.rem(me + k, 32)
        return (to // 8, lax.rem(to, 8), hd)

    def swapped(k, src, dst, ssem, rsem):
        device = (zl * 2 + zh, around(k) * 2 + core, hd)
        if k:
            return go(remote(src, dst, ssem.at[k], rsem.at[k], device))
        return go(Either(zh == core, src, dst, ssem.at[0], rsem.at[0], device))

    load = [
        go(pltpu.make_async_copy(a, b, s.in_sem.at[i]))
        for i, (a, b) in enumerate(
            [
                (frames_h.at[0], s.frames),
                (w_h.at[1], s.w.at[1]),
                (w_h.at[0], s.w.at[0]),
                (w_h.at[2], s.w.at[2]),
                (cot_h.at[0], s.cot),
                (taps_h, s.taps),
                (w_h.at[3], s.w.at[3]),
            ]
        )
    ]
    barrier = pltpu.get_barrier_semaphore()
    others = [at_plane(k) for k in range(1, 32)] + [at_y(k) for k in range(1, 4)]
    for device in others:
        pl.semaphore_signal(barrier, inc=1, device_id=device, device_id_type=MESH)

    def projected(rows, p, factor=None):
        y = jnp.dot(rows, s.w[p], preferred_element_type=F32)
        return (y if factor is None else y * factor).astype(BF).T

    load[0].wait()
    load[1].wait()
    y = projected(s.frames[...], 1)
    for h in range(4):
        s.k_s[h] = y[h * HD : (h + 1) * HD]
    pl.semaphore_wait(barrier, len(others))
    load[4].wait()
    halos = [
        go(remote(s.cot.at[T - HALF : T], s.uhalo.at[0], s.uh_s.at[0], s.uh_r.at[0], at_tm(1))),
        go(remote(s.cot.at[0:HALF], s.uhalo.at[1], s.uh_s.at[1], s.uh_r.at[1], at_tm(7))),
    ]
    k_c = [swapped(k, s.k_s.at[around(k)], s.k_r.at[x], s.ks, s.kr) for k in (1, 2, 3, 0)]
    load[2].wait()
    y = projected(s.frames[...], 0, SCALE * LOG2E)
    row = lax.broadcasted_iota(jnp.int32, (16, T), 0)
    block = lax.broadcasted_iota(jnp.int32, (1, T), 1) // BLK
    phase = count = jnp.zeros((1, T), F32)
    for b in range(6):
        entries = pattern_h[b]
        phase = jnp.where(block == b, entries[:, 0:1].astype(F32), phase)
        count = jnp.where(block == b, jnp.sum((entries >= 0).astype(F32), axis=1, keepdims=True), count)
    meta = jnp.where(row == 0, phase, jnp.where(row == 1, count, 0.0)).astype(BF)
    for h in range(4):
        s.q_s[h, 0:HD] = y[h * HD : (h + 1) * HD]
        s.q_s[h, HD:] = meta
    q_c = [swapped(k, s.q_s.at[around(k)], s.q_r.at[x], s.qs, s.qr) for k in (1, 2, 3, 0)]
    load[3].wait()
    y = projected(s.frames[...], 2)
    for h in range(4):
        s.v_s[h] = y[h * HD : (h + 1) * HD]
    v_c = [swapped(k, s.v_s.at[around(k)], s.v_r.at[x], s.vs, s.vr) for k in (1, 2, 3, 0)]

    load[5].wait()
    s.tapsf[...] = s.taps[...].astype(F32)
    s.upad[HALF : HALF + T] = s.cot[...].astype(F32)
    wait_all(halos)
    s.upad[0:HALF] = jnp.where(tm > 0, s.uhalo[0].astype(F32), 0.0)
    s.upad[HALF + T :] = jnp.where(tm < 7, s.uhalo[1].astype(F32), 0.0)

    def conv_back(it, carry):
        i, l = it // 12, lax.rem(it, 12)
        lanes = aligned(l * 128, 128, 128)
        base = i * CR
        acc = correlate(
            s.upad[aligned(base + HALF, CR, 16), lanes],
            lambda o, n: s.upad[aligned(base + o, n, 8), lanes],
            lambda j: s.tapsf[j : j + 1, lanes],
            {2 * HALF - j: j for j in range(KW)},
            CR,
        )
        s.bg[aligned(base, CR, CR), lanes] = acc.astype(BF)
        return carry

    lax.fori_loop(0, 12 * T // CR, conv_back, 0)
    load[6].wait()
    y = projected(s.bg[...], 3)
    for h in range(4):
        s.d_s[h] = y[h * HD : (h + 1) * HD]
    d_c = [swapped(k, s.d_s.at[around(k)], s.d_r.at[x], s.ds, s.dr) for k in (1, 2, 3, 0)]

    def forward(k, copy, buf, ssem, rsem):
        copy.wait()
        src = lax.rem(x + 4 - k, 4)
        return go(remote(buf.at[src], buf.at[4 + src], ssem.at[k], rsem.at[k], sibling))

    fk_c = [forward(k, c, s.k_r, s.fks, s.fkr) for k, c in zip((1, 2, 3, 0), k_c)]
    wait_all(q_c)
    for a in range(4):
        lanes = slice(a * T, (a + 1) * T)
        s.qt[:, lanes] = s.q_r[a, 0:HD]
        s.qn[lanes, :] = s.q_r[a, 0:HD].T
        got = s.q_r[a, HD:].astype(F32)
        row = lax.broadcasted_iota(jnp.int32, (64, T), 0)
        tile = row // 8
        owner = lax.rem(tile, 4) * 2 + jnp.where(tile < 4, core, 1 - core)
        key_block = owner * 6 + lax.rem(row, 8)
        query_block = (a * 2 + core) * 6 + lax.broadcasted_iota(jnp.int32, (64, T), 1) // BLK
        far = (lax.rem(key_block, 4).astype(F32) == got[0:1]) & ((key_block // 4).astype(F32) < got[1:2])
        near = jnp.abs(key_block - query_block) < 2
        s.live[:, lanes] = jnp.where(far | near, 1.0, 0.0)
    for t in range(4):
        s.kn[t] = s.k_r[t].T
    fv_c = [forward(k, c, s.v_r, s.fvs, s.fvr) for k, c in zip((1, 2, 3, 0), v_c)]
    wait_all(fk_c)
    for t in range(4, 8):
        s.kn[t] = s.k_r[t].T

    for c in range(Q // QC):
        lanes = slice(c * QC, (c + 1) * QC)
        q_t = s.qt[:, lanes]

        def scores(t, top):
            sc = jnp.dot(s.kn[t], q_t, preferred_element_type=F32)
            mask = s.live[aligned(t * 8, 8, 8), lanes]
            for b in range(6):
                part = jnp.where(mask[b : b + 1] > 0.5, sc[b * BLK : (b + 1) * BLK], -1e30)
                top = jnp.maximum(top, jnp.max(part.reshape(8, 8, QC), axis=0))
                s.st[t, b * BLK : (b + 1) * BLK] = part
            return top

        top = lax.fori_loop(0, 8, scores, jnp.full((8, QC), -jnp.inf, F32), unroll=8)
        top = jnp.max(top, axis=0, keepdims=True)
        if c == 0:
            wait_all(fv_c)

        def weigh(t, o):
            eb = jnp.exp2(s.st[t] - top).astype(BF)
            s.et[t, :, lanes] = eb
            values = jnp.concatenate([s.v_r[t], jnp.ones((16, T), BF)], axis=0)
            return o + jnp.dot(values, eb, preferred_element_type=F32)

        o = lax.fori_loop(0, 8, weigh, jnp.zeros((HD + 16, QC), F32), unroll=8)
        inverse = 1.0 / o[HD : HD + 1]
        o = o[0:HD]
        s.inverse[:, lanes] = inverse
        o = (o * inverse).astype(BF)
        for a in range(2):
            s.o_s[c * 2 + a] = o[:, a * T : (a + 1) * T]
    o_c = [swapped(k, s.o_s.at[around(k)], s.mix_r.at[x], s.os, s.orr) for k in (1, 2, 3, 0)]

    wait_all(d_c)
    for a in range(4):
        lanes = slice(a * T, (a + 1) * T)
        d = s.d_r[a].astype(F32)
        inverse = s.inverse[:, lanes]
        s.delta[:, lanes] = jnp.sum(d * s.o_s[a].astype(F32), axis=0, keepdims=True) * inverse
        d = (d * inverse).astype(BF)
        s.dt[:, lanes] = d
        s.dn[lanes, :] = d.T
    for t in range(8):
        s.vn[t] = s.v_r[t].T
    s.dq[...] = jnp.zeros_like(s.dq)

    def back(first, k, slot):
        t = first + around(k)
        for c in range(Q // QC):
            lanes = slice(c * QC, (c + 1) * QC)
            dp_ = jnp.dot(s.vn[t], s.dt[:, lanes], preferred_element_type=F32)
            s.dsb[slot, :, lanes] = (s.et[t, :, lanes].astype(F32) * (dp_ - s.delta[:, lanes])).astype(BF)
        dk = jnp.dot(s.dsb[slot], s.qn[...], preferred_element_type=F32) * (1 / LOG2E)
        dv = jnp.dot(s.et[t], s.dn[...], preferred_element_type=F32)
        s.dq[...] += jnp.dot(s.k_r[t], s.dsb[slot], preferred_element_type=F32)
        return dk, dv

    def back_pair(first, ks, out):
        for slot, k in enumerate(ks):
            dk, dv = back(first, k, slot)
            out[around(k), 0:HD] = dk.astype(BF).T
            out[around(k), HD:] = dv.astype(BF).T

    def sibling_pair(ks):
        back_pair(4, ks, s.part_s)
        for k in ks:
            i = around(k)
            p_c[k] = go(remote(s.part_s.at[i], s.part_r.at[i], s.ps.at[k], s.pr.at[k], sibling))

    p_c = {}
    sibling_pair((1, 2))

    wait_all(o_c)
    mixed = s.mix_r[...].reshape(F, T).T
    op_c = []
    for k in range(1, 4):
        rows = aligned(lax.rem(hd + k, 4) * F, F, F)
        s.op_s[k - 1] = lax.dot_general(mixed, s.w[3, rows, :], NT, preferred_element_type=F32).astype(BF)
        op_c.append(go(remote(s.op_s.at[k - 1], s.op_r.at[k - 1], s.ops.at[k - 1], s.opr.at[k - 1], at_y(k))))

    sibling_pair((3, 0))

    def away(p, left, right):
        for l in range(2):
            rows = aligned((l * 2 + 1 - core) * F, F, F)
            s.g_s[p, l] = jnp.dot(left[rows, :], right, preferred_element_type=F32).astype(BF)
        return go(remote(s.g_s.at[p], s.g_r.at[p], s.gs.at[p], s.gr.at[p], sibling))

    first_c, second_c = {}, {}

    def keep(p, left, right, copy):
        copy.wait()
        parts = [(i, r0, n, by_x) for i, (q, r0, n, by_x) in enumerate(PARTS) if q == p]
        for l in range(2):
            rows = aligned((l * 2 + core) * F, F, F)
            g = jnp.dot(left[rows, :], right, preferred_element_type=F32) + s.g_r[p, l].astype(F32)
            g = g.astype(BF)
            for xo in range(4):
                for h in range(2):
                    for i, r0, n, by_x in parts:
                        start = xo * 96 + h * 48 + r0
                        slot = xo * 4 + h * 2 + l if by_x else (h * 2 + l) * 4 + xo
                        getattr(s, f"h1_{i}")[slot] = g[start : start + n]
        for i, r0, n, by_x in parts:
            h1, s1 = getattr(s, f"h1_{i}"), getattr(s, f"s1_{i}")
            first_c[i] = []
            for k in range(1, 4):
                to = lax.rem((x if by_x else z) + k, 4)
                device = at_x(k) if by_x else at_z(k)
                c = remote(h1.at[pl.ds(to * 4, 4)], s1.at[k - 1], s.s1s.at[i, k], s.s1r.at[i, k], device)
                first_c[i].append(go(c))

    def second(i):
        by_x = PARTS[i][3]
        h1, s1 = getattr(s, f"h1_{i}"), getattr(s, f"s1_{i}")
        h2, s2 = getattr(s, f"h2_{i}"), getattr(s, f"s2_{i}")
        wait_all(first_c[i])
        own = h1[pl.ds((x if by_x else z) * 4, 4)].astype(F32)
        for k in range(3):
            own = own + s1[k].astype(F32)
        h2[...] = own.astype(BF)
        second_c[i] = []
        for k in range(1, 4):
            to = lax.rem((z if by_x else x) + k, 4)
            device = at_z(k) if by_x else at_x(k)
            c = remote(h2.at[to], s2.at[k - 1], s.s2s.at[i, k], s.s2r.at[i, k], device)
            second_c[i].append(go(c))

    def last(i):
        p, r0, n, by_x = PARTS[i]
        h2, s2 = getattr(s, f"h2_{i}"), getattr(s, f"s2_{i}")
        wait_all(second_c[i])
        own = h2[z if by_x else x].astype(F32)
        for k in range(3):
            own = own + s2[k].astype(F32)
        pg_out[p, r0 : r0 + n] = own

    dkv_c = []
    for ks in ((1, 2), (3, 0)):
        for slot, k in enumerate(ks):
            dk, dv = back(0, k, slot)
            p_c[k].wait()
            i = around(k)
            s.dkv_s[i, 0:HD] = (dk.T + s.part_r[i, 0:HD].astype(F32)).astype(BF)
            s.dkv_s[i, HD:] = (dv.T + s.part_r[i, HD:].astype(F32)).astype(BF)
        for k in ks:
            dkv_c.append(swapped(k, s.dkv_s.at[around(k)], s.dkv_r.at[x], s.dkvs, s.dkvr))
    for a in range(4):
        s.dq_s[a] = (s.dq[:, a * T : (a + 1) * T] * SCALE).astype(BF)
    dq_c = [swapped(k, s.dq_s.at[around(k)], s.dq_r.at[x], s.dqs, s.dqr) for k in (1, 2, 3, 0)]

    summed = lax.dot_general(mixed, s.w[3, aligned(hd * F, F, F), :], NT, preferred_element_type=F32)
    wait_all(op_c)
    for k in range(3):
        summed = summed + s.op_r[k].astype(F32)
    mine = aligned(hd * F, F, 128)
    s.res[...] = (s.frames[:, mine].astype(F32) + summed).astype(BF)
    halos = [
        go(remote(s.res.at[T - HALF : T], s.rhalo.at[0], s.rh_s.at[0], s.rh_r.at[0], at_tm(1))),
        go(remote(s.res.at[0:HALF], s.rhalo.at[1], s.rh_s.at[1], s.rh_r.at[1], at_tm(7))),
    ]

    bg_t, frames_t = s.w.at[0], s.w.at[1]
    bg_t[...] = s.bg[...].T
    g3 = away(3, bg_t, mixed)

    keep(3, bg_t, mixed, g3)
    frames_t[...] = s.frames[...].T
    wait_all(dkv_c)
    dk = s.dkv_r[:, 0:HD].reshape(F, T).T
    g1 = away(1, frames_t, dk)
    dv = s.dkv_r[:, HD:].reshape(F, T).T
    g2 = away(2, frames_t, dv)
    wait_all(dq_c)
    dq = s.dq_r[...].reshape(F, T).T
    g0 = away(0, frames_t, dq)
    keep(1, frames_t, dk, g1)
    keep(2, frames_t, dv, g2)
    keep(0, frames_t, dq, g0)

    s.rpad[HALF : HALF + T] = s.res[...].astype(F32)
    wait_all(halos)
    s.rpad[0:HALF] = jnp.where(tm > 0, s.rhalo[0].astype(F32), 0.0)
    s.rpad[HALF + T :] = jnp.where(tm < 7, s.rhalo[1].astype(F32), 0.0)

    def conv(it, carry):
        i, l = it // 3, lax.rem(it, 3)
        lanes = aligned(l * 128, 128, 128)
        whole = aligned(hd * F + l * 128, 128, 128)
        base = i * CR
        window = lambda o, n: s.rpad[aligned(base + o, n, 8), lanes]
        acc = correlate(
            window(HALF, CR), window, lambda j: s.tapsf[j : j + 1, whole], {j: j for j in range(KW)}, CR
        )
        s.enc[aligned(base, CR, CR), lanes] = acc.astype(BF)
        return carry

    lax.fori_loop(0, 3 * T // CR, conv, 0)
    e_c = [go(remote(s.enc, enc_out.at[:, mine], s.es.at[k], s.er.at[k], at_y(k))) for k in range(1, 4)]
    e_c.append(go(pltpu.make_async_copy(s.enc, enc_out.at[:, mine], s.in_sem.at[8])))

    s.kacc[...] = jnp.zeros_like(s.kacc)

    def taps_grad(it, carry):
        i, l = it // 3, lax.rem(it, 3)
        lanes = aligned(l * 128, 128, 128)
        base = i * CR
        up = s.cot[aligned(base, CR, CR), aligned(hd * F + l * 128, 128, 128)].astype(F32)
        edge = jnp.zeros((8, 128), F32)
        up = jnp.concatenate([edge, up, edge], axis=0)
        for r in range(8):
            moved = up[8 - r : CR + 16 - r] if r else up[8 : CR + 8]
            for a in range(KW // 8):
                term = moved * s.rpad[aligned(base + 8 * a, CR + 8 if r else CR, 8), lanes]
                s.kacc[8 * a + r, :, lanes] += jnp.sum(term.reshape(-1, 8, 128), axis=0)
        return carry

    lax.fori_loop(0, 3 * T // CR, taps_grad, 0)
    for j in range(KW):
        s.kg[j] = jnp.sum(s.kacc[j], axis=0, keepdims=True)
    kg_c = []
    for k in range(1, 32):
        to = lax.rem(me + k, 32)
        kg_c.append(go(remote(s.kg.at[to], s.kgr.at[k], s.kgs.at[k], s.kgrs.at[k], at_plane(k))))

    for i in (0, 2, 1, 4, 3):
        second(i)
    wait_all(kg_c)
    total = s.kg[me]
    for k in range(1, 32):
        total = total + s.kgr[k]
    s.kgy[hd] = total
    ky_c = [go(remote(s.kgy.at[hd], s.kgy.at[hd], s.kys.at[k], s.kyr.at[k], at_y(k))) for k in range(1, 4)]
    for i in (0, 2, 1, 4, 3):
        last(i)
    wait_all(ky_c)
    for y in range(4):
        kg_out[:, y * F : (y + 1) * F] = s.kgy[y]
    wait_all(e_c)


def shards(frames, projections, kernel, pattern, cotangent):
    vmem = pl.BlockSpec(memory_space=pltpu.VMEM)
    anym = pl.BlockSpec(memory_space=pl.ANY)
    enc, pg, kg = pl.pallas_call(
        layer_kernel,
        out_shape=(
            jax.ShapeDtypeStruct((T, C), BF),
            jax.ShapeDtypeStruct((4, 48, F), F32),
            jax.ShapeDtypeStruct((1, C), F32),
        ),
        in_specs=[anym, anym, anym, vmem, anym],
        out_specs=(anym, vmem, vmem),
        scratch_shapes=list(SCRATCH.values()),
        compiler_params=pltpu.CompilerParams(
            collective_id=0, has_side_effects=True, vmem_limit_bytes=55 << 20
        ),
        name="conformer_layer",
    )(frames, projections, kernel, jnp.transpose(pattern, (1, 0, 2)), cotangent)
    return enc[None], pg, kg


def solution(mesh):
    placed = (
        P("dp", "tm", None),
        P(None, None, "head"),
        P(),
        P("dp", "tm", None),
        P("dp", "tm", None),
    )
    return jax.shard_map(
        shards,
        mesh=mesh,
        in_specs=placed,
        out_specs=(P("dp", "tm", None), P(None, ("dp", "tm"), "head"), P(("dp", "tm"), None)),
        check_vma=False,
    )
```

```python
import types

import jax
import jax.numpy as jnp
from jax import lax
from jax.experimental import pallas as pl
from jax.experimental.pallas import tpu as pltpu
from jax.sharding import PartitionSpec as P

HD = 96
BLK = 64
KW = 32
HALF = KW // 2
T = 384
C = 1536
F = 384
Q = 4 * T
QC = 768
CR = 192
MESH = pl.DeviceIdType.MESH
BF = jnp.bfloat16
F32 = jnp.float32
SCALE = HD**-0.5
LOG2E = 1.4426950408889634
NT = (((1,), (1,)), ((), ()))


def dma(*shape):
    return pltpu.SemaphoreType.DMA(shape)


def vm(dtype, *shape):
    return pltpu.VMEM(shape, dtype)


SCRATCH = dict(
    frames=vm(BF, T, C), cot=vm(BF, T, C), w=vm(BF, 4, C, F), taps=vm(BF, KW, C),
    in_sem=dma(9),
    upad=vm(F32, T + 2 * HALF, C), uhalo=vm(BF, 2, HALF, C), tapsf=vm(F32, KW, C),
    bg=vm(BF, T, C), uh_s=dma(2), uh_r=dma(2),
    q_s=vm(BF, 4, HD + 16, T), k_s=vm(BF, 4, HD, T), v_s=vm(BF, 4, HD, T), d_s=vm(BF, 4, HD, T),
    q_r=vm(BF, 4, HD + 16, T), d_r=vm(BF, 4, HD, T), k_r=vm(BF, 8, HD, T), v_r=vm(BF, 8, HD, T),
    qs=dma(4), qr=dma(4), ks=dma(4), kr=dma(4), vs=dma(4), vr=dma(4), ds=dma(4), dr=dma(4),
    fks=dma(4), fkr=dma(4), fvs=dma(4), fvr=dma(4),
    kn=vm(BF, 8, T, HD), vn=vm(BF, 8, T, HD), qt=vm(BF, HD, Q), qn=vm(BF, Q, HD), dt=vm(BF, HD, Q), dn=vm(BF, Q, HD),
    live=vm(F32, 64, Q), st=vm(F32, 8, T, QC), et=vm(BF, 8, T, Q), dsb=vm(BF, 2, T, Q), dq=vm(F32, HD, Q),
    inverse=vm(F32, 1, Q), delta=vm(F32, 1, Q),
    o_s=vm(BF, 4, HD, T), dq_s=vm(BF, 4, HD, T), part_s=vm(BF, 4, 2 * HD, T), part_r=vm(BF, 4, 2 * HD, T),
    dkv_s=vm(BF, 4, 2 * HD, T), mix_r=vm(BF, 4, HD, T), dq_r=vm(BF, 4, HD, T), dkv_r=vm(BF, 4, 2 * HD, T),
    os=dma(4), orr=dma(4), dqs=dma(4), dqr=dma(4), ps=dma(4), pr=dma(4), dkvs=dma(4), dkvr=dma(4),
    op_s=vm(BF, 3, T, F), op_r=vm(BF, 3, T, F), ops=dma(3), opr=dma(3),
    rpad=vm(F32, T + 2 * HALF, F), res=vm(BF, T, F), rhalo=vm(BF, 2, HALF, F), enc=vm(BF, T, F),
    rh_s=dma(2), rh_r=dma(2), es=dma(4), er=dma(4),
    kacc=vm(F32, KW, 8, F), kg=vm(F32, KW, 1, F), kgr=vm(F32, KW, 1, F), kgy=vm(F32, 4, 1, F),
    kgs=dma(32), kgrs=dma(32), kys=dma(4), kyr=dma(4),
    g_s=vm(BF, 4, 2, F, F), g_r=vm(BF, 4, 2, F, F), gs=dma(4), gr=dma(4),
    s1s=dma(5, 4), s1r=dma(5, 4), s2s=dma(5, 4), s2r=dma(5, 4),
)


PARTS = ((3, 0, 48, True), (1, 0, 48, False), (2, 0, 48, True), (0, 0, 32, False), (0, 32, 16, True))
for i, (_, _, n, _) in enumerate(PARTS):
    SCRATCH[f"h1_{i}"] = vm(BF, 16, n, F)
    SCRATCH[f"s1_{i}"] = vm(BF, 3, 4, n, F)
    SCRATCH[f"h2_{i}"] = vm(BF, 4, n, F)
    SCRATCH[f"s2_{i}"] = vm(BF, 3, n, F)


def remote(src, dst, ssem, rsem, device):
    return pltpu.make_async_remote_copy(
        src_ref=src, dst_ref=dst, send_sem=ssem, recv_sem=rsem, device_id=device, device_id_type=MESH
    )


class Either:
    def __init__(self, here, src, dst, ssem, rsem, device):
        self.here = here
        self.local = pltpu.make_async_copy(src, dst, rsem)
        self.far = remote(src, dst, ssem, rsem, device)

    def start(self):
        pl.when(self.here)(lambda: self.local.start())
        pl.when(jnp.logical_not(self.here))(lambda: self.far.start())

    def wait(self):
        pl.when(self.here)(lambda: self.local.wait())
        pl.when(jnp.logical_not(self.here))(lambda: self.far.wait())


def go(copy):
    copy.start()
    return copy


def wait_all(copies):
    for c in copies:
        c.wait()


def correlate(acc, load, taps, offsets, rows):
    for r in range(8):
        part = None
        for o in sorted(offsets):
            if o % 8 == r:
                term = taps(offsets[o]) * load(o - r, rows + 8 if r else rows)
                part = term if part is None else part + term
        acc = acc + (part[r : r + rows] if r else part)
    return acc


def aligned(start, size, by):
    return pl.ds(pl.multiple_of(start, by), size)


def layer_kernel(frames_h, w_h, taps_h, pattern_h, cot_h, enc_out, pg_out, kg_out, *scratch):
    s = types.SimpleNamespace(**dict(zip(SCRATCH, scratch)))
    dp, tm, hd = lax.axis_index("dp"), lax.axis_index("tm"), lax.axis_index("head")
    zl, core = dp // 2, lax.rem(dp, 2)
    x, zh = tm // 2, lax.rem(tm, 2)
    z = zh * 2 + zl
    me = dp * 8 + tm
    around = lambda k: lax.rem(x + k, 4)
    at_tm = lambda k: (dp, lax.rem(tm + k, 8), hd)
    at_x = lambda k: (dp, around(k) * 2 + zh, hd)
    at_y = lambda k: (dp, tm, lax.rem(hd + k, 4))
    sibling = (zl * 2 + 1 - core, tm, hd)

    def at_z(k):
        to = lax.rem(z + k, 4)
        return (lax.rem(to, 2) * 2 + core, x * 2 + to // 2, hd)

    def at_plane(k):
        to = lax.rem(me + k, 32)
        return (to // 8, lax.rem(to, 8), hd)

    def swapped(k, src, dst, ssem, rsem):
        device = (zl * 2 + zh, around(k) * 2 + core, hd)
        if k:
            return go(remote(src, dst, ssem.at[k], rsem.at[k], device))
        return go(Either(zh == core, src, dst, ssem.at[0], rsem.at[0], device))

    load = [
        go(pltpu.make_async_copy(a, b, s.in_sem.at[i]))
        for i, (a, b) in enumerate(
            [
                (frames_h.at[0], s.frames),
                (w_h.at[1], s.w.at[1]),
                (w_h.at[0], s.w.at[0]),
                (w_h.at[2], s.w.at[2]),
                (cot_h.at[0], s.cot),
                (taps_h, s.taps),
                (w_h.at[3], s.w.at[3]),
            ]
        )
    ]
    barrier = pltpu.get_barrier_semaphore()
    others = [at_plane(k) for k in range(1, 32)] + [at_y(k) for k in range(1, 4)]
    for device in others:
        pl.semaphore_signal(barrier, inc=1, device_id=device, device_id_type=MESH)

    def projected(rows, p, factor=None):
        y = jnp.dot(rows, s.w[p], preferred_element_type=F32)
        return (y if factor is None else y * factor).astype(BF).T

    load[0].wait()
    load[1].wait()
    y = projected(s.frames[...], 1)
    for h in range(4):
        s.k_s[h] = y[h * HD : (h + 1) * HD]
    pl.semaphore_wait(barrier, len(others))
    load[4].wait()
    halos = [
        go(remote(s.cot.at[T - HALF : T], s.uhalo.at[0], s.uh_s.at[0], s.uh_r.at[0], at_tm(1))),
        go(remote(s.cot.at[0:HALF], s.uhalo.at[1], s.uh_s.at[1], s.uh_r.at[1], at_tm(7))),
    ]
    k_c = [swapped(k, s.k_s.at[around(k)], s.k_r.at[x], s.ks, s.kr) for k in (1, 2, 3, 0)]
    load[2].wait()
    y = projected(s.frames[...], 0, SCALE * LOG2E)
    row = lax.broadcasted_iota(jnp.int32, (16, T), 0)
    block = lax.broadcasted_iota(jnp.int32, (1, T), 1) // BLK
    phase = count = jnp.zeros((1, T), F32)
    for b in range(6):
        entries = pattern_h[b]
        phase = jnp.where(block == b, entries[:, 0:1].astype(F32), phase)
        count = jnp.where(block == b, jnp.sum((entries >= 0).astype(F32), axis=1, keepdims=True), count)
    meta = jnp.where(row == 0, phase, jnp.where(row == 1, count, 0.0)).astype(BF)
    for h in range(4):
        s.q_s[h, 0:HD] = y[h * HD : (h + 1) * HD]
        s.q_s[h, HD:] = meta
    q_c = [swapped(k, s.q_s.at[around(k)], s.q_r.at[x], s.qs, s.qr) for k in (1, 2, 3, 0)]
    load[3].wait()
    y = projected(s.frames[...], 2)
    for h in range(4):
        s.v_s[h] = y[h * HD : (h + 1) * HD]
    v_c = [swapped(k, s.v_s.at[around(k)], s.v_r.at[x], s.vs, s.vr) for k in (1, 2, 3, 0)]

    load[5].wait()
    s.tapsf[...] = s.taps[...].astype(F32)
    s.upad[HALF : HALF + T] = s.cot[...].astype(F32)
    wait_all(halos)
    s.upad[0:HALF] = jnp.where(tm > 0, s.uhalo[0].astype(F32), 0.0)
    s.upad[HALF + T :] = jnp.where(tm < 7, s.uhalo[1].astype(F32), 0.0)

    def conv_back(it, carry):
        i, l = it // 12, lax.rem(it, 12)
        lanes = aligned(l * 128, 128, 128)
        base = i * CR
        acc = correlate(
            s.upad[aligned(base + HALF, CR, 16), lanes],
            lambda o, n: s.upad[aligned(base + o, n, 8), lanes],
            lambda j: s.tapsf[j : j + 1, lanes],
            {2 * HALF - j: j for j in range(KW)},
            CR,
        )
        s.bg[aligned(base, CR, CR), lanes] = acc.astype(BF)
        return carry

    lax.fori_loop(0, 12 * T // CR, conv_back, 0)
    load[6].wait()
    y = projected(s.bg[...], 3)
    for h in range(4):
        s.d_s[h] = y[h * HD : (h + 1) * HD]
    d_c = [swapped(k, s.d_s.at[around(k)], s.d_r.at[x], s.ds, s.dr) for k in (1, 2, 3, 0)]

    def forward(k, copy, buf, ssem, rsem):
        copy.wait()
        src = lax.rem(x + 4 - k, 4)
        return go(remote(buf.at[src], buf.at[4 + src], ssem.at[k], rsem.at[k], sibling))

    fk_c = [forward(k, c, s.k_r, s.fks, s.fkr) for k, c in zip((1, 2, 3, 0), k_c)]
    wait_all(q_c)
    for a in range(4):
        lanes = slice(a * T, (a + 1) * T)
        s.qt[:, lanes] = s.q_r[a, 0:HD]
        s.qn[lanes, :] = s.q_r[a, 0:HD].T
        got = s.q_r[a, HD:].astype(F32)
        row = lax.broadcasted_iota(jnp.int32, (64, T), 0)
        tile = row // 8
        owner = lax.rem(tile, 4) * 2 + jnp.where(tile < 4, core, 1 - core)
        key_block = owner * 6 + lax.rem(row, 8)
        query_block = (a * 2 + core) * 6 + lax.broadcasted_iota(jnp.int32, (64, T), 1) // BLK
        far = (lax.rem(key_block, 4).astype(F32) == got[0:1]) & ((key_block // 4).astype(F32) < got[1:2])
        near = jnp.abs(key_block - query_block) < 2
        s.live[:, lanes] = jnp.where(far | near, 1.0, 0.0)
    for t in range(4):
        s.kn[t] = s.k_r[t].T
    fv_c = [forward(k, c, s.v_r, s.fvs, s.fvr) for k, c in zip((1, 2, 3, 0), v_c)]
    wait_all(fk_c)
    for t in range(4, 8):
        s.kn[t] = s.k_r[t].T

    for c in range(Q // QC):
        lanes = slice(c * QC, (c + 1) * QC)
        q_t = s.qt[:, lanes]

        def scores(t, top):
            sc = jnp.dot(s.kn[t], q_t, preferred_element_type=F32)
            mask = s.live[aligned(t * 8, 8, 8), lanes]
            for b in range(6):
                part = jnp.where(mask[b : b + 1] > 0.5, sc[b * BLK : (b + 1) * BLK], -1e30)
                top = jnp.maximum(top, jnp.max(part.reshape(8, 8, QC), axis=0))
                s.st[t, b * BLK : (b + 1) * BLK] = part
            return top

        top = lax.fori_loop(0, 8, scores, jnp.full((8, QC), -jnp.inf, F32), unroll=8)
        top = jnp.max(top, axis=0, keepdims=True)
        if c == 0:
            wait_all(fv_c)

        def weigh(t, o):
            eb = jnp.exp2(s.st[t] - top).astype(BF)
            s.et[t, :, lanes] = eb
            values = jnp.concatenate([s.v_r[t], jnp.ones((16, T), BF)], axis=0)
            return o + jnp.dot(values, eb, preferred_element_type=F32)

        o = lax.fori_loop(0, 8, weigh, jnp.zeros((HD + 16, QC), F32), unroll=8)
        inverse = 1.0 / o[HD : HD + 1]
        o = o[0:HD]
        s.inverse[:, lanes] = inverse
        o = (o * inverse).astype(BF)
        for a in range(2):
            s.o_s[c * 2 + a] = o[:, a * T : (a + 1) * T]
    o_c = [swapped(k, s.o_s.at[around(k)], s.mix_r.at[x], s.os, s.orr) for k in (1, 2, 3, 0)]

    wait_all(d_c)
    for a in range(4):
        lanes = slice(a * T, (a + 1) * T)
        d = s.d_r[a].astype(F32)
        inverse = s.inverse[:, lanes]
        s.delta[:, lanes] = jnp.sum(d * s.o_s[a].astype(F32), axis=0, keepdims=True) * inverse
        d = (d * inverse).astype(BF)
        s.dt[:, lanes] = d
        s.dn[lanes, :] = d.T
    for t in range(8):
        s.vn[t] = s.v_r[t].T
    s.dq[...] = jnp.zeros_like(s.dq)

    def back(first, k, slot):
        t = first + around(k)
        for c in range(Q // QC):
            lanes = slice(c * QC, (c + 1) * QC)
            dp_ = jnp.dot(s.vn[t], s.dt[:, lanes], preferred_element_type=F32)
            s.dsb[slot, :, lanes] = (s.et[t, :, lanes].astype(F32) * (dp_ - s.delta[:, lanes])).astype(BF)
        dk = jnp.dot(s.dsb[slot], s.qn[...], preferred_element_type=F32) * (1 / LOG2E)
        dv = jnp.dot(s.et[t], s.dn[...], preferred_element_type=F32)
        s.dq[...] += jnp.dot(s.k_r[t], s.dsb[slot], preferred_element_type=F32)
        return dk, dv

    def back_pair(first, ks, out):
        for slot, k in enumerate(ks):
            dk, dv = back(first, k, slot)
            out[around(k), 0:HD] = dk.astype(BF).T
            out[around(k), HD:] = dv.astype(BF).T

    def sibling_pair(ks):
        back_pair(4, ks, s.part_s)
        for k in ks:
            i = around(k)
            p_c[k] = go(remote(s.part_s.at[i], s.part_r.at[i], s.ps.at[k], s.pr.at[k], sibling))

    p_c = {}
    sibling_pair((1, 2))

    sibling_pair((3, 0))

    wait_all(o_c)
    mixed = s.mix_r[...].reshape(F, T).T
    op_c = []
    for k in range(1, 4):
        rows = aligned(lax.rem(hd + k, 4) * F, F, F)
        s.op_s[k - 1] = lax.dot_general(mixed, s.w[3, rows, :], NT, preferred_element_type=F32).astype(BF)
        op_c.append(go(remote(s.op_s.at[k - 1], s.op_r.at[k - 1], s.ops.at[k - 1], s.opr.at[k - 1], at_y(k))))


    def away(p, left, right):
        for l in range(2):
            rows = aligned((l * 2 + 1 - core) * F, F, F)
            s.g_s[p, l] = jnp.dot(left[rows, :], right, preferred_element_type=F32).astype(BF)
        return go(remote(s.g_s.at[p], s.g_r.at[p], s.gs.at[p], s.gr.at[p], sibling))

    first_c, second_c = {}, {}

    def keep(p, left, right, copy):
        copy.wait()
        parts = [(i, r0, n, by_x) for i, (q, r0, n, by_x) in enumerate(PARTS) if q == p]
        for l in range(2):
            rows = aligned((l * 2 + core) * F, F, F)
            g = jnp.dot(left[rows, :], right, preferred_element_type=F32) + s.g_r[p, l].astype(F32)
            g = g.astype(BF)
            for xo in range(4):
                for h in range(2):
                    for i, r0, n, by_x in parts:
                        start = xo * 96 + h * 48 + r0
                        slot = xo * 4 + h * 2 + l if by_x else (h * 2 + l) * 4 + xo
                        getattr(s, f"h1_{i}")[slot] = g[start : start + n]
        for i, r0, n, by_x in parts:
            h1, s1 = getattr(s, f"h1_{i}"), getattr(s, f"s1_{i}")
            first_c[i] = []
            for k in range(1, 4):
                to = lax.rem((x if by_x else z) + k, 4)
                device = at_x(k) if by_x else at_z(k)
                c = remote(h1.at[pl.ds(to * 4, 4)], s1.at[k - 1], s.s1s.at[i, k], s.s1r.at[i, k], device)
                first_c[i].append(go(c))

    def second(i):
        by_x = PARTS[i][3]
        h1, s1 = getattr(s, f"h1_{i}"), getattr(s, f"s1_{i}")
        h2, s2 = getattr(s, f"h2_{i}"), getattr(s, f"s2_{i}")
        wait_all(first_c[i])
        own = h1[pl.ds((x if by_x else z) * 4, 4)].astype(F32)
        for k in range(3):
            own = own + s1[k].astype(F32)
        h2[...] = own.astype(BF)
        second_c[i] = []
        for k in range(1, 4):
            to = lax.rem((z if by_x else x) + k, 4)
            device = at_z(k) if by_x else at_x(k)
            c = remote(h2.at[to], s2.at[k - 1], s.s2s.at[i, k], s.s2r.at[i, k], device)
            second_c[i].append(go(c))

    def last(i):
        p, r0, n, by_x = PARTS[i]
        h2, s2 = getattr(s, f"h2_{i}"), getattr(s, f"s2_{i}")
        wait_all(second_c[i])
        own = h2[z if by_x else x].astype(F32)
        for k in range(3):
            own = own + s2[k].astype(F32)
        pg_out[p, r0 : r0 + n] = own

    dkv_c = []
    for ks in ((1, 2), (3, 0)):
        for slot, k in enumerate(ks):
            dk, dv = back(0, k, slot)
            p_c[k].wait()
            i = around(k)
            s.dkv_s[i, 0:HD] = (dk.T + s.part_r[i, 0:HD].astype(F32)).astype(BF)
            s.dkv_s[i, HD:] = (dv.T + s.part_r[i, HD:].astype(F32)).astype(BF)
        for k in ks:
            dkv_c.append(swapped(k, s.dkv_s.at[around(k)], s.dkv_r.at[x], s.dkvs, s.dkvr))
    for a in range(4):
        s.dq_s[a] = (s.dq[:, a * T : (a + 1) * T] * SCALE).astype(BF)
    dq_c = [swapped(k, s.dq_s.at[around(k)], s.dq_r.at[x], s.dqs, s.dqr) for k in (1, 2, 3, 0)]

    summed = lax.dot_general(mixed, s.w[3, aligned(hd * F, F, F), :], NT, preferred_element_type=F32)
    wait_all(op_c)
    for k in range(3):
        summed = summed + s.op_r[k].astype(F32)
    mine = aligned(hd * F, F, 128)
    s.res[...] = (s.frames[:, mine].astype(F32) + summed).astype(BF)
    halos = [
        go(remote(s.res.at[T - HALF : T], s.rhalo.at[0], s.rh_s.at[0], s.rh_r.at[0], at_tm(1))),
        go(remote(s.res.at[0:HALF], s.rhalo.at[1], s.rh_s.at[1], s.rh_r.at[1], at_tm(7))),
    ]

    bg_t, frames_t = s.w.at[0], s.w.at[1]
    bg_t[...] = s.bg[...].T
    g3 = away(3, bg_t, mixed)

    keep(3, bg_t, mixed, g3)
    frames_t[...] = s.frames[...].T
    wait_all(dkv_c)
    dk = s.dkv_r[:, 0:HD].reshape(F, T).T
    g1 = away(1, frames_t, dk)
    dv = s.dkv_r[:, HD:].reshape(F, T).T
    g2 = away(2, frames_t, dv)
    wait_all(dq_c)
    dq = s.dq_r[...].reshape(F, T).T
    g0 = away(0, frames_t, dq)
    keep(1, frames_t, dk, g1)
    keep(2, frames_t, dv, g2)
    keep(0, frames_t, dq, g0)

    s.rpad[HALF : HALF + T] = s.res[...].astype(F32)
    wait_all(halos)
    s.rpad[0:HALF] = jnp.where(tm > 0, s.rhalo[0].astype(F32), 0.0)
    s.rpad[HALF + T :] = jnp.where(tm < 7, s.rhalo[1].astype(F32), 0.0)

    def conv(it, carry):
        i, l = it // 3, lax.rem(it, 3)
        lanes = aligned(l * 128, 128, 128)
        whole = aligned(hd * F + l * 128, 128, 128)
        base = i * CR
        window = lambda o, n: s.rpad[aligned(base + o, n, 8), lanes]
        acc = correlate(
            window(HALF, CR), window, lambda j: s.tapsf[j : j + 1, whole], {j: j for j in range(KW)}, CR
        )
        s.enc[aligned(base, CR, CR), lanes] = acc.astype(BF)
        return carry

    lax.fori_loop(0, 3 * T // CR, conv, 0)
    e_c = [go(remote(s.enc, enc_out.at[:, mine], s.es.at[k], s.er.at[k], at_y(k))) for k in range(1, 4)]
    e_c.append(go(pltpu.make_async_copy(s.enc, enc_out.at[:, mine], s.in_sem.at[8])))

    s.kacc[...] = jnp.zeros_like(s.kacc)

    def taps_grad(it, carry):
        i, l = it // 3, lax.rem(it, 3)
        lanes = aligned(l * 128, 128, 128)
        base = i * CR
        up = s.cot[aligned(base, CR, CR), aligned(hd * F + l * 128, 128, 128)].astype(F32)
        edge = jnp.zeros((8, 128), F32)
        up = jnp.concatenate([edge, up, edge], axis=0)
        for r in range(8):
            moved = up[8 - r : CR + 16 - r] if r else up[8 : CR + 8]
            for a in range(KW // 8):
                term = moved * s.rpad[aligned(base + 8 * a, CR + 8 if r else CR, 8), lanes]
                s.kacc[8 * a + r, :, lanes] += jnp.sum(term.reshape(-1, 8, 128), axis=0)
        return carry

    lax.fori_loop(0, 3 * T // CR, taps_grad, 0)
    for j in range(KW):
        s.kg[j] = jnp.sum(s.kacc[j], axis=0, keepdims=True)
    kg_c = []
    for k in range(1, 32):
        to = lax.rem(me + k, 32)
        kg_c.append(go(remote(s.kg.at[to], s.kgr.at[k], s.kgs.at[k], s.kgrs.at[k], at_plane(k))))

    for i in (0, 2, 1, 4, 3):
        second(i)
    wait_all(kg_c)
    total = s.kg[me]
    for k in range(1, 32):
        total = total + s.kgr[k]
    s.kgy[hd] = total
    ky_c = [go(remote(s.kgy.at[hd], s.kgy.at[hd], s.kys.at[k], s.kyr.at[k], at_y(k))) for k in range(1, 4)]
    for i in (0, 2, 1, 4, 3):
        last(i)
    wait_all(ky_c)
    for y in range(4):
        kg_out[:, y * F : (y + 1) * F] = s.kgy[y]
    wait_all(e_c)


def shards(frames, projections, kernel, pattern, cotangent):
    vmem = pl.BlockSpec(memory_space=pltpu.VMEM)
    anym = pl.BlockSpec(memory_space=pl.ANY)
    enc, pg, kg = pl.pallas_call(
        layer_kernel,
        out_shape=(
            jax.ShapeDtypeStruct((T, C), BF),
            jax.ShapeDtypeStruct((4, 48, F), F32),
            jax.ShapeDtypeStruct((1, C), F32),
        ),
        in_specs=[anym, anym, anym, vmem, anym],
        out_specs=(anym, vmem, vmem),
        scratch_shapes=list(SCRATCH.values()),
        compiler_params=pltpu.CompilerParams(
            collective_id=0, has_side_effects=True, vmem_limit_bytes=55 << 20
        ),
        name="conformer_layer",
    )(frames, projections, kernel, jnp.transpose(pattern, (1, 0, 2)), cotangent)
    return enc[None], pg, kg


def solution(mesh):
    placed = (
        P("dp", "tm", None),
        P(None, None, "head"),
        P(),
        P("dp", "tm", None),
        P("dp", "tm", None),
    )
    return jax.shard_map(
        shards,
        mesh=mesh,
        in_specs=placed,
        out_specs=(P("dp", "tm", None), P(None, ("dp", "tm"), "head"), P(("dp", "tm"), None)),
        check_vma=False,
    )
```
